32 devices in a mesh: ctx: 4 (over z), exp: 8 (over y, x, core).
Axes of the slice: x: 2, y: 2, z: 4, core: 2. Of those that a mesh axis runs over, the one named last changes fastest.
Arguments:
- tokens: bfloat16 [8, 2048, 1024], P('exp', 'ctx'), may hold values from -6 to 6
- w_query: bfloat16 [1024, 1024], P(('ctx', 'exp')), may hold values from -0.1875 to 0.1875
- w_key: bfloat16 [1024, 1024], P(('ctx', 'exp')), may hold values from -0.1875 to 0.1875
- w_value: bfloat16 [1024, 1024], P(('ctx', 'exp')), may hold values from -0.1875 to 0.1875
- w_out: bfloat16 [1024, 1024], P(('ctx', 'exp')), may hold values from -0.75 to 0.75
- w_router: bfloat16 [1024, 8], P(('ctx', 'exp')), may hold values from -0.125 to 0.125
- gain_attn: bfloat16 [1024], P(('ctx', 'exp')), may hold values from 0.5 to 1.5
- gain_mlp: bfloat16 [1024], P(('ctx', 'exp')), may hold values from 0.5 to 1.5
- pos_bias: bfloat16 [512], P(('ctx', 'exp')), may hold values from -5 to 5
- exp_gate: bfloat16 [8, 1024, 2816], P('exp', 'ctx'), may hold values from -0.1875 to 0.1875
- exp_up: bfloat16 [8, 1024, 2816], P('exp', 'ctx'), may hold values from -0.1875 to 0.1875
- exp_down: bfloat16 [8, 2816, 1024], P('exp', 'ctx'), may hold values from -0.109375 to 0.109375
- doc_lengths: int32 [8, 8], P('exp'), may hold values from 1 to 2048, as said below
- bucket_of: int32 [1024], replicated, may hold values from 0 to 31
- expert_ids: int32 [8, 2048, 2], P('exp', 'ctx'), may hold values from 0 to 7, all different within a row; in each aligned block of 512 rows (0 to 511, 512 to 1023, ..., all dimensions but the last counted through in order) at most 160 rows name the same one
- cotangent: bfloat16 [8, 2048, 1024], P('exp', 'ctx'), may hold values from -6 to 6
Outputs:
- output: bfloat16 [8, 2048, 1024], P('exp', 'ctx')
- input_grad: float32 [8, 2048, 1024], P('exp', 'ctx')
- grad_query: float32 [1024, 1024], P(('ctx', 'exp'))
- grad_key: float32 [1024, 1024], P(('ctx', 'exp'))
- grad_value: float32 [1024, 1024], P(('ctx', 'exp'))
- grad_out: float32 [1024, 1024], P(('ctx', 'exp'))
- grad_router: float32 [1024, 8], P(('ctx', 'exp'))
- grad_gain_attn: float32 [1024], P(('ctx', 'exp'))
- grad_gain_mlp: float32 [1024], P(('ctx', 'exp'))
- grad_pos_bias: float32 [512], P(('ctx', 'exp'))
- grad_gate: float32 [8, 1024, 2816], P('exp', 'ctx')
- grad_up: float32 [8, 1024, 2816], P('exp', 'ctx')
- grad_down: float32 [8, 2816, 1024], P('exp', 'ctx')
The draws below stay inside these ranges and needn't reach their ends.
Inputs may be any that keep to these rules, and one draw needn't show every extreme that they name: `doc_lengths`: the 8 lengths of a sequence sum to 2048. `expert_ids`: a token names 2 different experts; among the 512 tokens of one aligned token block no expert is named more than 160 times.
All inputs are finite; a program needn't handle non-finite values.
Results may differ from the reference program's by a relative error of at most 0.017.
Values may be sent and summed in bfloat16 or wider, within the bound.
A program may use at most 320 MiB of HBM per device.

```python
import math
import jax
import jax.numpy as jnp
import numpy as np
from jax import lax

D = 1024
HEADS = 16
HEAD_DIM = 64
FF = 2816
BUCKETS = 32
TOP = 2
WINDOW = 1024
DOCS = 8
TOK_DEV = 512
EXPERTS = 8
SEQS = 8
SEQ_LEN = 2048
CAP = 160
REACH = 2
N_CTX = 4


def draw_doc_lengths(key, part):
    key = jax.random.fold_in(key, 11)
    first_key, second_key = jax.random.split(key)
    shorter = jax.random.randint(first_key, (SEQS, DOCS), 1, TOK_DEV // 8 + 1)
    long_at = jax.random.randint(second_key, (SEQS, 1), 0, DOCS)
    is_long = jnp.arange(DOCS)[None, :] == long_at
    others = jnp.sum(jnp.where(is_long, 0, shorter), axis=1, keepdims=True)
    return jnp.where(is_long, SEQ_LEN - others, shorter).astype(jnp.int32)


def with_ends(values, key, least, high):
    shape = values.shape
    spot = [jax.random.randint(jax.random.fold_in(key, axis), (), 0, shape[axis]) for axis in range(len(shape))]
    values = values.at[tuple(spot)].set(least)
    longest = shape.index(max(shape))
    spot[longest] = (spot[longest] + 1) % shape[longest]
    return values.at[tuple(spot)].set(high)


def block_scale(key, dims, shards, smallest, top_value):
    def one(position, parts):
        heights = jax.random.uniform(jax.random.fold_in(jax.random.fold_in(key, 6), position), (parts,), jnp.float32, smallest / len(shards), top_value / len(shards))
        return jnp.repeat(jnp.exp(heights), dims[position] // parts).reshape((-1,) + (1,) * (len(dims) - position - 1))

    loudness = one(*shards[0])
    for cut in shards[1:]:
        loudness = loudness * one(*cut)
    return loudness


def routed_block(rng, own, number, rows, number_of, top, limit, skew):
    sequence = jax.random.permutation(rng, number_of)
    heavy_load, usual = load_shares(number_of, rows * top, limit, skew, True), load_shares(number_of, rows * top, limit, skew, False)
    places = jnp.arange(number_of)

    def named(sizes, rotation):
        used = int((sizes > 0).sum())
        fixed = max(1, used // 4)
        moved = fixed + (places - fixed + rotation * (used - fixed)) % max(1, number_of - fixed)
        return jnp.zeros((number_of,), jnp.int32).at[sequence[jnp.where(places < fixed, places, moved)]].set(jnp.asarray(sizes, jnp.int32))

    sizes = jnp.where(number % 4 == 0, named(heavy_load, number // 4), named(usual, number - number // 4 - 1))
    mixed = jax.random.permutation(jax.random.fold_in(own, 3), number_of)
    giver, sink = mixed[0:number_of // 2 * 2:2], mixed[1:number_of // 2 * 2:2]
    room = jnp.minimum(sizes[giver] - 1, limit - sizes[sink]) // 2
    room = jnp.where((giver == sequence[0]) | (sink == sequence[0]) | (sizes[sink] == 0), 0, jnp.maximum(room, 0))
    moved = jax.random.randint(jax.random.fold_in(own, 4), (number_of // 2,), 0, 1 << 20) % (room + 1)
    sizes = sizes.at[giver].add(-moved).at[sink].add(moved)
    items = jnp.searchsorted(jnp.cumsum(sizes), jnp.arange(rows * top), side="right").astype(jnp.int32)
    grid = items.reshape(top, rows).T
    grid = grid[jax.random.permutation(jax.random.fold_in(own, 1), rows)]
    rotation = jax.random.randint(jax.random.fold_in(own, 2), (rows, 1), 0, top)
    return jnp.take_along_axis(grid, (jnp.arange(top)[None, :] + rotation) % top, axis=1)


def load_shares(count, total, most, lean, full):
    weights = [(1 << 20) // math.isqrt(rank ** lean) + 1 for rank in range(1, count + 1)]
    largest = most if full else min(most, max(-(-total // count), total * weights[0] // sum(weights)))
    least = 1 if total - largest >= count - 1 else 0
    given, rest = [largest] + [least] * (count - 1), total - largest - least * (count - 1)
    while rest > 0:
        movable = [i for i in range(1, count) if given[i] < largest] or [i for i in range(1, count) if given[i] < most]
        whole, budget = sum([weights[i] for i in movable]), rest
        for i in movable:
            extra = min(most - given[i], max(1, budget * weights[i] // whole), rest)
            given[i] = given[i] + extra
            rest = rest - extra
    return np.array(given)


def gaussian(own_key, extent, deviation, limit, cuts=(), kind=jnp.bfloat16):
    entries = jax.random.normal(own_key, extent, jnp.float32) * deviation
    if len(cuts) > 0:
        entries = block_scale(own_key, extent, cuts, -0.22, 0.18) * entries
    return jnp.clip(entries, min=-limit, max=limit).astype(kind)


def setup_inputs(seed: int = 0) -> dict:
    seeds = jax.random.split(jax.random.key(seed), 17)
    tokens = gaussian(seeds[0], (SEQS, SEQ_LEN, D), 1.0, 6.0, ((0, 8), (1, 4)))
    w_query = gaussian(seeds[1], (D, D), D ** -0.5, 0.1875, ((0, 32),))
    w_key = gaussian(seeds[2], (D, D), D ** -0.5, 0.1875, ((0, 32),))
    w_value = gaussian(seeds[3], (D, D), D ** -0.5, 0.1875, ((0, 32),))
    w_out = gaussian(seeds[4], (D, D), (D // 16) ** -0.5, 0.75, ((0, 32),))
    w_router = gaussian(seeds[5], (D, EXPERTS), (2 * D) ** -0.5, 0.125, ((0, 32),))
    gain_attn = jnp.clip(1.0 + 0.1 * jax.random.normal(seeds[6], (D,), jnp.float32), 0.5, 1.5).astype(jnp.bfloat16)
    gain_mlp = jnp.clip(1.0 + 0.1 * jax.random.normal(seeds[7], (D,), jnp.float32), 0.5, 1.5).astype(jnp.bfloat16)
    pos_bias = gaussian(seeds[8], (HEADS * BUCKETS,), 1.0, 5.0, ((0, 32),))
    exp_gate = gaussian(seeds[9], (EXPERTS, D, FF), D ** -0.5, 0.1875, ((0, 8), (1, 4)))
    exp_up = gaussian(seeds[10], (EXPERTS, D, FF), D ** -0.5, 0.1875, ((0, 8), (1, 4)))
    exp_down = gaussian(seeds[11], (EXPERTS, FF, D), FF ** -0.5, 0.109375, ((0, 8), (1, 4)))
    doc_lengths = draw_doc_lengths(jax.random.fold_in(seeds[16], 71), 0)
    bucket_of = with_ends(jax.random.randint(seeds[13], (WINDOW,), 0, BUCKETS), jax.random.fold_in(seeds[13], 1), 0, BUCKETS - 1).astype(jnp.int32)
    expert_ids_keys = jax.random.split(jax.random.fold_in(seeds[14], 1), SEQS * SEQ_LEN // TOK_DEV)
    expert_ids_turns = jax.random.permutation(jax.random.fold_in(seeds[14], 3), SEQS * SEQ_LEN // TOK_DEV)
    expert_ids = jax.vmap(lambda own, number: routed_block(jax.random.fold_in(seeds[14], 2), own, number, TOK_DEV, EXPERTS, TOP, CAP, 2))(expert_ids_keys, expert_ids_turns).reshape((SEQS, SEQ_LEN, TOP))
    cotangent = gaussian(seeds[15], (SEQS, SEQ_LEN, D), 1.0, 6.0, ((0, 8), (1, 4)))
    return {"tokens": tokens, "w_query": w_query, "w_key": w_key, "w_value": w_value, "w_out": w_out, "w_router": w_router, "gain_attn": gain_attn, "gain_mlp": gain_mlp, "pos_bias": pos_bias, "exp_gate": exp_gate, "exp_up": exp_up, "exp_down": exp_down, "doc_lengths": doc_lengths, "bucket_of": bucket_of, "expert_ids": expert_ids, "cotangent": cotangent}


@jax.custom_vjp
def low(v):
    return lax.optimization_barrier(v.astype(jnp.bfloat16)).astype(jnp.float32)

@jax.custom_vjp
def low_back(v):
    return v

def low_keep(v):
    return (low(v), None)

def low_pass(kept, grad):
    return (grad,)

def back_keep(v):
    return (v, None)

def back_low(kept, grad):
    return (low(grad),)
low.defvjp(low_keep, low_pass)
low_back.defvjp(back_keep, back_low)
EPSILON = 1e-06
PRECISION_MAX = lax.Precision.HIGHEST

def norm_rows(values, gain):
    return values * lax.rsqrt(lax.optimization_barrier(jnp.mean(values * values, axis=-1, keepdims=True)) + EPSILON) * gain

def slot_of(choices):
    onehot = (choices[..., None] == jnp.arange(EXPERTS, dtype=jnp.int32)).astype(jnp.int32)
    return lax.optimization_barrier(jnp.sum(jnp.cumsum(onehot, axis=-2) * onehot, axis=-1)) - 1

def attend_sequence(queries, keys, values, lengths, bias_dist):
    margin = REACH * TOK_DEV
    ends = jnp.cumsum(lengths)
    padding = jnp.zeros((margin, D), jnp.float32)
    keys_pad = jnp.concatenate([padding, keys], axis=0)
    values_pad = jnp.concatenate([padding, values], axis=0)

    def block(start):
        query_heads = lax.dynamic_slice_in_dim(queries, start, TOK_DEV, 0).reshape(TOK_DEV, HEADS, HEAD_DIM)
        key_heads = lax.dynamic_slice_in_dim(keys_pad, start, margin + TOK_DEV, 0).reshape(-1, HEADS, HEAD_DIM)
        value_heads = lax.dynamic_slice_in_dim(values_pad, start, margin + TOK_DEV, 0).reshape(-1, HEADS, HEAD_DIM)
        query_pos = start + jnp.arange(TOK_DEV, dtype=jnp.int32)
        key_pos = start - margin + jnp.arange(margin + TOK_DEV, dtype=jnp.int32)
        query_doc = lax.optimization_barrier(jnp.sum((query_pos[:, None] >= ends[None, :]).astype(jnp.int32), axis=1))
        key_doc = lax.optimization_barrier(jnp.sum((key_pos[:, None] >= ends[None, :]).astype(jnp.int32), axis=1))
        distance = query_pos[:, None] - key_pos[None, :]
        allowed = (key_pos[None, :] >= 0) & (distance >= 0) & (distance < WINDOW) & (query_doc[:, None] == key_doc[None, :])
        bias = jnp.take(bias_dist, jnp.clip(distance, 0, WINDOW - 1).astype(jnp.int32), axis=1)
        raw = jnp.einsum('thd,shd->hts', query_heads, key_heads, precision=PRECISION_MAX) * HEAD_DIM ** (-0.5) + bias
        raw = low_back(raw)
        scores = jnp.where(allowed[None], raw, -1e+30)
        largest = lax.optimization_barrier(jnp.max(scores, axis=-1, keepdims=True))
        expo = jnp.exp(scores - largest)
        probs = expo / lax.optimization_barrier(jnp.sum(expo, axis=-1, keepdims=True))
        attention_output = jnp.einsum('hts,shd->thd', low(probs), value_heads, precision=PRECISION_MAX)
        return attention_output.reshape(TOK_DEV, D)
    starts = jnp.arange(N_CTX, dtype=jnp.int32) * TOK_DEV
    result = lax.map(jax.checkpoint(block), starts)
    return result.reshape(SEQ_LEN, D)

def expert_block(operands):
    inputs, gate_w, up_w, down_w = operands
    rows = inputs.reshape(-1, D)
    gate_pre = low_back(jnp.dot(rows, gate_w, precision=PRECISION_MAX))
    up_pre = low_back(jnp.dot(rows, up_w, precision=PRECISION_MAX))
    hidden = low(jax.nn.gelu(gate_pre, approximate=True) * up_pre)
    produced = low_back(low(jnp.dot(hidden, down_w, precision=PRECISION_MAX)))
    return produced.reshape(inputs.shape)

def reference(tokens, w_query, w_key, w_value, w_out, w_router, gain_attn, gain_mlp, pos_bias, exp_gate, exp_up, exp_down, doc_lengths, bucket_of, expert_ids, cotangent):
    blocks_all = SEQS * N_CTX
    flat_ids = expert_ids.reshape(blocks_all, TOK_DEV * TOP).astype(jnp.int32)
    slots = slot_of(flat_ids).astype(jnp.int32)
    block_index = jnp.arange(blocks_all, dtype=jnp.int32)[:, None]

    def forward(inputs, query_w, key_w, value_w, output_weight, router_weight, gain_one, gain_two, bias_flat, gate_all, up_all, down_all):
        normalized_input = low(norm_rows(inputs, gain_one))

        def project(weight_matrix):
            return low_back(low(jnp.einsum('tjb,bx->tjx', normalized_input, weight_matrix, precision=PRECISION_MAX)))
        queries = project(query_w)
        keys = project(key_w)
        values = project(value_w)
        bias_dist = jnp.take(bias_flat.reshape(HEADS, BUCKETS), bucket_of, axis=1)

        def one_sequence(operands):
            return attend_sequence(operands[0], operands[1], operands[2], operands[3], bias_dist)
        attention_output = lax.map(one_sequence, (queries, keys, values, doc_lengths))
        attention_output = low_back(low(attention_output))
        branch_output = low_back(jnp.einsum('tjb,bx->tjx', attention_output, output_weight, precision=PRECISION_MAX))
        middle = inputs + branch_output
        normalized_expert_input = low(norm_rows(middle, gain_two))
        router_scores = jnp.einsum('tjb,bx->tjx', normalized_expert_input, router_weight, precision=PRECISION_MAX)
        chosen = jnp.take_along_axis(router_scores, expert_ids, axis=-1)
        gates = jax.nn.softmax(chosen, axis=-1)
        source = jnp.repeat(normalized_expert_input.reshape(blocks_all, TOK_DEV, D), TOP, axis=1)
        buffer = jnp.zeros((EXPERTS, blocks_all, CAP, D), jnp.float32).at[flat_ids, block_index, slots].set(source)
        results = lax.map(jax.checkpoint(expert_block), (buffer, gate_all, up_all, down_all))
        produced = results[flat_ids, block_index, slots].reshape(SEQS, SEQ_LEN, TOP, D)
        return middle + lax.optimization_barrier(jnp.sum(gates[..., None] * produced, axis=2))
    floats = [array.astype(jnp.float32) for array in (tokens, w_query, w_key, w_value, w_out, w_router, gain_attn, gain_mlp, pos_bias, exp_gate, exp_up, exp_down)]
    result, pullback = jax.vjp(forward, *floats)
    gradients = pullback(cotangent.astype(jnp.float32))
    return (result.astype(jnp.bfloat16), gradients[0], gradients[1], gradients[2], gradients[3], gradients[4], gradients[5], gradients[6], gradients[7], gradients[8], gradients[9], gradients[10], gradients[11])
```

```python
import functools

import jax
import jax.numpy as jnp
from jax import lax
from jax.experimental import pallas as pl
from jax.experimental.pallas import tpu as pltpu
from jax.sharding import PartitionSpec as P

HEADS = 16
HEAD_DIM = 64
BUCKETS = 32
TOP = 2
WINDOW = 1024

EPSILON = 1e-06
NEGATIVE = -1e30
LANES = 128
CHUNK = 256
FF_TILE = 256
VMEM_LIMIT = 58 * 2**20
BF16 = jnp.bfloat16
F32 = jnp.float32


def shift_ctx(block, distance):
    devices = range(lax.axis_size("ctx"))
    route = [(i - distance, i) for i in devices if i - distance in devices]
    return lax.ppermute(block, "ctx", route)


def norm_rows(values, gain):
    return values * lax.rsqrt(jnp.mean(values * values, axis=-1, keepdims=True) + EPSILON) * gain


def dot(left, right):
    return jnp.dot(left, right, preferred_element_type=F32)


def dot_rows(left, right):
    return lax.dot_general(left, right, (((0,), (0,)), ((), ())), preferred_element_type=F32)


def dot_last(left, right):
    return lax.dot_general(left, right, (((1,), (1,)), ((), ())), preferred_element_type=F32)


def params(**more):
    return pltpu.CompilerParams(vmem_limit_bytes=VMEM_LIMIT, **more)


def band_kernel(bias_ref, band_ref):
    blocks = WINDOW // LANES
    for a in range(blocks + 1):
        upper = bias_ref[0, :, (blocks + 1 - a) * LANES : (blocks + 2 - a) * LANES]
        lower = bias_ref[0, :, (blocks - a) * LANES : (blocks + 1 - a) * LANES]
        row = jnp.concatenate([upper, lower], axis=1)
        wide = jnp.broadcast_to(row, (LANES, 2 * LANES))
        rolled = pltpu.roll(wide, 0, 1, stride=1, stride_axis=0)
        band_ref[0, a * LANES : (a + 1) * LANES, :] = rolled[:, :LANES]


def make_band(bias_dist):
    edge = jnp.full((HEADS, LANES), NEGATIVE, F32)
    padded = jnp.concatenate([edge, bias_dist, edge], axis=1)[:, None, :]
    return pl.pallas_call(
        band_kernel,
        grid=(HEADS,),
        in_specs=[pl.BlockSpec((1, 1, WINDOW + 2 * LANES), lambda h: (h, 0, 0))],
        out_specs=pl.BlockSpec((1, WINDOW + LANES, LANES), lambda h: (h, 0, 0)),
        out_shape=jax.ShapeDtypeStruct((HEADS, WINDOW + LANES, LANES), F32),
        compiler_params=params(),
        name="bias_band",
    )(padded)


def unband_kernel(band_ref, dist_ref):
    blocks = WINDOW // LANES
    row = lax.broadcasted_iota(jnp.int32, (LANES, LANES), 0)
    column = lax.broadcasted_iota(jnp.int32, (LANES, LANES), 1)
    flip = (row + column == LANES - 1).astype(F32)
    sums = [None] * (blocks + 2)
    for a in range(blocks + 1):
        block = band_ref[0, a * LANES : (a + 1) * LANES, :]
        block = jnp.dot(flip, block, precision=lax.Precision.HIGHEST, preferred_element_type=F32)
        wide = jnp.concatenate([block, jnp.zeros((LANES, LANES), F32)], axis=1)
        rolled = pltpu.roll(wide, LANES + 1, 1, stride=1, stride_axis=0)
        total = jnp.sum(rolled, axis=0, keepdims=True)
        for place, part in ((blocks + 1 - a, total[:, :LANES]), (blocks - a, total[:, LANES:])):
            sums[place] = part if sums[place] is None else sums[place] + part
    dist_ref[0, :, :] = jnp.concatenate(sums[1 : blocks + 1], axis=1)


def sum_band(band_grad):
    return pl.pallas_call(
        unband_kernel,
        grid=(HEADS,),
        in_specs=[pl.BlockSpec((1, WINDOW + LANES, LANES), lambda h: (h, 0, 0))],
        out_specs=pl.BlockSpec((1, 1, WINDOW), lambda h: (h, 0, 0)),
        out_shape=jax.ShapeDtypeStruct((HEADS, 1, WINDOW), F32),
        compiler_params=params(),
        name="bias_band_sums",
    )(band_grad)[:, 0, :]


def head_lanes(head):
    lane = lax.broadcasted_iota(jnp.int32, (1, 2 * HEAD_DIM), 1)
    return (lane >= head * HEAD_DIM) & (lane < (head + 1) * HEAD_DIM)


def masked_scores(head, start, q_ref, k_ref, qdoc_ref, kdoc_ref):
    span = WINDOW + CHUNK
    mine = head_lanes(head)
    q_rows, k_rows = pl.ds(start, CHUNK), pl.ds(start, span)
    q_part = jnp.where(mine, q_ref[q_rows, :], qdoc_ref[q_rows, :])
    k_part = jnp.where(mine, k_ref[k_rows, :], kdoc_ref[k_rows, :])
    return dot_last(k_part, q_part)


def sub_blocks():
    return [(s * LANES, WINDOW + LANES) for s in range(CHUNK // LANES)]


def spread(parts):
    span = WINDOW + CHUNK
    columns = []
    for (first, rows), part in zip(sub_blocks(), parts):
        pieces = []
        if first:
            pieces.append(jnp.zeros((first, LANES), part.dtype))
        pieces.append(part)
        if span - first - rows:
            pieces.append(jnp.zeros((span - first - rows, LANES), part.dtype))
        columns.append(jnp.concatenate(pieces, axis=0) if len(pieces) > 1 else part)
    return jnp.concatenate(columns, axis=1)


def attend_kernel(q_ref, k_ref, v_ref, qdoc_ref, kdoc_ref, band_ref, o_ref, lse_ref):
    span = WINDOW + CHUNK
    for start in range(0, q_ref.shape[0], CHUNK):
        v_turned = v_ref[pl.ds(start, span), :].T
        outs = []
        for head in range(2):
            scores = masked_scores(head, start, q_ref, k_ref, qdoc_ref, kdoc_ref)
            band = band_ref[head]
            low, scale, logs = [], [], []
            for s, (first, rows) in enumerate(sub_blocks()):
                part = scores[first : first + rows, s * LANES : (s + 1) * LANES] + band
                top = jnp.max(part, axis=0, keepdims=True)
                expo = jnp.exp(part - top)
                total = jnp.sum(expo, axis=0, keepdims=True)
                low.append(expo.astype(BF16))
                scale.append(1.0 / total)
                logs.append(top + jnp.log(total))
            out = dot(v_turned[head * HEAD_DIM : (head + 1) * HEAD_DIM], spread(low))
            outs.append(out * jnp.concatenate(scale, axis=1))
            lse_ref[0, head : head + 1, pl.ds(start, CHUNK)] = jnp.concatenate(logs, axis=1)
        o_ref[pl.ds(start, CHUNK), :] = jnp.concatenate(outs, axis=0).T.astype(BF16)


def attend(queries, keys, values, query_doc, key_doc, band):
    rows, width = queries.shape
    keys_rows = keys.shape[0]
    pairs = HEADS // 2
    wide = 2 * HEAD_DIM
    cost = pl.CostEstimate(
        flops=4 * rows * WINDOW * width * 4,
        bytes_accessed=2 * (2 * keys_rows + 2 * rows) * width + 4 * HEADS * WINDOW * LANES,
        transcendentals=HEADS * rows * WINDOW,
    )
    return pl.pallas_call(
        attend_kernel,
        grid=(pairs,),
        in_specs=[
            pl.BlockSpec((rows, wide), lambda p: (0, p)),
            pl.BlockSpec((keys_rows, wide), lambda p: (0, p)),
            pl.BlockSpec((keys_rows, wide), lambda p: (0, p)),
            pl.BlockSpec((rows, wide), lambda p: (0, 0)),
            pl.BlockSpec((keys_rows, wide), lambda p: (0, 0)),
            pl.BlockSpec((2, WINDOW + LANES, LANES), lambda p: (p, 0, 0)),
        ],
        out_specs=[
            pl.BlockSpec((rows, wide), lambda p: (0, p)),
            pl.BlockSpec((1, 2, rows), lambda p: (p, 0, 0)),
        ],
        out_shape=[
            jax.ShapeDtypeStruct((rows, width), BF16),
            jax.ShapeDtypeStruct((pairs, 2, rows), F32),
        ],
        compiler_params=params(),
        cost_estimate=cost,
        name="attend",
    )(queries, keys, values, query_doc, key_doc, band)


def attend_back_kernel(
    q_ref, k_ref, v_ref, g_ref, o_ref, lse_ref, qdoc_ref, kdoc_ref, band_ref,
    dq_ref, dk_ref, dv_ref, dband_ref, dk_sum, dv_sum,
):
    span = WINDOW + CHUNK
    dk_sum[...] = jnp.zeros_like(dk_sum)
    dv_sum[...] = jnp.zeros_like(dv_sum)
    for start in range(0, q_ref.shape[0], CHUNK):
        q_rows, k_rows = pl.ds(start, CHUNK), pl.ds(start, span)
        k_turned = k_ref[k_rows, :].T
        product = (g_ref[q_rows, :].astype(F32) * o_ref[q_rows, :].astype(F32)).T
        dq_parts = []
        for head in range(2):
            mine = head_lanes(head)
            zero = jnp.zeros((), BF16)
            scores = masked_scores(head, start, q_ref, k_ref, qdoc_ref, kdoc_ref)
            g_part = jnp.where(mine, g_ref[q_rows, :], zero)
            q_part = jnp.where(mine, q_ref[q_rows, :], zero)
            prob_grad = dot_last(v_ref[k_rows, :], g_part)
            delta = jnp.sum(product[head * HEAD_DIM : (head + 1) * HEAD_DIM], axis=0, keepdims=True)
            lse = lse_ref[0, head : head + 1, q_rows]
            band = band_ref[head]
            prob_low, grad_low, grad_sum = [], [], None
            for s, (first, rows) in enumerate(sub_blocks()):
                lanes = slice(s * LANES, (s + 1) * LANES)
                probs = jnp.exp(scores[first : first + rows, lanes] + band - lse[:, lanes])
                grad = probs * (prob_grad[first : first + rows, lanes] - delta[:, lanes])
                prob_low.append(probs.astype(BF16))
                grad_low.append(grad.astype(BF16))
                grad_sum = grad if grad_sum is None else grad_sum + grad
            if start == 0:
                dband_ref[head] = grad_sum
            else:
                dband_ref[head] = dband_ref[head] + grad_sum
            grads = spread(grad_low)
            dk_sum[k_rows, :] += dot(grads, q_part)
            dv_sum[k_rows, :] += dot(spread(prob_low), g_part)
            dq_parts.append(dot(k_turned[head * HEAD_DIM : (head + 1) * HEAD_DIM], grads))
        turned = jnp.concatenate(dq_parts, axis=0).T
        dq_ref[q_rows, :] = (turned * HEAD_DIM ** (-0.5)).astype(BF16)
    dk_ref[...] = dk_sum[...].astype(BF16)
    dv_ref[...] = dv_sum[...].astype(BF16)


def attend_back(queries, keys, values, grad, out, lse, query_doc, key_doc, band):
    rows, width = queries.shape
    keys_rows = keys.shape[0]
    pairs = HEADS // 2
    wide = 2 * HEAD_DIM
    cost = pl.CostEstimate(
        flops=10 * rows * WINDOW * width * 4,
        bytes_accessed=2 * (4 * keys_rows + 4 * rows) * width + 8 * HEADS * WINDOW * LANES,
        transcendentals=HEADS * rows * WINDOW,
    )
    q_spec = pl.BlockSpec((rows, wide), lambda p: (0, p))
    k_spec = pl.BlockSpec((keys_rows, wide), lambda p: (0, p))
    band_spec = pl.BlockSpec((2, WINDOW + LANES, LANES), lambda p: (p, 0, 0))
    return pl.pallas_call(
        attend_back_kernel,
        grid=(pairs,),
        in_specs=[
            q_spec,
            k_spec,
            k_spec,
            q_spec,
            q_spec,
            pl.BlockSpec((1, 2, rows), lambda p: (p, 0, 0)),
            pl.BlockSpec((rows, wide), lambda p: (0, 0)),
            pl.BlockSpec((keys_rows, wide), lambda p: (0, 0)),
            band_spec,
        ],
        out_specs=[q_spec, k_spec, k_spec, band_spec],
        out_shape=[
            jax.ShapeDtypeStruct((rows, width), BF16),
            jax.ShapeDtypeStruct((keys_rows, width), BF16),
            jax.ShapeDtypeStruct((keys_rows, width), BF16),
            jax.ShapeDtypeStruct((HEADS, WINDOW + LANES, LANES), F32),
        ],
        scratch_shapes=[pltpu.VMEM((keys_rows, wide), F32), pltpu.VMEM((keys_rows, wide), F32)],
        compiler_params=params(),
        cost_estimate=cost,
        name="attend_back",
    )(queries, keys, values, grad, out, lse, query_doc, key_doc, band)


def expert_kernel(
    x_ref, c_ref, names_ref, router_ref, gate_ref, up_ref, down_ref,
    made_ref, back_ref, drouter_ref, dgate_ref, dup_ref, ddown_ref,
    x_turned, grad_low, gate_col, hidden_s, dgate_s, dup_s, made_sum, back_sum,
):
    step = pl.program_id(0)
    last = pl.num_programs(0) - 1
    rows, width = x_ref.shape
    tile = 256
    lane = lax.broadcasted_iota(jnp.int32, (1, LANES), 1)
    own = lane == lax.axis_index("exp")

    def each_tile(body):
        def loop(i, carry):
            body(pl.ds(pl.multiple_of(i * tile, tile), tile))
            return carry

        lax.fori_loop(0, rows // tile, loop, 0)

    @pl.when(step == 0)
    def _():
        def start(at):
            x = x_ref[at, :]
            names = names_ref[at, :].astype(F32)
            logits = dot_last(x, router_ref[...]) * names
            mine = jnp.sum(jnp.where(own, logits, 0.0), axis=1, keepdims=True)
            theirs = jnp.sum(jnp.where(own, 0.0, logits), axis=1, keepdims=True)
            gate = jax.nn.sigmoid(mine - theirs)
            gate_col[at, :] = jnp.broadcast_to(gate, (tile, LANES))
            grad_low[at, :] = (gate * c_ref[at, :].astype(F32)).astype(BF16)
            x_turned[:, at] = x.T
            made_sum[at, :] = jnp.zeros((tile, width), F32)
            back_sum[at, :] = jnp.zeros((tile, width), F32)

        each_tile(start)

    def middle(at):
        x = x_ref[at, :]
        grad = grad_low[at, :]
        gate_pre = dot(x, gate_ref[...])
        up_pre = dot(x, up_ref[...])
        hidden_grad = dot_last(grad, down_ref[...])
        root = 0.7978845608028654
        square = gate_pre * gate_pre
        bent = jnp.tanh(gate_pre * (root + root * 0.044715 * square))
        half = 0.5 * (1.0 + bent)
        act = gate_pre * half
        slope = half + 0.5 * gate_pre * (1.0 - bent * bent) * (root + 3.0 * root * 0.044715 * square)
        hidden = (act * up_pre).astype(BF16)
        dgate = (hidden_grad * up_pre * slope).astype(BF16)
        dup = (hidden_grad * act).astype(BF16)
        hidden_s[at, :] = hidden
        dgate_s[at, :] = dgate
        dup_s[at, :] = dup
        made_sum[at, :] += dot(hidden, down_ref[...])
        back_sum[at, :] += dot_last(dgate, gate_ref[...]) + dot_last(dup, up_ref[...])

    each_tile(middle)

    def weights(i, carry):
        at = pl.ds(pl.multiple_of(i * tile, tile), tile)
        turned = x_turned[at, :]
        dgate_ref[at, :] = dot(turned, dgate_s[...]).astype(BF16)
        dup_ref[at, :] = dot(turned, dup_s[...]).astype(BF16)
        return carry

    lax.fori_loop(0, width // tile, weights, 0)
    ddown_ref[...] = dot(hidden_s[...].T, grad_low[...]).astype(BF16)

    @pl.when(step == last)
    def _():
        drouter_ref[...] = jnp.zeros_like(drouter_ref)

        def finish(at):
            made = made_sum[at, :].astype(BF16).astype(F32)
            gate = gate_col[at, :][:, :1]
            names = names_ref[at, :].astype(F32)
            push = jnp.sum(c_ref[at, :].astype(F32) * made, axis=1, keepdims=True)
            push = push * gate * (1.0 - gate)
            logits_grad = push * jnp.where(own, names, -names)
            high = logits_grad.astype(BF16)
            low = (logits_grad - high.astype(F32)).astype(BF16)
            back_ref[at, :] = (back_sum[at, :] + dot(high, router_ref[...]) + dot(low, router_ref[...])).astype(BF16)
            drouter_ref[...] += dot(x_turned[:, at], high) + dot(x_turned[:, at], low)
            made_ref[at, :] = (gate * made).astype(BF16)

        each_tile(finish)


def run_expert(rows_in, cot_in, names_in, router_turned, gate_w, up_w, down_w):
    rows, width = rows_in.shape
    units = gate_w.shape[1]
    whole = lambda f: (0, 0)
    cost = pl.CostEstimate(
        flops=18 * rows * width * units,
        bytes_accessed=12 * units * width + 10 * rows * width,
        transcendentals=rows * units,
    )
    return pl.pallas_call(
        expert_kernel,
        grid=(units // FF_TILE,),
        in_specs=[
            pl.BlockSpec((rows, width), whole),
            pl.BlockSpec((rows, width), whole),
            pl.BlockSpec((rows, LANES), whole),
            pl.BlockSpec((LANES, width), whole),
            pl.BlockSpec((width, FF_TILE), lambda f: (0, f)),
            pl.BlockSpec((width, FF_TILE), lambda f: (0, f)),
            pl.BlockSpec((FF_TILE, width), lambda f: (f, 0)),
        ],
        out_specs=[
            pl.BlockSpec((rows, width), whole),
            pl.BlockSpec((rows, width), whole),
            pl.BlockSpec((width, LANES), whole),
            pl.BlockSpec((width, FF_TILE), lambda f: (0, f)),
            pl.BlockSpec((width, FF_TILE), lambda f: (0, f)),
            pl.BlockSpec((FF_TILE, width), lambda f: (f, 0)),
        ],
        out_shape=[
            jax.ShapeDtypeStruct((rows, width), BF16),
            jax.ShapeDtypeStruct((rows, width), BF16),
            jax.ShapeDtypeStruct((width, LANES), F32),
            jax.ShapeDtypeStruct((width, units), BF16),
            jax.ShapeDtypeStruct((width, units), BF16),
            jax.ShapeDtypeStruct((units, width), BF16),
        ],
        scratch_shapes=[
            pltpu.VMEM((width, rows), BF16),
            pltpu.VMEM((rows, width), BF16),
            pltpu.VMEM((rows, LANES), F32),
            pltpu.VMEM((rows, FF_TILE), BF16),
            pltpu.VMEM((rows, FF_TILE), BF16),
            pltpu.VMEM((rows, FF_TILE), BF16),
            pltpu.VMEM((rows, width), F32),
            pltpu.VMEM((rows, width), F32),
        ],
        compiler_params=params(),
        cost_estimate=cost,
        name="expert",
    )(rows_in, cot_in, names_in, router_turned, gate_w, up_w, down_w)


def exchange(blocks):
    return lax.all_to_all(blocks, "exp", split_axis=0, concat_axis=0, tiled=True)


def body(
    tokens,
    w_query,
    w_key,
    w_value,
    w_out,
    w_router,
    gain_attn,
    gain_mlp,
    pos_bias,
    exp_gate,
    exp_up,
    exp_down,
    doc_lengths,
    bucket_of,
    expert_ids,
    cotangent,
):
    both = ("ctx", "exp")
    own_tokens = tokens[0]
    rows, width = own_tokens.shape
    experts = w_router.shape[1]
    capacity = (5 * TOP * rows + 4 * experts - 1) // (4 * experts)
    reach = (WINDOW + rows - 2) // rows
    scale = HEAD_DIM ** (-0.5)
    ctx_index = lax.axis_index("ctx")
    exp_index = lax.axis_index("exp")
    part = w_query.shape[0]
    bias_part = pos_bias.shape[0]
    devices = width // part

    small = jnp.concatenate([w_router.reshape(-1), gain_attn, gain_mlp, pos_bias])
    small = jnp.pad(small, (0, width - small.shape[0]))[None]
    packed = jnp.concatenate([small, w_query, w_key, w_value, w_out], axis=0)
    gathered = lax.all_gather(packed, both, axis=0)
    full_query, full_key, full_value, full_out = (
        gathered[:, 1 + i * part : 1 + (i + 1) * part].reshape(width, width) for i in range(4)
    )
    small = gathered[:, 0]
    at = part * experts
    full_router = small[:, :at].reshape(width, experts)
    full_gain_attn = small[:, at : at + part].reshape(width).astype(F32)
    full_gain_mlp = small[:, at + part : at + 2 * part].reshape(width).astype(F32)
    table = small[:, at + 2 * part : at + 2 * part + bias_part].reshape(HEADS, BUCKETS)
    gate_w = lax.all_gather(exp_gate[0], "ctx", axis=0, tiled=True)
    up_w = lax.all_gather(exp_up[0], "ctx", axis=0, tiled=True)
    down_w = lax.all_gather(exp_down[0], "ctx", axis=0, tiled=True)

    halo = [own_tokens]
    for _ in range(reach):
        halo.insert(0, shift_ctx(halo[0], 1))
    inputs_all = jnp.concatenate(halo, axis=0).astype(F32)
    inputs = own_tokens.astype(F32)

    expert_range = jnp.arange(experts, dtype=jnp.int32)
    named = jnp.any(expert_ids[0][:, :, None] == expert_range, axis=1)
    named_low = named.astype(BF16)
    step = jnp.arange(rows, dtype=jnp.int32)
    earlier = (step[:, None] > step[None, :]).astype(BF16)
    slots = dot(earlier, named_low).astype(jnp.int32)
    slots = jnp.where(named, slots, -1).T
    routes = (slots[:, None, :] == jnp.arange(capacity, dtype=jnp.int32)[None, :, None]).astype(BF16)
    routes = routes.reshape(experts * capacity, rows)

    names = jnp.pad(named_low, ((0, 0), (0, LANES - experts)))
    early = dot(routes, jnp.concatenate([cotangent[0], names], axis=1)).astype(BF16)
    early = exchange(early.reshape(experts, capacity, width + LANES)).reshape(-1, width + LANES)
    cot_in, names_in = early[:, :width], early[:, width:]

    onehot_bucket = (bucket_of[None, :] == jnp.arange(BUCKETS, dtype=jnp.int32)[:, None]).astype(BF16)
    band = make_band(dot(table, onehot_bucket))
    ends = jnp.cumsum(doc_lengths[0])

    def documents(positions):
        return jnp.sum((positions[:, None] >= ends[None, :]).astype(jnp.int32), axis=1)[:, None]

    feature = (jnp.arange(2 * HEAD_DIM, dtype=jnp.int32) % HEAD_DIM)[None, :]
    docs = doc_lengths.shape[1] + 1
    query_pos = ctx_index * rows + step
    key_pos = (ctx_index - reach) * rows + jnp.arange((reach + 1) * rows, dtype=jnp.int32)
    query_doc = (feature == documents(query_pos)).astype(BF16)
    same = (feature == documents(key_pos)) & (key_pos[:, None] >= 0)
    key_doc = jnp.where(same | (feature >= docs), 0.0, NEGATIVE).astype(BF16)

    normed_all = norm_rows(inputs_all, full_gain_attn).astype(BF16)
    normed = normed_all[reach * rows :]
    queries = (dot(normed, full_query).astype(BF16)) * jnp.asarray(scale, BF16)
    keys = dot(normed_all, full_key).astype(BF16)
    values = dot(normed_all, full_value).astype(BF16)
    attended, lse = attend(queries, keys, values, query_doc, key_doc, band)
    middle = inputs + dot(attended, full_out)
    normed_mlp = norm_rows(middle, full_gain_mlp).astype(BF16)

    sent = dot(routes, normed_mlp).astype(BF16)
    arrived = exchange(sent.reshape(experts, capacity, width)).reshape(-1, width)
    router_turned = jnp.pad(full_router.T, ((0, LANES - experts), (0, 0)))
    made, back, router_grad, gate_grad, up_grad, down_grad = run_expert(
        arrived, cot_in, names_in, router_turned, gate_w, up_w, down_w
    )
    back = exchange(back.reshape(experts, capacity, width)).reshape(-1, width)
    made = exchange(made.reshape(experts, capacity, width)).reshape(-1, width)
    output = (middle + dot_rows(routes, made)).astype(BF16)
    expert_grads = [
        lax.psum_scatter(grad, "ctx", scatter_dimension=0, tiled=True).astype(F32)[None]
        for grad in (gate_grad, up_grad, down_grad)
    ]

    upstream = cotangent[0].astype(F32)
    normed_mlp_grad = dot_rows(routes, back)
    _, second_pull = jax.vjp(norm_rows, middle, full_gain_mlp)
    middle_norm_grad, gain_mlp_grad = second_pull(normed_mlp_grad)
    middle_grad = upstream + middle_norm_grad
    branch_grad = middle_grad.astype(BF16)
    out_grad = dot_rows(attended, branch_grad)
    attended_grad = dot_last(branch_grad, full_out).astype(BF16)
    query_grad, key_grad, value_grad, band_grad = attend_back(
        queries, keys, values, attended_grad, attended, lse, query_doc, key_doc, band
    )
    bias_grad = jnp.dot(
        sum_band(band_grad), onehot_bucket.T.astype(F32), precision=lax.Precision.HIGHEST
    )

    normed_grad_all = dot_last(key_grad, full_key) + dot_last(value_grad, full_value)
    own_grad = normed_grad_all[reach * rows :] + dot_last(query_grad, full_query)
    halo_grad = normed_grad_all[: reach * rows]
    returning = None
    for stride in range(reach, 0, -1):
        piece = halo_grad[(reach - stride) * rows : (reach - stride + 1) * rows]
        piece = piece if returning is None else piece + returning.astype(F32)
        returning = shift_ctx(piece.astype(BF16), -1)
    _, first_pull = jax.vjp(norm_rows, inputs_all, full_gain_attn)
    gain_attn_grad = first_pull(jnp.concatenate([halo_grad, own_grad], axis=0))[1]
    _, own_pull = jax.vjp(norm_rows, inputs, full_gain_attn)
    input_grad = middle_grad + own_pull(own_grad + returning.astype(F32))[0]

    bias_column = jnp.pad(bias_grad.reshape(devices, bias_part), ((0, 0), (0, part - bias_part)))
    tail = jnp.concatenate(
        [
            router_grad[:, :experts],
            gain_attn_grad[:, None],
            gain_mlp_grad[:, None],
            bias_column.reshape(width, 1),
        ],
        axis=1,
    )
    tail = jnp.pad(tail, ((0, 0), (0, LANES - tail.shape[1])))
    grads = jnp.concatenate(
        [
            dot_rows(normed, query_grad),
            dot_rows(normed_all, key_grad),
            dot_rows(normed_all, value_grad),
            tail,
        ],
        axis=1,
    )
    out_sum = lax.psum_scatter(out_grad, both, scatter_dimension=0, tiled=True)
    sums = lax.psum_scatter(grads, both, scatter_dimension=0, tiled=True)
    tail = sums[:, 3 * width :]
    return (
        output[None],
        input_grad[None],
        sums[:, :width],
        sums[:, width : 2 * width],
        sums[:, 2 * width : 3 * width],
        out_sum,
        tail[:, :experts],
        tail[:, experts],
        tail[:, experts + 1],
        tail[:bias_part, experts + 2],
        expert_grads[0],
        expert_grads[1],
        expert_grads[2],
    )


def solution(mesh):
    rows3 = P("exp", "ctx", None)
    dense2 = P(("ctx", "exp"), None)
    dense1 = P(("ctx", "exp"))
    return jax.shard_map(
        body,
        mesh=mesh,
        in_specs=(
            rows3,
            dense2,
            dense2,
            dense2,
            dense2,
            dense2,
            dense1,
            dense1,
            dense1,
            rows3,
            rows3,
            rows3,
            P("exp", None),
            P(),
            rows3,
            rows3,
        ),
        out_specs=(
            rows3,
            rows3,
            dense2,
            dense2,
            dense2,
            dense2,
            dense2,
            dense1,
            dense1,
            dense1,
            rows3,
            rows3,
            rows3,
        ),
        check_vma=False,
    )
```

```python
import functools

import jax
import jax.numpy as jnp
from jax import lax
from jax.experimental import pallas as pl
from jax.experimental.pallas import tpu as pltpu
from jax.sharding import PartitionSpec as P

HEADS = 16
HEAD_DIM = 64
BUCKETS = 32
TOP = 2
WINDOW = 1024

EPSILON = 1e-06
NEGATIVE = -1e30
LANES = 128
CHUNK = 256
FF_TILE = 256
ROW_TILE = 256
VMEM_LIMIT = 58 * 2**20
BF16 = jnp.bfloat16
F32 = jnp.float32


def shift_ctx(block, distance):
    devices = range(lax.axis_size("ctx"))
    route = [(i - distance, i) for i in devices if i - distance in devices]
    return lax.ppermute(block, "ctx", route)


def norm_rows(values, gain):
    return values * lax.rsqrt(jnp.mean(values * values, axis=-1, keepdims=True) + EPSILON) * gain


def dot(left, right):
    return jnp.dot(left, right, preferred_element_type=F32)


def dot_rows(left, right):
    return lax.dot_general(left, right, (((0,), (0,)), ((), ())), preferred_element_type=F32)


def dot_last(left, right):
    return lax.dot_general(left, right, (((1,), (1,)), ((), ())), preferred_element_type=F32)


def params(**more):
    return pltpu.CompilerParams(vmem_limit_bytes=VMEM_LIMIT, **more)


def brief():
    return pl.CostEstimate(flops=2**20, bytes_accessed=2**20, transcendentals=0)


def band_kernel(bias_ref, band_ref):
    blocks = WINDOW // LANES
    size = (blocks + 2) * LANES
    for head in range(bias_ref.shape[0]):
        row = jnp.broadcast_to(bias_ref[head : head + 1, :], (8, size))
        eight = pltpu.roll(row, 0, 1, stride=1, stride_axis=0)
        for group in range(LANES // 8):
            wide = pltpu.roll(eight, 8 * group, 1) if group else eight
            for a in range(blocks + 1):
                first = a * LANES + group * 8
                at = (blocks + 1 - a) * LANES
                band_ref[head, first : first + 8, :] = wide[:, at : at + LANES]


def make_band(bias_dist):
    group = 8
    edge = jnp.full((HEADS, LANES), NEGATIVE, F32)
    padded = jnp.concatenate([edge, bias_dist, edge], axis=1)
    return pl.pallas_call(
        band_kernel,
        grid=(HEADS // group,),
        in_specs=[pl.BlockSpec((group, WINDOW + 2 * LANES), lambda h: (h, 0))],
        out_specs=pl.BlockSpec((group, WINDOW + LANES, LANES), lambda h: (h, 0, 0)),
        out_shape=jax.ShapeDtypeStruct((HEADS, WINDOW + LANES, LANES), F32),
        compiler_params=params(),
        cost_estimate=brief(),
        name="bias_band",
    )(padded)


def unband_kernel(band_ref, dist_ref):
    blocks = WINDOW // LANES
    size = (blocks + 2) * LANES
    row = lax.broadcasted_iota(jnp.int32, (8, 1), 0)
    edge = jnp.zeros((8, LANES), F32)
    for head in range(band_ref.shape[0]):
        total = None
        for group in range(LANES // 8):
            pieces = [edge]
            for a in range(blocks, -1, -1):
                first = a * LANES + group * 8
                pieces.append(band_ref[head, first : first + 8, :])
            wide = jnp.concatenate(pieces, axis=1)
            if group:
                wide = pltpu.roll(wide, size - 8 * group, 1)
            total = wide if total is None else total + wide
        dist = jnp.zeros_like(total)
        for r in range(8):
            turned = pltpu.roll(total, size - r, 1) if r else total
            dist = dist + jnp.where(row == r, turned, 0.0)
        dist_ref[head : head + 1, :] = jnp.sum(dist, axis=0, keepdims=True)[:, LANES : LANES + WINDOW]


def sum_band(band_grad):
    group = 8
    return pl.pallas_call(
        unband_kernel,
        grid=(HEADS // group,),
        in_specs=[pl.BlockSpec((group, WINDOW + LANES, LANES), lambda h: (h, 0, 0))],
        out_specs=pl.BlockSpec((group, WINDOW), lambda h: (h, 0)),
        out_shape=jax.ShapeDtypeStruct((HEADS, WINDOW), F32),
        compiler_params=params(),
        cost_estimate=brief(),
        name="bias_band_sums",
    )(band_grad)


def head_lanes(head):
    lane = lax.broadcasted_iota(jnp.int32, (1, 2 * HEAD_DIM), 1)
    return (lane >= head * HEAD_DIM) & (lane < (head + 1) * HEAD_DIM)


def masked_scores(head, start, q_ref, k_ref, qdoc_ref, kdoc_ref):
    span = WINDOW + CHUNK
    mine = head_lanes(head)
    q_rows, k_rows = pl.ds(start, CHUNK), pl.ds(start, span)
    q_part = jnp.where(mine, q_ref[q_rows, :], qdoc_ref[q_rows, :])
    k_part = jnp.where(mine, k_ref[k_rows, :], kdoc_ref[k_rows, :])
    return dot_last(k_part, q_part)


def sub_blocks():
    return [(s * LANES, WINDOW + LANES) for s in range(CHUNK // LANES)]


def spread(parts):
    span = WINDOW + CHUNK
    columns = []
    for (first, rows), part in zip(sub_blocks(), parts):
        pieces = []
        if first:
            pieces.append(jnp.zeros((first, LANES), part.dtype))
        pieces.append(part)
        if span - first - rows:
            pieces.append(jnp.zeros((span - first - rows, LANES), part.dtype))
        columns.append(jnp.concatenate(pieces, axis=0) if len(pieces) > 1 else part)
    return jnp.concatenate(columns, axis=1)


def attend_kernel(q_ref, k_ref, v_ref, qdoc_ref, kdoc_ref, band_ref, o_ref, lse_ref):
    span = WINDOW + CHUNK
    for start in range(0, q_ref.shape[0], CHUNK):
        v_turned = v_ref[pl.ds(start, span), :].T
        outs = []
        for head in range(2):
            scores = masked_scores(head, start, q_ref, k_ref, qdoc_ref, kdoc_ref)
            band = band_ref[head]
            low, scale, logs = [], [], []
            for s, (first, rows) in enumerate(sub_blocks()):
                part = scores[first : first + rows, s * LANES : (s + 1) * LANES] + band
                top = jnp.max(part, axis=0, keepdims=True)
                expo = jnp.exp(part - top)
                total = jnp.sum(expo, axis=0, keepdims=True)
                low.append(expo.astype(BF16))
                scale.append(1.0 / total)
                logs.append(top + jnp.log(total))
            out = dot(v_turned[head * HEAD_DIM : (head + 1) * HEAD_DIM], spread(low))
            outs.append(out * jnp.concatenate(scale, axis=1))
            lse_ref[0, head : head + 1, pl.ds(start, CHUNK)] = jnp.concatenate(logs, axis=1)
        o_ref[pl.ds(start, CHUNK), :] = jnp.concatenate(outs, axis=0).T.astype(BF16)


def attend(queries, keys, values, query_doc, key_doc, band):
    rows, width = queries.shape
    keys_rows = keys.shape[0]
    pairs = HEADS // 2
    wide = 2 * HEAD_DIM
    return pl.pallas_call(
        attend_kernel,
        grid=(pairs,),
        in_specs=[
            pl.BlockSpec((rows, wide), lambda p: (0, p)),
            pl.BlockSpec((keys_rows, wide), lambda p: (0, p)),
            pl.BlockSpec((keys_rows, wide), lambda p: (0, p)),
            pl.BlockSpec((rows, wide), lambda p: (0, 0)),
            pl.BlockSpec((keys_rows, wide), lambda p: (0, 0)),
            pl.BlockSpec((2, WINDOW + LANES, LANES), lambda p: (p, 0, 0)),
        ],
        out_specs=[
            pl.BlockSpec((rows, wide), lambda p: (0, p)),
            pl.BlockSpec((1, 2, rows), lambda p: (p, 0, 0)),
        ],
        out_shape=[
            jax.ShapeDtypeStruct((rows, width), BF16),
            jax.ShapeDtypeStruct((pairs, 2, rows), F32),
        ],
        compiler_params=params(),
        cost_estimate=brief(),
        name="attend",
    )(queries, keys, values, query_doc, key_doc, band)


def attend_back_kernel(
    q_ref, k_ref, v_ref, g_ref, o_ref, lse_ref, qdoc_ref, kdoc_ref, band_ref,
    dq_ref, dk_ref, dv_ref, dband_ref, dk_sum, dv_sum,
):
    span = WINDOW + CHUNK
    dk_sum[...] = jnp.zeros_like(dk_sum)
    dv_sum[...] = jnp.zeros_like(dv_sum)
    for start in range(0, q_ref.shape[0], CHUNK):
        q_rows, k_rows = pl.ds(start, CHUNK), pl.ds(start, span)
        k_turned = k_ref[k_rows, :].T
        product = (g_ref[q_rows, :].astype(F32) * o_ref[q_rows, :].astype(F32)).T
        dq_parts = []
        for head in range(2):
            mine = head_lanes(head)
            zero = jnp.zeros((), BF16)
            scores = masked_scores(head, start, q_ref, k_ref, qdoc_ref, kdoc_ref)
            g_part = jnp.where(mine, g_ref[q_rows, :], zero)
            q_part = jnp.where(mine, q_ref[q_rows, :], zero)
            prob_grad = dot_last(v_ref[k_rows, :], g_part)
            delta = jnp.sum(product[head * HEAD_DIM : (head + 1) * HEAD_DIM], axis=0, keepdims=True)
            lse = lse_ref[0, head : head + 1, q_rows]
            band = band_ref[head]
            prob_low, grad_low, grad_sum = [], [], None
            for s, (first, rows) in enumerate(sub_blocks()):
                lanes = slice(s * LANES, (s + 1) * LANES)
                probs = jnp.exp(scores[first : first + rows, lanes] + band - lse[:, lanes])
                grad = probs * (prob_grad[first : first + rows, lanes] - delta[:, lanes])
                prob_low.append(probs.astype(BF16))
                grad_low.append(grad.astype(BF16))
                grad_sum = grad if grad_sum is None else grad_sum + grad
            if start == 0:
                dband_ref[head] = grad_sum
            else:
                dband_ref[head] = dband_ref[head] + grad_sum
            grads = spread(grad_low)
            dk_sum[k_rows, :] += dot(grads, q_part)
            dv_sum[k_rows, :] += dot(spread(prob_low), g_part)
            dq_parts.append(dot(k_turned[head * HEAD_DIM : (head + 1) * HEAD_DIM], grads))
        turned = jnp.concatenate(dq_parts, axis=0).T
        dq_ref[q_rows, :] = (turned * HEAD_DIM ** (-0.5)).astype(BF16)
    dk_ref[...] = dk_sum[...].astype(BF16)
    dv_ref[...] = dv_sum[...].astype(BF16)


def attend_back(queries, keys, values, grad, out, lse, query_doc, key_doc, band):
    rows, width = queries.shape
    keys_rows = keys.shape[0]
    pairs = HEADS // 2
    wide = 2 * HEAD_DIM
    q_spec = pl.BlockSpec((rows, wide), lambda p: (0, p))
    k_spec = pl.BlockSpec((keys_rows, wide), lambda p: (0, p))
    band_spec = pl.BlockSpec((2, WINDOW + LANES, LANES), lambda p: (p, 0, 0))
    return pl.pallas_call(
        attend_back_kernel,
        grid=(pairs,),
        in_specs=[
            q_spec,
            k_spec,
            k_spec,
            q_spec,
            q_spec,
            pl.BlockSpec((1, 2, rows), lambda p: (p, 0, 0)),
            pl.BlockSpec((rows, wide), lambda p: (0, 0)),
            pl.BlockSpec((keys_rows, wide), lambda p: (0, 0)),
            band_spec,
        ],
        out_specs=[q_spec, k_spec, k_spec, band_spec],
        out_shape=[
            jax.ShapeDtypeStruct((rows, width), BF16),
            jax.ShapeDtypeStruct((keys_rows, width), BF16),
            jax.ShapeDtypeStruct((keys_rows, width), BF16),
            jax.ShapeDtypeStruct((HEADS, WINDOW + LANES, LANES), F32),
        ],
        scratch_shapes=[pltpu.VMEM((keys_rows, wide), F32), pltpu.VMEM((keys_rows, wide), F32)],
        compiler_params=params(),
        cost_estimate=brief(),
        name="attend_back",
    )(queries, keys, values, grad, out, lse, query_doc, key_doc, band)


def down_blocks(units, width, count):
    held, share = width // count, units // count
    spare = held - share
    if not spare:
        return [((0, 0), (0, 0), (units, width))]
    wide = width * share // held
    blocks = []
    for z in range(count):
        blocks.append(((z * held, 0), (z * share, 0), (share, wide)))
        for m in range(share // spare):
            thin = width - wide
            blocks.append(((z * held + share, m * thin), (z * share + m * spare, wide), (spare, thin)))
    return blocks


def expert_kernel(first, last, units, count, *refs):
    refs = list(refs)
    take = lambda: refs.pop(0)
    x_ref, chunk_ref = take(), take()
    if first or last:
        c_ref, names_ref, router_ref = take(), take(), take()
    if not first:
        low_ref, made_in, back_in = take(), take(), take()
    if last and not first:
        gate_in = take()
    hidden_ref, dboth_ref = take(), take()
    if first:
        low_out = take()
    if first and not last:
        gate_out = take()
    made_ref, back_ref = take(), take()
    if last:
        drouter_ref = take()
    down_s = take()
    rows, width = x_ref.shape
    x = x_ref[...]
    own = lax.broadcasted_iota(jnp.int32, (1, LANES), 1) == lax.axis_index("exp")
    if first:
        names = names_ref[...].astype(F32)
        logits = dot_last(x, router_ref[...]) * names
        mine = jnp.sum(jnp.where(own, logits, 0.0), axis=1, keepdims=True)
        theirs = jnp.sum(jnp.where(own, 0.0, logits), axis=1, keepdims=True)
        gate = jax.nn.sigmoid(mine - theirs)
        low_out[...] = (gate * c_ref[...].astype(F32)).astype(BF16)
        if not last:
            gate_out[...] = jnp.broadcast_to(gate, (rows, LANES))
        low_ref = low_out
    elif last:
        gate = gate_in[...][:, :1]
    @pl.when(pl.program_id(0) == 0)
    def _():
        for (row, column), (to_row, to_column), (high, wide) in down_blocks(units, width, count):
            from_columns = slice(2 * units + column, 2 * units + column + wide)
            down_s[to_row : to_row + high, to_column : to_column + wide] = chunk_ref[row : row + high, from_columns]

    for t in range(units // FF_TILE):
        at = slice(t * FF_TILE, (t + 1) * FF_TILE)
        up_at = slice(units + t * FF_TILE, units + (t + 1) * FF_TILE)
        gate_pre = dot(x, chunk_ref[:, at])
        up_pre = dot(x, chunk_ref[:, up_at])
        hidden_grad = dot_last(low_ref[...], down_s[at, :])
        root = 0.7978845608028654
        square = gate_pre * gate_pre
        bent = jnp.tanh(gate_pre * (root + root * 0.044715 * square))
        half = 0.5 * (1.0 + bent)
        act = gate_pre * half
        slope = half + 0.5 * gate_pre * (1.0 - bent * bent) * (root + 3.0 * root * 0.044715 * square)
        hidden_ref[:, at] = (act * up_pre).astype(BF16)
        dboth_ref[:, at] = (hidden_grad * up_pre * slope).astype(BF16)
        dboth_ref[:, up_at] = (hidden_grad * act).astype(BF16)
    made = dot(hidden_ref[...], down_s[...])
    back = dot_last(dboth_ref[...], chunk_ref[:, : 2 * units])
    if not first:
        made = made + made_in[...]
        back = back + back_in[...]
    if last:
        made = made.astype(BF16).astype(F32)
        names = names_ref[...].astype(F32)
        push = jnp.sum(c_ref[...].astype(F32) * made, axis=1, keepdims=True)
        push = push * gate * (1.0 - gate)
        logits_grad = push * jnp.where(own, names, -names)
        high = logits_grad.astype(BF16)
        low = (logits_grad - high.astype(F32)).astype(BF16)
        made = gate * made
        back = back + dot(high, router_ref[...]) + dot(low, router_ref[...])
        turned = x.T
        update = dot(turned, high) + dot(turned, low)

        @pl.when(pl.program_id(0) == 0)
        def _():
            drouter_ref[...] = update

        @pl.when(pl.program_id(0) > 0)
        def _():
            drouter_ref[...] += update

    made_ref[...] = made.astype(made_ref.dtype)
    back_ref[...] = back.astype(back_ref.dtype)


def run_expert(first, last, units, count, x, chunk, extras, carried):
    rows, width = x.shape
    whole = lambda i: (0, 0)
    step = lambda i: (i, 0)
    wide = pl.BlockSpec((ROW_TILE, width), step)
    thin = pl.BlockSpec((ROW_TILE, LANES), step)
    struct = jax.ShapeDtypeStruct
    cot_in, names_in, router = extras
    operands = [x, chunk]
    in_specs = [wide, pl.BlockSpec(chunk.shape, whole, pipeline_mode=pl.Buffered(1))]
    if first or last:
        operands += [cot_in, names_in, router]
        in_specs += [wide, thin, pl.BlockSpec((LANES, width), whole)]
    if not first:
        low, made, back, gate = carried
        operands += [low, made, back]
        in_specs += [wide, wide, wide]
        if last:
            operands.append(gate)
            in_specs.append(thin)
    out_shape = [struct((rows, units), BF16), struct((rows, 2 * units), BF16)]
    out_specs = [pl.BlockSpec((ROW_TILE, units), step), pl.BlockSpec((ROW_TILE, 2 * units), step)]
    if first:
        out_shape.append(struct((rows, width), BF16))
        out_specs.append(wide)
        if not last:
            out_shape.append(struct((rows, LANES), F32))
            out_specs.append(thin)
    kept = BF16 if last else F32
    out_shape += [struct((rows, width), kept), struct((rows, width), kept)]
    out_specs += [wide, wide]
    if last:
        out_shape.append(struct((width, LANES), F32))
        out_specs.append(pl.BlockSpec((width, LANES), whole))
    outs = list(
        pl.pallas_call(
            functools.partial(expert_kernel, first, last, units, count),
            grid=(rows // ROW_TILE,),
            in_specs=in_specs,
            out_specs=out_specs,
            out_shape=out_shape,
            scratch_shapes=[pltpu.VMEM((units, width), BF16)],
            compiler_params=params(),
            cost_estimate=brief(),
            name="expert",
        )(*operands)
    )
    hidden, dboth = outs[:2]
    if first:
        low = outs[2]
        gate = None if last else outs[3]
    if last:
        made, back, drouter = outs[-3:]
        return hidden, dboth, (low, made, back, gate), drouter
    made, back = outs[-2:]
    return hidden, dboth, (low, made, back, gate), None


def expert_weights_kernel(units, count, x_ref, low_ref, dboth_ref, hidden_ref, grad_ref, x_turned, hidden_turned, rest):
    step = pl.program_id(0)
    tile = low_ref.shape[1]
    width = x_ref.shape[1]
    both_steps = 2 * units // tile

    @pl.when(step == 0)
    def _():
        x_turned[...] = x_ref[...].T

    @pl.when(step < both_steps)
    def _():
        grad_ref[...] = dot(x_turned[...], dboth_ref[...]).astype(BF16)

    @pl.when(step == both_steps)
    def _():
        hidden_turned[...] = hidden_ref[...].T

    blocks = down_blocks(units, width, count)
    if len(blocks) == 1:

        @pl.when(step >= both_steps)
        def _():
            grad_ref[...] = dot(hidden_turned[...], low_ref[...]).astype(BF16)

    else:
        @pl.when(step == both_steps)
        def _():
            rest[...] = dot(hidden_turned[...], low_ref[...]).astype(BF16)

        for place in range(width // tile - 1):

            @pl.when(step == both_steps + 1 + place)
            def _(place=place):
                total = dot(hidden_turned[...], low_ref[...]).astype(BF16)
                for (row, column), (from_row, from_column), (high, wide) in blocks:
                    if from_column == 0:
                        grad_ref[row : row + high, :] = total[from_row : from_row + high]
                    elif column == place * tile:
                        grad_ref[row : row + high, :] = rest[from_row : from_row + high, :]


def expert_weights(units, count, x, low, dboth, hidden):
    rows, width = x.shape
    tile = 256
    both_steps, down_steps = 2 * units // tile, width // tile
    uneven = units < width
    if uneven:
        assert width - width * units // width == tile
    columns = 2 * units + width - (tile if uneven else 0)
    whole = lambda i: (0, 0)

    def low_at(i):
        place = jnp.maximum(i - both_steps, 0)
        return (0, lax.rem(place + down_steps - 1, down_steps) if uneven else place)

    def grad_at(i):
        return (0, jnp.where(i < both_steps, i, jnp.maximum(i - 1, both_steps)) if uneven else i)

    return pl.pallas_call(
        functools.partial(expert_weights_kernel, units, count),
        grid=(both_steps + down_steps,),
        in_specs=[
            pl.BlockSpec((rows, width), whole),
            pl.BlockSpec((rows, tile), low_at),
            pl.BlockSpec((rows, tile), lambda i: (0, jnp.minimum(i, both_steps - 1))),
            pl.BlockSpec((rows, units), whole),
        ],
        out_specs=pl.BlockSpec((width, tile), grad_at),
        out_shape=jax.ShapeDtypeStruct((width, columns), BF16),
        scratch_shapes=[
            pltpu.VMEM((width, rows), BF16),
            pltpu.VMEM((units, rows), BF16),
            pltpu.VMEM((units, tile), BF16),
        ],
        compiler_params=params(),
        cost_estimate=brief(),
        name="expert_weights",
    )(x, low, dboth, hidden)


def ctx_moves(distance):
    devices = range(lax.axis_size("ctx"))
    return [(i - distance, i) for i in devices if i - distance in devices]


def after(value, *others):
    return lax.optimization_barrier((value,) + others)[0]


def gather_ctx(piece, marks=()):
    count, index, size = lax.axis_size("ctx"), lax.axis_index("ctx"), piece.shape[0]
    full = jnp.zeros((count * size,) + piece.shape[1:], piece.dtype)
    place = lambda buffer, part, at: lax.dynamic_update_slice_in_dim(buffer, part, at * size, 0)
    full = place(full, piece, index)
    up = down = piece
    for hop in range(1, count):
        up, down = shift_ctx(up, 1), shift_ctx(down, -1)
        if hop <= len(marks):
            up, down, _ = lax.optimization_barrier((up, down, marks[hop - 1]))
        for part, at, held in ((up, index - hop, index >= hop), (down, index + hop, index + hop < count)):
            at = jnp.clip(at, 0, count - 1)
            old = lax.dynamic_slice_in_dim(full, at * size, size, 0)
            full = place(full, jnp.where(held, part, old), at)
    return full


def swap_exp(block, bit):
    return lax.ppermute(block, "exp", [(i, i ^ bit) for i in range(lax.axis_size("exp"))])


def bit_set(bit):
    return (lax.axis_index("exp") // bit) % 2 == 1


def exp_bits():
    size, bits = lax.axis_size("exp"), []
    while 1 << len(bits) < size:
        bits.append(1 << len(bits))
    return bits


def gather_both(piece, marks):
    count = lax.axis_size("ctx")
    bits = exp_bits()
    start = column = gather_ctx(piece[None])
    if marks:
        column = after(column, marks[0])
    halves = []
    for half, order in ((column[: count // 2], bits[1:]), (column[count // 2 :], bits[:0:-1])):
        half = half[None]
        for bit in order:
            other = swap_exp(half, bit)
            half = jnp.where(bit_set(bit), jnp.concatenate([other, half]), jnp.concatenate([half, other]))
        halves.append((half, order))
    done = []
    for half, order in halves:
        half = after(half, marks[-1])
        other = swap_exp(half, 1)
        mine_first = bit_set(1)
        pair = jnp.stack([jnp.where(mine_first, other, half), jnp.where(mine_first, half, other)])
        shape = (2,) + (2,) * len(order) + half.shape[1:]
        pair = pair.reshape(shape)
        axes = [1 + order[::-1].index(bit) for bit in bits[:0:-1]] + [0]
        axes = [len(axes)] + axes + list(range(len(axes) + 1, pair.ndim))
        pair = pair.transpose(axes)
        done.append(pair.reshape((count // 2, 1 << len(bits)) + piece.shape))
    return done, start


def join_weights(done, first, rows):
    width = done[0].shape[-1]
    return jnp.concatenate([half[:, :, first : first + rows].reshape(-1, width) for half in done])


def scatter_ctx(parts, marks=(), seen=None):
    count, index = lax.axis_size("ctx"), lax.axis_index("ctx")

    def part(at):
        return lax.dynamic_index_in_dim(parts, jnp.clip(at, 0, count - 1), 0, keepdims=False).astype(F32)

    up = down = None
    for hop in range(1, count):
        distance = count - hop
        mine_up, mine_down = part(index + distance), part(index - distance)
        up = mine_up if up is None else mine_up + up.astype(F32)
        down = mine_down if down is None else mine_down + down.astype(F32)
        route = [(i, i + 1) for i in range(hop)]
        up = lax.ppermute(up.astype(BF16), "ctx", route)
        down = lax.ppermute(down.astype(BF16), "ctx", [(count - 1 - i, count - 1 - j) for i, j in route])
        if hop <= len(marks) and marks[hop - 1] is not None:
            up, down, _ = lax.optimization_barrier((up, down, marks[hop - 1]))
        if seen is not None:
            seen.append((up, down))
    if seen is not None:
        return part(index)
    return part(index) + up.astype(F32) + down.astype(F32)


def scatter_both(keep, send):
    count, bits = lax.axis_size("ctx"), exp_bits()
    whole = keep.astype(F32) + swap_exp(send, 1).astype(F32)
    chip = whole.reshape((count, -1) + whole.shape[1:])
    sums = []
    for half, order in ((chip[: count // 2], bits[1:]), (chip[count // 2 :], bits[:0:-1])):
        half = half.reshape((count // 2,) + (2,) * (len(bits) - 1) + half.shape[2:])
        left = bits[:0:-1]
        for bit in order:
            axis = 1 + left.index(bit)
            low = lax.index_in_dim(half, 0, axis, keepdims=False)
            high = lax.index_in_dim(half, 1, axis, keepdims=False)
            keep = jnp.where(bit_set(bit), high, low)
            send = jnp.where(bit_set(bit), low, high).astype(BF16)
            half = keep + swap_exp(send, bit).astype(F32)
            left = [b for b in left if b != bit]
        sums.append(half)
    return scatter_ctx(jnp.concatenate(sums)), whole


def slab_kernel(part, x_ref, q_ref, k_ref, v_ref, o_ref, g_ref, tail_ref, keep_ref, send_ref, x_turned, o_turned, total):
    core = lax.rem(lax.axis_index("exp"), 2)
    own = q_ref.shape[0]

    @pl.when(pl.program_id(0) == 0)
    def _():
        x_turned[...] = x_ref[...].T
        o_turned[...] = o_ref[...].T

    for place, (left, right) in enumerate(
        (
            (x_turned[:, x_turned.shape[1] - own :], q_ref[...]),
            (x_turned[...], k_ref[...]),
            (x_turned[...], v_ref[...]),
            (o_turned[...], g_ref[...]),
        )
    ):
        total[...] = dot(left, right)
        rows = slice(place * part, (place + 1) * part)
        for slab in range(keep_ref.shape[0]):
            first = 2 * slab * part
            keep_ref[slab, rows, :] = total[pl.ds(first + core * part, part), :].astype(BF16)
            send_ref[slab, rows, :] = total[pl.ds(first + (1 - core) * part, part), :].astype(BF16)
    for slab in range(keep_ref.shape[0]):
        keep_ref[slab, 4 * part :, :] = tail_ref[2 * slab + core]
        send_ref[slab, 4 * part :, :] = tail_ref[2 * slab + 1 - core]


def make_slabs(normed_all, query_grad, key_grad, value_grad, attended, branch_grad, tail):
    devices, extra, width = tail.shape
    all_rows, own = normed_all.shape[0], query_grad.shape[0]
    part, tile = width // devices, 256
    slab_rows = 4 * part + extra
    whole = lambda i: (0, 0)
    column = lambda i: (0, i)
    out = pl.BlockSpec((devices // 2, slab_rows, tile), lambda i: (0, 0, i))
    shape = jax.ShapeDtypeStruct((devices // 2, slab_rows, width), BF16)
    return pl.pallas_call(
        functools.partial(slab_kernel, part),
        grid=(width // tile,),
        in_specs=[
            pl.BlockSpec((all_rows, width), whole),
            pl.BlockSpec((own, tile), column),
            pl.BlockSpec((all_rows, tile), column),
            pl.BlockSpec((all_rows, tile), column),
            pl.BlockSpec((own, width), whole),
            pl.BlockSpec((own, tile), column),
            pl.BlockSpec((devices, extra, tile), lambda i: (0, 0, i)),
        ],
        out_specs=[out, out],
        out_shape=[shape, shape],
        scratch_shapes=[
            pltpu.VMEM((width, all_rows), BF16),
            pltpu.VMEM((width, own), BF16),
            pltpu.VMEM((width, tile), F32),
        ],
        compiler_params=params(),
        cost_estimate=brief(),
        name="slabs",
    )(normed_all, query_grad, key_grad, value_grad, attended, branch_grad, tail)


def exchange(blocks):
    return lax.all_to_all(blocks, "exp", split_axis=0, concat_axis=0, tiled=True)


def body(
    tokens,
    w_query,
    w_key,
    w_value,
    w_out,
    w_router,
    gain_attn,
    gain_mlp,
    pos_bias,
    exp_gate,
    exp_up,
    exp_down,
    doc_lengths,
    bucket_of,
    expert_ids,
    cotangent,
):
    both = ("ctx", "exp")
    own_tokens = tokens[0]
    rows, width = own_tokens.shape
    experts = w_router.shape[1]
    capacity = (5 * TOP * rows + 4 * experts - 1) // (4 * experts)
    reach = (WINDOW + rows - 2) // rows
    scale = HEAD_DIM ** (-0.5)
    ctx_index, ctx_count = lax.axis_index("ctx"), lax.axis_size("ctx")
    exp_index = lax.axis_index("exp")
    part = w_query.shape[0]
    bias_part = pos_bias.shape[0]
    devices = width // part

    small = jnp.concatenate([w_router.reshape(-1), gain_attn, gain_mlp, pos_bias])
    small = jnp.pad(small, (0, width - small.shape[0]))[None]
    small = jnp.pad(small, ((0, 15), (0, 0)))
    halo = [own_tokens]
    for _ in range(reach):
        halo.insert(0, shift_ctx(halo[0], 1))
    dense, column = gather_both(
        jnp.concatenate([w_query, w_key, w_value, w_out, small], axis=0), halo[-2::-1]
    )
    full_query, full_key, full_value, full_out = (join_weights(dense, i * part, part) for i in range(4))
    small = join_weights(dense, 4 * part, 1)
    at = part * experts
    full_router = small[:, :at].reshape(width, experts)
    full_gain_attn = small[:, at : at + part].reshape(width).astype(F32)
    full_gain_mlp = small[:, at + part : at + 2 * part].reshape(width).astype(F32)
    table = small[:, at + 2 * part : at + 2 * part + bias_part].reshape(HEADS, BUCKETS)

    inputs_all = jnp.concatenate(halo, axis=0).astype(F32)
    inputs = own_tokens.astype(F32)

    held, share = exp_gate.shape[1], exp_down.shape[1]
    chunks, first = [], 0
    while first < share:
        size = min(held, share - first)
        units = size * ctx_count
        columns = [slice(z * share + first, z * share + first + size) for z in range(ctx_count)]
        parts = [weight[0][:, at] for weight in (exp_gate, exp_up) for at in columns]
        down = exp_down[0][first : first + size]
        if size < held:
            wide, spare = width * size // held, held - size
            below = [down[m * spare : (m + 1) * spare, wide:] for m in range(size // spare)]
            down = jnp.concatenate([down[:, :wide], jnp.concatenate(below, axis=1)], axis=0)
        packed = after(jnp.concatenate(parts + [down], axis=1), column, halo[0])
        chunks.append((units, size, lax.all_gather(packed, "ctx", axis=0, tiled=True)))
        first += size

    expert_range = jnp.arange(experts, dtype=jnp.int32)
    named = jnp.any(expert_ids[0][:, :, None] == expert_range, axis=1)
    named_low = named.astype(BF16)
    step = jnp.arange(rows, dtype=jnp.int32)
    earlier = (step[:, None] > step[None, :]).astype(BF16)
    slots = dot(earlier, named_low).astype(jnp.int32)
    slots = jnp.where(named, slots, -1).T
    routes = (slots[:, None, :] == jnp.arange(capacity, dtype=jnp.int32)[None, :, None]).astype(BF16)
    routes = routes.reshape(experts * capacity, rows)

    names = jnp.pad(named_low, ((0, 0), (0, LANES - experts)))
    early = dot(routes, jnp.concatenate([cotangent[0], names], axis=1)).astype(BF16)
    early = after(early, full_router)
    early = exchange(early.reshape(experts, capacity, width + LANES)).reshape(-1, width + LANES)
    cot_in, names_in = early[:, :width], early[:, width:]

    onehot_bucket = (bucket_of[None, :] == jnp.arange(BUCKETS, dtype=jnp.int32)[:, None]).astype(BF16)
    band = make_band(dot(table, onehot_bucket))
    ends = jnp.cumsum(doc_lengths[0])

    def documents(positions):
        return jnp.sum((positions[:, None] >= ends[None, :]).astype(jnp.int32), axis=1)[:, None]

    feature = (jnp.arange(2 * HEAD_DIM, dtype=jnp.int32) % HEAD_DIM)[None, :]
    docs = doc_lengths.shape[1] + 1
    query_pos = ctx_index * rows + step
    key_pos = (ctx_index - reach) * rows + jnp.arange((reach + 1) * rows, dtype=jnp.int32)
    query_doc = (feature == documents(query_pos)).astype(BF16)
    same = (feature == documents(key_pos)) & (key_pos[:, None] >= 0)
    key_doc = jnp.where(same | (feature >= docs), 0.0, NEGATIVE).astype(BF16)

    normed_all = norm_rows(inputs_all, full_gain_attn).astype(BF16)
    normed = normed_all[reach * rows :]
    queries = (dot(normed, full_query).astype(BF16)) * jnp.asarray(scale, BF16)
    keys = dot(normed_all, full_key).astype(BF16)
    values = dot(normed_all, full_value).astype(BF16)
    attended, lse = attend(queries, keys, values, query_doc, key_doc, band)
    middle = inputs + dot(attended, full_out)
    normed_mlp = norm_rows(middle, full_gain_mlp).astype(BF16)

    sent = dot(routes, normed_mlp).astype(BF16)
    arrived = exchange(sent.reshape(experts, capacity, width)).reshape(-1, width)
    router_turned = jnp.pad(full_router.T, ((0, LANES - experts), (0, 0)))
    extras = (cot_in, names_in, router_turned)
    carried, grads, rows_in, seen = None, [], arrived, []
    first_sum = None
    for place, (units, _, chunk) in enumerate(chunks):
        last = place == len(chunks) - 1
        hidden, dboth, carried, router_grad = run_expert(
            place == 0, last, units, ctx_count, rows_in, chunk, extras, carried
        )
        grads.append(expert_weights(units, ctx_count, arrived, carried[0], dboth, hidden))
        if place == 0:
            first_sum = scatter_ctx(grads[0].reshape(ctx_count, held, -1), (), seen)
        rows_in = after(arrived, grads[-1], *seen[min(place, len(seen) - 1)])
    _, made, back, _ = carried
    back = exchange(back.reshape(experts, capacity, width)).reshape(-1, width)
    made = exchange(made.reshape(experts, capacity, width)).reshape(-1, width)
    back = after(back, grads[-1])
    output = (middle + dot_rows(routes, made)).astype(BF16)

    upstream = cotangent[0].astype(F32)
    normed_mlp_grad = dot_rows(routes, back)
    _, second_pull = jax.vjp(norm_rows, middle, full_gain_mlp)
    middle_norm_grad, gain_mlp_grad = second_pull(normed_mlp_grad)
    middle_grad = upstream + middle_norm_grad
    branch_grad = middle_grad.astype(BF16)
    attended_grad = dot_last(branch_grad, full_out).astype(BF16)
    query_grad, key_grad, value_grad, band_grad = attend_back(
        queries, keys, values, attended_grad, attended, lse, query_doc, key_doc, band
    )
    bias_grad = jnp.dot(
        sum_band(band_grad), onehot_bucket.T.astype(F32), precision=lax.Precision.HIGHEST
    )

    normed_grad_all = dot_last(key_grad, full_key) + dot_last(value_grad, full_value)
    own_grad = normed_grad_all[reach * rows :] + dot_last(query_grad, full_query)
    halo_grad = normed_grad_all[: reach * rows]
    _, first_pull = jax.vjp(norm_rows, inputs_all, full_gain_attn)
    gain_attn_grad = first_pull(jnp.concatenate([halo_grad, own_grad], axis=0))[1]
    tail = jnp.concatenate(
        [
            router_grad[:, :experts].reshape(devices, -1),
            gain_attn_grad.reshape(devices, part),
            gain_mlp_grad.reshape(devices, part),
            bias_grad.reshape(devices, bias_part),
        ],
        axis=1,
    ).astype(BF16)
    tail = jnp.pad(tail[:, None, :], ((0, 0), (0, 15), (0, width - tail.shape[1])))
    keep, send = make_slabs(normed_all, query_grad, key_grad, value_grad, attended, branch_grad, tail)
    sums, chip = scatter_both(keep, send)

    first_up, first_down = seen[-1]
    first_sum = first_sum + after(first_up, sums).astype(F32) + after(first_down, sums).astype(F32)
    expert_sums = [first_sum] + [lax.psum_scatter(grad, "ctx", scatter_dimension=0, tiled=True).astype(F32) for grad in grads[1:]]
    gate_parts, up_parts, down_parts = [], [], []
    for (units, size, _), total in zip(chunks, expert_sums):
        gate_parts.append(total[:, :units])
        up_parts.append(total[:, units : 2 * units])
        down = total[:, 2 * units :]
        if size < held:
            wide, spare = width * size // held, held - size
            thin = width - wide
            below = [down[size:, m * thin : (m + 1) * thin] for m in range(size // spare)]
            down = jnp.concatenate([down[:size], jnp.concatenate(below, axis=0)], axis=1)
        down_parts.append(down)
    def in_order(parts):
        shares = [part[:, z * (part.shape[1] // ctx_count) : (z + 1) * (part.shape[1] // ctx_count)]
                  for z in range(ctx_count) for part in parts]
        return jnp.concatenate(shares, axis=1)[None]

    expert_grads = (
        in_order(gate_parts),
        in_order(up_parts),
        jnp.concatenate(down_parts, axis=0)[None],
    )
    returning = None
    for stride, mark in zip(range(reach, 0, -1), [keep] * (reach - 1) + [chip]):
        piece = halo_grad[(reach - stride) * rows : (reach - stride + 1) * rows]
        piece = piece if returning is None else piece + returning.astype(F32)
        returning = after(shift_ctx(piece.astype(BF16), -1), mark)
    _, own_pull = jax.vjp(norm_rows, inputs, full_gain_attn)
    input_grad = middle_grad + own_pull(own_grad + returning.astype(F32))[0]
    tail = sums[4 * part]
    at = part * experts
    return (
        output[None],
        input_grad[None],
        sums[:part],
        sums[part : 2 * part],
        sums[2 * part : 3 * part],
        sums[3 * part : 4 * part],
        tail[:at].reshape(part, experts),
        tail[at : at + part],
        tail[at + part : at + 2 * part],
        tail[at + 2 * part : at + 2 * part + bias_part],
        expert_grads[0],
        expert_grads[1],
        expert_grads[2],
    )


def solution(mesh):
    rows3 = P("exp", "ctx", None)
    dense2 = P(("ctx", "exp"), None)
    dense1 = P(("ctx", "exp"))
    return jax.shard_map(
        body,
        mesh=mesh,
        in_specs=(
            rows3,
            dense2,
            dense2,
            dense2,
            dense2,
            dense2,
            dense1,
            dense1,
            dense1,
            rows3,
            rows3,
            rows3,
            P("exp", None),
            P(),
            rows3,
            rows3,
        ),
        out_specs=(
            rows3,
            rows3,
            dense2,
            dense2,
            dense2,
            dense2,
            dense2,
            dense1,
            dense1,
            dense1,
            rows3,
            rows3,
            rows3,
        ),
        check_vma=False,
    )
```

```python
import functools

import jax
import jax.numpy as jnp
from jax import lax
from jax.experimental import pallas as pl
from jax.experimental.pallas import tpu as pltpu
from jax.sharding import PartitionSpec as P

HEADS = 16
HEAD_DIM = 64
BUCKETS = 32
TOP = 2
WINDOW = 1024

EPSILON = 1e-06
NEGATIVE = -1e30
LANES = 128
CHUNK = 256
FF_TILE = 256
ROW_TILE = 256
VMEM_LIMIT = 58 * 2**20
BF16 = jnp.bfloat16
F32 = jnp.float32


def shift_ctx(block, distance):
    devices = range(lax.axis_size("ctx"))
    route = [(i - distance, i) for i in devices if i - distance in devices]
    return lax.ppermute(block, "ctx", route)


def norm_rows(values, gain):
    return values * lax.rsqrt(jnp.mean(values * values, axis=-1, keepdims=True) + EPSILON) * gain


def dot(left, right):
    return jnp.dot(left, right, preferred_element_type=F32)


def dot_rows(left, right):
    return lax.dot_general(left, right, (((0,), (0,)), ((), ())), preferred_element_type=F32)


def dot_last(left, right):
    return lax.dot_general(left, right, (((1,), (1,)), ((), ())), preferred_element_type=F32)


def params(**more):
    return pltpu.CompilerParams(vmem_limit_bytes=VMEM_LIMIT, **more)


def brief():
    return pl.CostEstimate(flops=2**20, bytes_accessed=2**20, transcendentals=0)


def band_kernel(bias_ref, band_ref):
    blocks = WINDOW // LANES
    size = (blocks + 2) * LANES
    for head in range(bias_ref.shape[0]):
        row = jnp.broadcast_to(bias_ref[head : head + 1, :], (8, size))
        eight = pltpu.roll(row, 0, 1, stride=1, stride_axis=0)
        for group in range(LANES // 8):
            wide = pltpu.roll(eight, 8 * group, 1) if group else eight
            for a in range(blocks + 1):
                first = a * LANES + group * 8
                at = (blocks + 1 - a) * LANES
                band_ref[head, first : first + 8, :] = wide[:, at : at + LANES]


def make_band(bias_dist):
    group = 8
    edge = jnp.full((HEADS, LANES), NEGATIVE, F32)
    padded = jnp.concatenate([edge, bias_dist, edge], axis=1)
    return pl.pallas_call(
        band_kernel,
        grid=(HEADS // group,),
        in_specs=[pl.BlockSpec((group, WINDOW + 2 * LANES), lambda h: (h, 0))],
        out_specs=pl.BlockSpec((group, WINDOW + LANES, LANES), lambda h: (h, 0, 0)),
        out_shape=jax.ShapeDtypeStruct((HEADS, WINDOW + LANES, LANES), F32),
        compiler_params=params(),
        cost_estimate=brief(),
        name="bias_band",
    )(padded)


def unband_kernel(band_ref, dist_ref):
    blocks = WINDOW // LANES
    size = (blocks + 2) * LANES
    row = lax.broadcasted_iota(jnp.int32, (8, 1), 0)
    edge = jnp.zeros((8, LANES), F32)
    for head in range(band_ref.shape[0]):
        total = None
        for group in range(LANES // 8):
            pieces = [edge]
            for a in range(blocks, -1, -1):
                first = a * LANES + group * 8
                pieces.append(band_ref[head, first : first + 8, :])
            wide = jnp.concatenate(pieces, axis=1)
            if group:
                wide = pltpu.roll(wide, size - 8 * group, 1)
            total = wide if total is None else total + wide
        dist = jnp.zeros_like(total)
        for r in range(8):
            turned = pltpu.roll(total, size - r, 1) if r else total
            dist = dist + jnp.where(row == r, turned, 0.0)
        dist_ref[head : head + 1, :] = jnp.sum(dist, axis=0, keepdims=True)[:, LANES : LANES + WINDOW]


def sum_band(band_grad):
    group = 8
    return pl.pallas_call(
        unband_kernel,
        grid=(HEADS // group,),
        in_specs=[pl.BlockSpec((group, WINDOW + LANES, LANES), lambda h: (h, 0, 0))],
        out_specs=pl.BlockSpec((group, WINDOW), lambda h: (h, 0)),
        out_shape=jax.ShapeDtypeStruct((HEADS, WINDOW), F32),
        compiler_params=params(),
        cost_estimate=brief(),
        name="bias_band_sums",
    )(band_grad)


def head_lanes(head):
    lane = lax.broadcasted_iota(jnp.int32, (1, 2 * HEAD_DIM), 1)
    return (lane >= head * HEAD_DIM) & (lane < (head + 1) * HEAD_DIM)


def masked_scores(head, start, q_ref, k_ref, qdoc_ref, kdoc_ref):
    span = WINDOW + CHUNK
    mine = head_lanes(head)
    q_rows, k_rows = pl.ds(start, CHUNK), pl.ds(start, span)
    q_part = jnp.where(mine, q_ref[q_rows, :], qdoc_ref[q_rows, :])
    k_part = jnp.where(mine, k_ref[k_rows, :], kdoc_ref[k_rows, :])
    return dot_last(k_part, q_part)


def sub_blocks():
    return [(s * LANES, WINDOW + LANES) for s in range(CHUNK // LANES)]


def spread(parts):
    span = WINDOW + CHUNK
    columns = []
    for (first, rows), part in zip(sub_blocks(), parts):
        pieces = []
        if first:
            pieces.append(jnp.zeros((first, LANES), part.dtype))
        pieces.append(part)
        if span - first - rows:
            pieces.append(jnp.zeros((span - first - rows, LANES), part.dtype))
        columns.append(jnp.concatenate(pieces, axis=0) if len(pieces) > 1 else part)
    return jnp.concatenate(columns, axis=1)


def attend_kernel(q_ref, k_ref, v_ref, qdoc_ref, kdoc_ref, band_ref, o_ref, lse_ref):
    span = WINDOW + CHUNK
    for start in range(0, q_ref.shape[0], CHUNK):
        v_turned = v_ref[pl.ds(start, span), :].T
        outs = []
        for head in range(2):
            scores = masked_scores(head, start, q_ref, k_ref, qdoc_ref, kdoc_ref)
            band = band_ref[head]
            low, scale, logs = [], [], []
            for s, (first, rows) in enumerate(sub_blocks()):
                part = scores[first : first + rows, s * LANES : (s + 1) * LANES] + band
                top = jnp.max(part, axis=0, keepdims=True)
                expo = jnp.exp(part - top)
                total = jnp.sum(expo, axis=0, keepdims=True)
                low.append(expo.astype(BF16))
                scale.append(1.0 / total)
                logs.append(top + jnp.log(total))
            out = dot(v_turned[head * HEAD_DIM : (head + 1) * HEAD_DIM], spread(low))
            outs.append(out * jnp.concatenate(scale, axis=1))
            lse_ref[0, head : head + 1, pl.ds(start, CHUNK)] = jnp.concatenate(logs, axis=1)
        o_ref[pl.ds(start, CHUNK), :] = jnp.concatenate(outs, axis=0).T.astype(BF16)


def attend(queries, keys, values, query_doc, key_doc, band):
    rows, width = queries.shape
    keys_rows = keys.shape[0]
    pairs = HEADS // 2
    wide = 2 * HEAD_DIM
    return pl.pallas_call(
        attend_kernel,
        grid=(pairs,),
        in_specs=[
            pl.BlockSpec((rows, wide), lambda p: (0, p)),
            pl.BlockSpec((keys_rows, wide), lambda p: (0, p)),
            pl.BlockSpec((keys_rows, wide), lambda p: (0, p)),
            pl.BlockSpec((rows, wide), lambda p: (0, 0)),
            pl.BlockSpec((keys_rows, wide), lambda p: (0, 0)),
            pl.BlockSpec((2, WINDOW + LANES, LANES), lambda p: (p, 0, 0)),
        ],
        out_specs=[
            pl.BlockSpec((rows, wide), lambda p: (0, p)),
            pl.BlockSpec((1, 2, rows), lambda p: (p, 0, 0)),
        ],
        out_shape=[
            jax.ShapeDtypeStruct((rows, width), BF16),
            jax.ShapeDtypeStruct((pairs, 2, rows), F32),
        ],
        compiler_params=params(),
        cost_estimate=brief(),
        name="attend",
    )(queries, keys, values, query_doc, key_doc, band)


def attend_back_kernel(
    q_ref, k_ref, v_ref, g_ref, o_ref, lse_ref, qdoc_ref, kdoc_ref, band_ref,
    dq_ref, dk_ref, dv_ref, dband_ref, dk_sum, dv_sum,
):
    span = WINDOW + CHUNK
    dk_sum[...] = jnp.zeros_like(dk_sum)
    dv_sum[...] = jnp.zeros_like(dv_sum)
    for start in range(0, q_ref.shape[0], CHUNK):
        q_rows, k_rows = pl.ds(start, CHUNK), pl.ds(start, span)
        k_turned = k_ref[k_rows, :].T
        product = (g_ref[q_rows, :].astype(F32) * o_ref[q_rows, :].astype(F32)).T
        dq_parts = []
        for head in range(2):
            mine = head_lanes(head)
            zero = jnp.zeros((), BF16)
            scores = masked_scores(head, start, q_ref, k_ref, qdoc_ref, kdoc_ref)
            g_part = jnp.where(mine, g_ref[q_rows, :], zero)
            q_part = jnp.where(mine, q_ref[q_rows, :], zero)
            prob_grad = dot_last(v_ref[k_rows, :], g_part)
            delta = jnp.sum(product[head * HEAD_DIM : (head + 1) * HEAD_DIM], axis=0, keepdims=True)
            lse = lse_ref[0, head : head + 1, q_rows]
            band = band_ref[head]
            prob_low, grad_low, grad_sum = [], [], None
            for s, (first, rows) in enumerate(sub_blocks()):
                lanes = slice(s * LANES, (s + 1) * LANES)
                probs = jnp.exp(scores[first : first + rows, lanes] + band - lse[:, lanes])
                grad = probs * (prob_grad[first : first + rows, lanes] - delta[:, lanes])
                prob_low.append(probs.astype(BF16))
                grad_low.append(grad.astype(BF16))
                grad_sum = grad if grad_sum is None else grad_sum + grad
            if start == 0:
                dband_ref[head] = grad_sum
            else:
                dband_ref[head] = dband_ref[head] + grad_sum
            grads = spread(grad_low)
            dk_sum[k_rows, :] += dot(grads, q_part)
            dv_sum[k_rows, :] += dot(spread(prob_low), g_part)
            dq_parts.append(dot(k_turned[head * HEAD_DIM : (head + 1) * HEAD_DIM], grads))
        turned = jnp.concatenate(dq_parts, axis=0).T
        dq_ref[q_rows, :] = (turned * HEAD_DIM ** (-0.5)).astype(BF16)
    dk_ref[...] = dk_sum[...].astype(BF16)
    dv_ref[...] = dv_sum[...].astype(BF16)


def attend_back(queries, keys, values, grad, out, lse, query_doc, key_doc, band):
    rows, width = queries.shape
    keys_rows = keys.shape[0]
    pairs = HEADS // 2
    wide = 2 * HEAD_DIM
    q_spec = pl.BlockSpec((rows, wide), lambda p: (0, p))
    k_spec = pl.BlockSpec((keys_rows, wide), lambda p: (0, p))
    band_spec = pl.BlockSpec((2, WINDOW + LANES, LANES), lambda p: (p, 0, 0))
    return pl.pallas_call(
        attend_back_kernel,
        grid=(pairs,),
        in_specs=[
            q_spec,
            k_spec,
            k_spec,
            q_spec,
            q_spec,
            pl.BlockSpec((1, 2, rows), lambda p: (p, 0, 0)),
            pl.BlockSpec((rows, wide), lambda p: (0, 0)),
            pl.BlockSpec((keys_rows, wide), lambda p: (0, 0)),
            band_spec,
        ],
        out_specs=[q_spec, k_spec, k_spec, band_spec],
        out_shape=[
            jax.ShapeDtypeStruct((rows, width), BF16),
            jax.ShapeDtypeStruct((keys_rows, width), BF16),
            jax.ShapeDtypeStruct((keys_rows, width), BF16),
            jax.ShapeDtypeStruct((HEADS, WINDOW + LANES, LANES), F32),
        ],
        scratch_shapes=[pltpu.VMEM((keys_rows, wide), F32), pltpu.VMEM((keys_rows, wide), F32)],
        compiler_params=params(),
        cost_estimate=pl.CostEstimate(flops=20 * rows * WINDOW * width * 2, bytes_accessed=2**20, transcendentals=0),
        name="attend_back",
    )(queries, keys, values, grad, out, lse, query_doc, key_doc, band)


def down_blocks(units, width, count):
    held, share = width // count, units // count
    extra = share - held
    wide = width * extra // held
    blocks = []
    for z in range(count):
        blocks.append(((z * held, 0), (z * share, 0), (held, width)))
        for m in range(held // extra):
            blocks.append(((z * held + m * extra, width), (z * share + held, m * wide), (extra, wide)))
    return blocks


def pack_down(down, held):
    extra, width = down.shape[0] - held, down.shape[1]
    wide = width * extra // held
    rest = [down[held:, m * wide : (m + 1) * wide] for m in range(held // extra)]
    return jnp.concatenate([down[:held], jnp.concatenate(rest, axis=0)], axis=1)


def unpack_down(packed, size, width):
    held = packed.shape[0]
    extra = size - held
    rest = [packed[m * extra : (m + 1) * extra, width:] for m in range(held // extra)]
    return jnp.concatenate([packed[:, :width], jnp.concatenate(rest, axis=1)], axis=0)


def expert_kernel(first, last, units, count, parts, *refs):
    refs = list(refs)
    take = lambda: refs.pop(0)
    x_ref = take()
    pieces = [take() for _ in range(parts)]
    if first or last:
        c_ref, names_ref, router_ref = take(), take(), take()
    if not first:
        low_ref, made_in, back_in = take(), take(), take()
    if last and not first:
        gate_in = take()
    hidden_ref, dboth_ref = take(), take()
    if first:
        low_out = take()
    if first and not last:
        gate_out = take()
    made_ref, back_ref = take(), take()
    if last:
        drouter_ref = take()
    chunk_ref, down_s, sems = take(), take(), take()
    rows, width = x_ref.shape
    held = width // count
    index = lax.axis_index("ctx")

    def slot(z):
        return chunk_ref.at[z * held : (z + 1) * held]

    @pl.when(pl.program_id(0) == 0)
    def _():
        if parts == 1:
            for z in range(count):
                pltpu.make_async_copy(pieces[0].at[z * held : (z + 1) * held], slot(z), sems.at[z]).start()
        for z in range(count if parts > 1 else 0):
            for here in range(count):
                hop = abs(here - z)
                source = pieces[0 if hop == 0 else 2 * hop - 1 if z < here else 2 * hop]

                @pl.when(index == here)
                def _(source=source, z=z):
                    pltpu.make_async_copy(source, slot(z), sems.at[z]).start()

        for z in range(count):
            pltpu.make_async_copy(pieces[0].at[:held], slot(z), sems.at[z]).wait()

    x = x_ref[...]
    own = lax.broadcasted_iota(jnp.int32, (1, LANES), 1) == lax.axis_index("exp")
    if first:
        names = names_ref[...].astype(F32)
        logits = dot_last(x, router_ref[...]) * names
        mine = jnp.sum(jnp.where(own, logits, 0.0), axis=1, keepdims=True)
        theirs = jnp.sum(jnp.where(own, 0.0, logits), axis=1, keepdims=True)
        gate = jax.nn.sigmoid(mine - theirs)
        low_out[...] = (gate * c_ref[...].astype(F32)).astype(BF16)
        if not last:
            gate_out[...] = jnp.broadcast_to(gate, (rows, LANES))
        low_ref = low_out
    elif last:
        gate = gate_in[...][:, :1]
    @pl.when(pl.program_id(0) == 0)
    def _():
        for (row, column), (to_row, to_column), (high, wide) in down_blocks(units, width, count):
            from_columns = slice(2 * units + column, 2 * units + column + wide)
            down_s[to_row : to_row + high, to_column : to_column + wide] = chunk_ref[row : row + high, from_columns]

    for t in range(units // FF_TILE):
        at = slice(t * FF_TILE, (t + 1) * FF_TILE)
        up_at = slice(units + t * FF_TILE, units + (t + 1) * FF_TILE)
        gate_pre = dot(x, chunk_ref[:, at])
        up_pre = dot(x, chunk_ref[:, up_at])
        hidden_grad = dot_last(low_ref[...], down_s[at, :])
        root = 0.7978845608028654
        square = gate_pre * gate_pre
        bent = jnp.tanh(gate_pre * (root + root * 0.044715 * square))
        half = 0.5 * (1.0 + bent)
        act = gate_pre * half
        slope = half + 0.5 * gate_pre * (1.0 - bent * bent) * (root + 3.0 * root * 0.044715 * square)
        hidden_ref[:, at] = (act * up_pre).astype(BF16)
        dboth_ref[:, at] = (hidden_grad * up_pre * slope).astype(BF16)
        dboth_ref[:, up_at] = (hidden_grad * act).astype(BF16)
    made = dot(hidden_ref[...], down_s[...])
    back = dot_last(dboth_ref[...], chunk_ref[:, : 2 * units])
    if not first:
        made = made + made_in[...]
        back = back + back_in[...]
    if last:
        made = made.astype(BF16).astype(F32)
        names = names_ref[...].astype(F32)
        push = jnp.sum(c_ref[...].astype(F32) * made, axis=1, keepdims=True)
        push = push * gate * (1.0 - gate)
        logits_grad = push * jnp.where(own, names, -names)
        high = logits_grad.astype(BF16)
        low = (logits_grad - high.astype(F32)).astype(BF16)
        made = gate * made
        back = back + dot(high, router_ref[...]) + dot(low, router_ref[...])
        turned = x.T
        update = dot(turned, high) + dot(turned, low)

        @pl.when(pl.program_id(0) == 0)
        def _():
            drouter_ref[...] = update

        @pl.when(pl.program_id(0) > 0)
        def _():
            drouter_ref[...] += update

    made_ref[...] = made.astype(made_ref.dtype)
    back_ref[...] = back.astype(back_ref.dtype)


def run_expert(first, last, units, count, x, pieces, extras, carried):
    rows, width = x.shape
    whole = lambda i: (0, 0)
    step = lambda i: (i, 0)
    wide = pl.BlockSpec((ROW_TILE, width), step)
    thin = pl.BlockSpec((ROW_TILE, LANES), step)
    struct = jax.ShapeDtypeStruct
    early, router = extras
    operands = [x] + pieces
    in_specs = [wide] + [pl.BlockSpec(memory_space=pl.ANY)] * len(pieces)
    if first or last:
        operands += [early, early, router]
        names = pl.BlockSpec((ROW_TILE, LANES), lambda i: (i, width // LANES))
        in_specs += [wide, names, pl.BlockSpec((LANES, width), whole)]
    if not first:
        low, made, back, gate = carried
        operands += [low, made, back]
        in_specs += [wide, wide, wide]
        if last:
            operands.append(gate)
            in_specs.append(thin)
    out_shape = [struct((rows, units), BF16), struct((rows, 2 * units), BF16)]
    out_specs = [pl.BlockSpec((ROW_TILE, units), step), pl.BlockSpec((ROW_TILE, 2 * units), step)]
    if first:
        out_shape.append(struct((rows, width), BF16))
        out_specs.append(wide)
        if not last:
            out_shape.append(struct((rows, LANES), F32))
            out_specs.append(thin)
    kept = BF16 if last else F32
    out_shape += [struct((rows, width), kept), struct((rows, width), kept)]
    out_specs += [wide, wide]
    if last:
        out_shape.append(struct((width, LANES), F32))
        out_specs.append(pl.BlockSpec((width, LANES), whole))
    outs = list(
        pl.pallas_call(
            functools.partial(expert_kernel, first, last, units, count, len(pieces)),
            grid=(rows // ROW_TILE,),
            in_specs=in_specs,
            out_specs=out_specs,
            out_shape=out_shape,
            scratch_shapes=[
                pltpu.VMEM((width, pieces[0].shape[1]), BF16),
                pltpu.VMEM((units, width), BF16),
                pltpu.SemaphoreType.DMA((count,)),
            ],
            compiler_params=params(),
            cost_estimate=brief(),
            name="expert",
        )(*operands)
    )
    hidden, dboth = outs[:2]
    if first:
        low = outs[2]
        gate = None if last else outs[3]
    if last:
        made, back, drouter = outs[-3:]
        return hidden, dboth, (low, made, back, gate), drouter
    made, back = outs[-2:]
    return hidden, dboth, (low, made, back, gate), None


def expert_weights_kernel(
    units, count, x_ref, low_ref, dboth_ref, hidden_ref, grad_ref, x_turned, hidden_turned, rest
):
    step = pl.program_id(0)
    tile = low_ref.shape[1]
    width = x_ref.shape[1]
    both_steps, down_steps = 2 * units // tile, width // tile

    @pl.when(step == 0)
    def _():
        x_turned[...] = x_ref[...].T

    @pl.when(step < both_steps)
    def _():
        grad_ref[...] = dot(x_turned[...], dboth_ref[...]).astype(BF16)

    @pl.when(step == both_steps)
    def _():
        hidden_turned[...] = hidden_ref[...].T

    for place in range(down_steps):

        @pl.when(step == both_steps + place)
        def _(place=place):
            total = dot(hidden_turned[...], low_ref[...]).astype(BF16)
            first = place * tile
            for (row, column), (from_row, from_column), (high, wide) in down_blocks(units, width, count):
                part = total[from_row : from_row + high]
                if column == 0:
                    grad_ref[row : row + high, :] = part
                elif from_column <= first < from_column + wide:
                    rest[row : row + high, first - from_column : first - from_column + tile] = part

    for place in range(rest.shape[1] // tile):

        @pl.when(step == both_steps + down_steps + place)
        def _(place=place):
            grad_ref[...] = rest[:, place * tile : (place + 1) * tile]


def expert_weights(units, count, x, low, dboth, hidden, long=False):
    rows, width = x.shape
    tile = 256
    extra = units - width
    both_steps, down_steps = 2 * units // tile, width // tile
    whole = lambda i: (0, 0)
    return pl.pallas_call(
        functools.partial(expert_weights_kernel, units, count),
        grid=(both_steps + down_steps + extra // tile,),
        in_specs=[
            pl.BlockSpec((rows, width), whole),
            pl.BlockSpec((rows, tile), lambda i: (0, jnp.clip(i - both_steps, 0, down_steps - 1))),
            pl.BlockSpec((rows, tile), lambda i: (0, jnp.minimum(i, both_steps - 1))),
            pl.BlockSpec((rows, units), whole),
        ],
        out_specs=pl.BlockSpec((width, tile), lambda i: (0, i)),
        out_shape=jax.ShapeDtypeStruct((width, 3 * units), BF16),
        scratch_shapes=[
            pltpu.VMEM((width, rows), BF16),
            pltpu.VMEM((units, rows), BF16),
            pltpu.VMEM((width, extra), BF16),
        ],
        compiler_params=params(),
        cost_estimate=pl.CostEstimate(flops=(6 * rows * width * units) if long else 2**20, bytes_accessed=2**20, transcendentals=0),
        name="expert_weights",
    )(x, low, dboth, hidden)


def ctx_moves(distance):
    devices = range(lax.axis_size("ctx"))
    return [(i - distance, i) for i in devices if i - distance in devices]


def together(*values):
    return lax.optimization_barrier(values)


def gather_ctx(piece):
    count, index, size = lax.axis_size("ctx"), lax.axis_index("ctx"), piece.shape[0]
    full = jnp.zeros((count * size,) + piece.shape[1:], piece.dtype)
    place = lambda buffer, part, at: lax.dynamic_update_slice_in_dim(buffer, part, at * size, 0)
    full = place(full, piece, index)
    up = down = piece
    for hop in range(1, count):
        up, down = shift_ctx(up, 1), shift_ctx(down, -1)
        for part, at, held in ((up, index - hop, index >= hop), (down, index + hop, index + hop < count)):
            at = jnp.clip(at, 0, count - 1)
            old = lax.dynamic_slice_in_dim(full, at * size, size, 0)
            full = place(full, jnp.where(held, part, old), at)
    return full


def gather_hop(up, down, hop):
    count = lax.axis_size("ctx")
    route = [(i, i + 1) for i in range(hop - 1, count - 1)]
    back = [(count - 1 - i, count - 1 - j) for i, j in route]
    return lax.ppermute(up, "ctx", route), lax.ppermute(down, "ctx", back)


def scatter_add(parts, hop, up=None, down=None):
    count, index = lax.axis_size("ctx"), lax.axis_index("ctx")

    def part(at):
        return lax.dynamic_index_in_dim(parts, jnp.clip(at, 0, count - 1), 0, keepdims=False).astype(F32)

    distance = count - hop
    mine_up, mine_down = part(index + distance), part(index - distance)
    if up is not None:
        mine_up, mine_down = mine_up + up.astype(F32), mine_down + down.astype(F32)
    return mine_up.astype(BF16), mine_down.astype(BF16)


def scatter_hop(up, down, hop):
    count = lax.axis_size("ctx")
    route = [(i, i + 1) for i in range(hop)]
    back = [(count - 1 - i, count - 1 - j) for i, j in route]
    return lax.ppermute(up, "ctx", route), lax.ppermute(down, "ctx", back)


def scatter_end(parts, up, down):
    own = lax.dynamic_index_in_dim(parts, lax.axis_index("ctx"), 0, keepdims=False).astype(F32)
    return own + up.astype(F32) + down.astype(F32)


def swap_exp(block, bit):
    return lax.ppermute(block, "exp", [(i, i ^ bit) for i in range(lax.axis_size("exp"))])


def bit_set(bit):
    return (lax.axis_index("exp") // bit) % 2 == 1


def exp_bits():
    size, bits = lax.axis_size("exp"), []
    while 1 << len(bits) < size:
        bits.append(1 << len(bits))
    return bits


def routes_exp():
    bits = exp_bits()
    return bits[1:], bits[:0:-1]


def spread_exp(column):
    count = column.shape[0]
    halves = []
    for half, order in zip((column[: count // 2], column[count // 2 :]), routes_exp()):
        half = half[None]
        for bit in order:
            other = swap_exp(half, bit)
            half = jnp.where(bit_set(bit), jnp.concatenate([other, half]), jnp.concatenate([half, other]))
        halves.append(half)
    return halves


def spread_core(halves):
    bits = exp_bits()
    done = []
    for half, order in zip(halves, routes_exp()):
        other = swap_exp(half, 1)
        mine_first = bit_set(1)
        pair = jnp.stack([jnp.where(mine_first, other, half), jnp.where(mine_first, half, other)])
        pair = pair.reshape((2,) + (2,) * len(order) + half.shape[1:])
        axes = [1 + order[::-1].index(bit) for bit in bits[:0:-1]] + [0]
        axes = [len(axes)] + axes + list(range(len(axes) + 1, pair.ndim))
        pair = pair.transpose(axes)
        done.append(pair.reshape((half.shape[1], 1 << len(bits)) + half.shape[2:]))
    return done


def join_weights(done, first, rows):
    width = done[0].shape[-1]
    return jnp.concatenate([half[:, :, first : first + rows].reshape(-1, width) for half in done])


def scatter_exp(keep, send):
    count, bits = lax.axis_size("ctx"), exp_bits()
    chip = (keep.astype(F32) + swap_exp(send, 1).astype(F32)).astype(BF16)
    chip = chip.reshape((count, -1) + chip.shape[1:])
    sums = []
    for half, order in zip((chip[: count // 2], chip[count // 2 :]), routes_exp()):
        half = half.reshape((count // 2,) + (2,) * (len(bits) - 1) + half.shape[2:])
        left = bits[:0:-1]
        for bit in order:
            axis = 1 + left.index(bit)
            low = lax.index_in_dim(half, 0, axis, keepdims=False)
            high = lax.index_in_dim(half, 1, axis, keepdims=False)
            keep = jnp.where(bit_set(bit), high, low)
            send = jnp.where(bit_set(bit), low, high)
            half = (keep.astype(F32) + swap_exp(send, bit).astype(F32)).astype(BF16)
            left = [b for b in left if b != bit]
        sums.append(half)
    return jnp.concatenate(sums)


def scatter_ctx(parts):
    sent = (None, None)
    for hop in range(1, lax.axis_size("ctx")):
        sent = scatter_hop(*scatter_add(parts, hop, *sent), hop)
    return scatter_end(parts, *sent)


def slab_kernel(part, x_ref, q_ref, k_ref, v_ref, o_ref, g_ref, tail_ref, keep_ref, send_ref, x_turned, o_turned, total):
    core = lax.rem(lax.axis_index("exp"), 2)
    own = q_ref.shape[0]

    @pl.when(pl.program_id(0) == 0)
    def _():
        x_turned[...] = x_ref[...].T
        o_turned[...] = o_ref[...].T

    for place, (left, right) in enumerate(
        (
            (x_turned[:, x_turned.shape[1] - own :], q_ref[...]),
            (x_turned[...], k_ref[...]),
            (x_turned[...], v_ref[...]),
            (o_turned[...], g_ref[...]),
        )
    ):
        total[...] = dot(left, right)
        rows = slice(place * part, (place + 1) * part)
        for slab in range(keep_ref.shape[0]):
            first = 2 * slab * part
            keep_ref[slab, rows, :] = total[pl.ds(first + core * part, part), :].astype(BF16)
            send_ref[slab, rows, :] = total[pl.ds(first + (1 - core) * part, part), :].astype(BF16)
    for slab in range(keep_ref.shape[0]):
        keep_ref[slab, 4 * part :, :] = tail_ref[2 * slab + core]
        send_ref[slab, 4 * part :, :] = tail_ref[2 * slab + 1 - core]


def make_slabs(normed_all, query_grad, key_grad, value_grad, attended, branch_grad, tail):
    devices, extra, width = tail.shape
    all_rows, own = normed_all.shape[0], query_grad.shape[0]
    part, tile = width // devices, 256
    slab_rows = 4 * part + extra
    whole = lambda i: (0, 0)
    column = lambda i: (0, i)
    out = pl.BlockSpec((devices // 2, slab_rows, tile), lambda i: (0, 0, i))
    shape = jax.ShapeDtypeStruct((devices // 2, slab_rows, width), BF16)
    return pl.pallas_call(
        functools.partial(slab_kernel, part),
        grid=(width // tile,),
        in_specs=[
            pl.BlockSpec((all_rows, width), whole),
            pl.BlockSpec((own, tile), column),
            pl.BlockSpec((all_rows, tile), column),
            pl.BlockSpec((all_rows, tile), column),
            pl.BlockSpec((own, width), whole),
            pl.BlockSpec((own, tile), column),
            pl.BlockSpec((devices, extra, tile), lambda i: (0, 0, i)),
        ],
        out_specs=[out, out],
        out_shape=[shape, shape],
        scratch_shapes=[
            pltpu.VMEM((width, all_rows), BF16),
            pltpu.VMEM((width, own), BF16),
            pltpu.VMEM((width, tile), F32),
        ],
        compiler_params=params(),
        cost_estimate=brief(),
        name="slabs",
    )(normed_all, query_grad, key_grad, value_grad, attended, branch_grad, tail)


def exchange(blocks):
    return lax.all_to_all(blocks, "exp", split_axis=0, concat_axis=0, tiled=True)


def body(
    tokens,
    w_query,
    w_key,
    w_value,
    w_out,
    w_router,
    gain_attn,
    gain_mlp,
    pos_bias,
    exp_gate,
    exp_up,
    exp_down,
    doc_lengths,
    bucket_of,
    expert_ids,
    cotangent,
):
    both = ("ctx", "exp")
    own_tokens = tokens[0]
    rows, width = own_tokens.shape
    experts = w_router.shape[1]
    capacity = (5 * TOP * rows + 4 * experts - 1) // (4 * experts)
    reach = (WINDOW + rows - 2) // rows
    scale = HEAD_DIM ** (-0.5)
    ctx_index, ctx_count = lax.axis_index("ctx"), lax.axis_size("ctx")
    exp_index = lax.axis_index("exp")
    part = w_query.shape[0]
    bias_part = pos_bias.shape[0]
    devices = width // part

    expert_range = jnp.arange(experts, dtype=jnp.int32)
    named = jnp.any(expert_ids[0][:, :, None] == expert_range, axis=1)
    named_low = named.astype(BF16)
    step = jnp.arange(rows, dtype=jnp.int32)
    earlier = (step[:, None] > step[None, :]).astype(BF16)
    slots = dot(earlier, named_low).astype(jnp.int32)
    slots = jnp.where(named, slots, -1).T
    routes = (slots[:, None, :] == jnp.arange(capacity, dtype=jnp.int32)[None, :, None]).astype(BF16)
    routes = routes.reshape(experts * capacity, rows)

    names = jnp.pad(named_low, ((0, 0), (0, LANES - experts)))
    early = dot(routes, jnp.concatenate([cotangent[0], names], axis=1)).astype(BF16)
    early = exchange(early.reshape(experts, capacity, width + LANES)).reshape(-1, width + LANES)

    held, share = exp_gate.shape[1], exp_down.shape[1]
    sizes = (share * 5 // 11, share * 6 // 11)
    packed, first = [], 0
    for size in sizes:
        columns = [slice(z * share + first, z * share + first + size) for z in range(ctx_count)]
        parts = [weight[0][:, at] for weight in (exp_gate, exp_up) for at in columns]
        packed.append(jnp.concatenate(parts + [pack_down(exp_down[0][first : first + size], held)], axis=1))
        first += size

    small = jnp.concatenate([w_router.reshape(-1), gain_attn, gain_mlp, pos_bias])
    small = jnp.pad(small, (0, width - small.shape[0]))[None]
    small = lax.all_gather(jnp.pad(small, ((0, 15), (0, 0))), both, axis=0)[:, 0]
    at = part * experts
    full_router = small[:, :at].reshape(width, experts)
    full_gain_attn = small[:, at : at + part].reshape(width).astype(F32)
    full_gain_mlp = small[:, at + part : at + 2 * part].reshape(width).astype(F32)
    table = small[:, at + 2 * part : at + 2 * part + bias_part].reshape(HEADS, BUCKETS)
    column = gather_ctx(jnp.concatenate([w_query, w_key, w_value, w_out], axis=0)[None])
    halo = [shift_ctx(own_tokens, 1), own_tokens]
    column, halo[0], early, packed[0] = together(column, halo[0], early, packed[0])
    for _ in range(1, reach):
        halo.insert(0, shift_ctx(halo[0], 1))
    packed[0], halo[0] = together(packed[0], halo[0])
    chunk0 = lax.all_gather(packed[0], "ctx", axis=0, tiled=True)
    onehot_bucket = (bucket_of[None, :] == jnp.arange(BUCKETS, dtype=jnp.int32)[:, None]).astype(BF16)
    band = make_band(dot(table, onehot_bucket))
    *halves, band = together(*spread_exp(column), band)
    dense = spread_core(halves)
    full_query, full_key, full_value, full_out = (join_weights(dense, i * part, part) for i in range(4))
    inputs_all = jnp.concatenate(halo, axis=0).astype(F32)
    inputs = own_tokens.astype(F32)

    ends = jnp.cumsum(doc_lengths[0])

    def documents(positions):
        return jnp.sum((positions[:, None] >= ends[None, :]).astype(jnp.int32), axis=1)[:, None]

    feature = (jnp.arange(2 * HEAD_DIM, dtype=jnp.int32) % HEAD_DIM)[None, :]
    docs = doc_lengths.shape[1] + 1
    query_pos = ctx_index * rows + step
    key_pos = (ctx_index - reach) * rows + jnp.arange((reach + 1) * rows, dtype=jnp.int32)
    query_doc = (feature == documents(query_pos)).astype(BF16)
    same = (feature == documents(key_pos)) & (key_pos[:, None] >= 0)
    key_doc = jnp.where(same | (feature >= docs), 0.0, NEGATIVE).astype(BF16)

    normed_all = norm_rows(inputs_all, full_gain_attn).astype(BF16)
    normed = normed_all[reach * rows :]
    queries = (dot(normed, full_query).astype(BF16)) * jnp.asarray(scale, BF16)
    keys = dot(normed_all, full_key).astype(BF16)
    values = dot(normed_all, full_value).astype(BF16)
    attended, lse = attend(queries, keys, values, query_doc, key_doc, band)
    middle = inputs + dot(attended, full_out)
    normed_mlp = norm_rows(middle, full_gain_mlp).astype(BF16)

    sent = dot(routes, normed_mlp).astype(BF16)
    arrived = exchange(sent.reshape(experts, capacity, width)).reshape(-1, width)
    router_turned = jnp.pad(full_router.T, ((0, LANES - experts), (0, 0)))
    extras = (early, router_turned)
    units0, units1 = (size * ctx_count for size in sizes)
    arrived, packed[1] = together(arrived, packed[1])
    up = down = packed[1]
    pieces = [up]
    hidden, dboth, carried, _ = run_expert(True, False, units0, ctx_count, arrived, [chunk0], extras, None)
    grad0 = expert_weights(units0, ctx_count, arrived, carried[0], dboth, hidden)
    sent = (None, None)
    for hop in range(1, ctx_count):
        up, down = gather_hop(up, down, hop)
        if hop == 1:
            up, down, grad0 = together(up, down, grad0)
            parts0 = grad0.reshape(ctx_count, held, -1)
        else:
            sent = scatter_hop(*scatter_add(parts0, hop - 1, *sent), hop - 1)
            up, down, *sent = together(up, down, *sent)
        pieces += [up, down]
    arrived, *sent = together(arrived, *scatter_add(parts0, ctx_count - 1, *sent))
    sent = scatter_hop(*sent, ctx_count - 1)
    hidden, dboth, carried, router_grad = run_expert(
        False, True, units1, ctx_count, arrived, pieces, extras, carried
    )
    low, made, back, _ = carried
    hidden, dboth, low, made, back, *sent = together(hidden, dboth, low, made, back, *sent)
    grad1 = expert_weights(units1, ctx_count, arrived, low, dboth, hidden, True)
    total1 = lax.psum_scatter(grad1, "ctx", scatter_dimension=0, tiled=True)
    back = exchange(back.reshape(experts, capacity, width)).reshape(-1, width)

    upstream = cotangent[0].astype(F32)
    normed_mlp_grad = dot_rows(routes, back)
    _, second_pull = jax.vjp(norm_rows, middle, full_gain_mlp)
    middle_norm_grad, gain_mlp_grad = second_pull(normed_mlp_grad)
    middle_grad = upstream + middle_norm_grad
    branch_grad = middle_grad.astype(BF16)
    attended_grad = dot_last(branch_grad, full_out).astype(BF16)
    made, attended_grad = together(made, attended_grad)
    made = exchange(made.reshape(experts, capacity, width)).reshape(-1, width)
    query_grad, key_grad, value_grad, band_grad = attend_back(
        queries, keys, values, attended_grad, attended, lse, query_doc, key_doc, band
    )
    bias_grad = jnp.dot(
        sum_band(band_grad), onehot_bucket.T.astype(F32), precision=lax.Precision.HIGHEST
    )

    normed_grad_all = dot_last(key_grad, full_key) + dot_last(value_grad, full_value)
    own_grad = normed_grad_all[reach * rows :] + dot_last(query_grad, full_query)
    halo_grad = normed_grad_all[: reach * rows]
    _, first_pull = jax.vjp(norm_rows, inputs_all, full_gain_attn)
    gain_attn_grad = first_pull(jnp.concatenate([halo_grad, own_grad], axis=0))[1]
    tail = jnp.concatenate(
        [
            router_grad[:, :experts].reshape(devices, -1),
            gain_attn_grad.reshape(devices, part),
            gain_mlp_grad.reshape(devices, part),
            bias_grad.reshape(devices, bias_part),
        ],
        axis=1,
    ).astype(BF16)
    tail = jnp.pad(tail[:, None, :], ((0, 0), (0, 15), (0, width - tail.shape[1])))
    query_grad, made = together(query_grad, made)
    output = (middle + dot_rows(routes, made)).astype(BF16)
    keep, send = make_slabs(normed_all, query_grad, key_grad, value_grad, attended, branch_grad, tail)
    parts = scatter_exp(keep, send)

    returning = None
    for stride in range(reach, 0, -1):
        piece = halo_grad[(reach - stride) * rows : (reach - stride + 1) * rows]
        if returning is not None:
            parts, returning, *sent = together(parts, returning, *sent)
            piece = piece + returning.astype(F32)
        returning = shift_ctx(piece.astype(BF16), -1)
    sums = scatter_ctx(parts)
    _, own_pull = jax.vjp(norm_rows, inputs, full_gain_attn)
    input_grad = middle_grad + own_pull(own_grad + returning.astype(F32))[0]
    scattered = [scatter_end(parts0, *sent), total1.astype(F32)]
    gate_parts, up_parts, down_parts = [], [], []
    for size, total in zip(sizes, scattered):
        units = size * ctx_count
        gate_parts.append(total[:, :units])
        up_parts.append(total[:, units : 2 * units])
        down_parts.append(unpack_down(total[:, 2 * units :], size, width))

    def in_order(parts):
        shares = [part[:, z * (part.shape[1] // ctx_count) : (z + 1) * (part.shape[1] // ctx_count)]
                  for z in range(ctx_count) for part in parts]
        return jnp.concatenate(shares, axis=1)[None]

    expert_grads = (
        in_order(gate_parts),
        in_order(up_parts),
        jnp.concatenate(down_parts, axis=0)[None],
    )
    tail = sums[4 * part]
    at = part * experts
    return (
        output[None],
        input_grad[None],
        sums[:part],
        sums[part : 2 * part],
        sums[2 * part : 3 * part],
        sums[3 * part : 4 * part],
        tail[:at].reshape(part, experts),
        tail[at : at + part],
        tail[at + part : at + 2 * part],
        tail[at + 2 * part : at + 2 * part + bias_part],
        expert_grads[0],
        expert_grads[1],
        expert_grads[2],
    )


def solution(mesh):
    rows3 = P("exp", "ctx", None)
    dense2 = P(("ctx", "exp"), None)
    dense1 = P(("ctx", "exp"))
    return jax.shard_map(
        body,
        mesh=mesh,
        in_specs=(
            rows3,
            dense2,
            dense2,
            dense2,
            dense2,
            dense2,
            dense1,
            dense1,
            dense1,
            rows3,
            rows3,
            rows3,
            P("exp", None),
            P(),
            rows3,
            rows3,
        ),
        out_specs=(
            rows3,
            rows3,
            dense2,
            dense2,
            dense2,
            dense2,
            dense2,
            dense1,
            dense1,
            dense1,
            rows3,
            rows3,
            rows3,
        ),
        check_vma=False,
    )
```

```python
import functools

import jax
import jax.numpy as jnp
from jax import lax
from jax.experimental import pallas as pl
from jax.experimental.pallas import tpu as pltpu
from jax.sharding import PartitionSpec as P

HEADS = 16
HEAD_DIM = 64
BUCKETS = 32
TOP = 2
WINDOW = 1024

EPSILON = 1e-06
NEGATIVE = -1e30
LANES = 128
CHUNK = 256
FF_TILE = 512
ROW_TILE = 256
VMEM_LIMIT = 58 * 2**20
BF16 = jnp.bfloat16
F32 = jnp.float32


def shift_ctx(block, distance):
    devices = range(lax.axis_size("ctx"))
    route = [(i - distance, i) for i in devices if i - distance in devices]
    return lax.ppermute(block, "ctx", route)


def norm_rows(values, gain):
    return values * lax.rsqrt(jnp.mean(values * values, axis=-1, keepdims=True) + EPSILON) * gain


def dot(left, right):
    return jnp.dot(left, right, preferred_element_type=F32)


def dot_rows(left, right):
    return lax.dot_general(left, right, (((0,), (0,)), ((), ())), preferred_element_type=F32)


def dot_last(left, right):
    return lax.dot_general(left, right, (((1,), (1,)), ((), ())), preferred_element_type=F32)


def params(**more):
    return pltpu.CompilerParams(vmem_limit_bytes=VMEM_LIMIT, **more)


def brief():
    return pl.CostEstimate(flops=2**20, bytes_accessed=2**20, transcendentals=0)


def band_kernel(bias_ref, band_ref):
    blocks = WINDOW // LANES
    size = (blocks + 2) * LANES
    for head in range(bias_ref.shape[0]):
        row = jnp.broadcast_to(bias_ref[head : head + 1, :], (8, size))
        eight = pltpu.roll(row, 0, 1, stride=1, stride_axis=0)
        for group in range(LANES // 8):
            wide = pltpu.roll(eight, 8 * group, 1) if group else eight
            for a in range(blocks + 1):
                first = a * LANES + group * 8
                at = (blocks + 1 - a) * LANES
                band_ref[head, first : first + 8, :] = wide[:, at : at + LANES]


def make_band(bias_dist):
    group = 8
    edge = jnp.full((HEADS, LANES), NEGATIVE, F32)
    padded = jnp.concatenate([edge, bias_dist, edge], axis=1)
    return pl.pallas_call(
        band_kernel,
        grid=(HEADS // group,),
        in_specs=[pl.BlockSpec((group, WINDOW + 2 * LANES), lambda h: (h, 0))],
        out_specs=pl.BlockSpec((group, WINDOW + LANES, LANES), lambda h: (h, 0, 0)),
        out_shape=jax.ShapeDtypeStruct((HEADS, WINDOW + LANES, LANES), F32),
        compiler_params=params(),
        cost_estimate=brief(),
        name="bias_band",
    )(padded)


def sum_band(band_ref):
    blocks = WINDOW // LANES
    size = (blocks + 2) * LANES
    row = lax.broadcasted_iota(jnp.int32, (8, 1), 0)
    edge = jnp.zeros((8, LANES), F32)
    total = None
    for group in range(LANES // 8):
        pieces = [edge]
        for a in range(blocks, -1, -1):
            first = a * LANES + group * 8
            pieces.append(band_ref[first : first + 8, :])
        wide = jnp.concatenate(pieces, axis=1)
        if group:
            wide = pltpu.roll(wide, size - 8 * group, 1)
        total = wide if total is None else total + wide
    dist = jnp.zeros_like(total)
    for r in range(8):
        turned = pltpu.roll(total, size - r, 1) if r else total
        dist = dist + jnp.where(row == r, turned, 0.0)
    return jnp.sum(dist, axis=0, keepdims=True)[:, LANES : LANES + WINDOW]


def head_lanes(head):
    lane = lax.broadcasted_iota(jnp.int32, (1, 2 * HEAD_DIM), 1)
    return (lane >= head * HEAD_DIM) & (lane < (head + 1) * HEAD_DIM)


def masked_scores(head, start, q_ref, k_ref, qdoc_ref, kdoc_ref):
    span = WINDOW + CHUNK
    mine = head_lanes(head)
    q_rows, k_rows = pl.ds(start, CHUNK), pl.ds(start, span)
    q_part = jnp.where(mine, q_ref[q_rows, :], qdoc_ref[q_rows, :])
    k_part = jnp.where(mine, k_ref[k_rows, :], kdoc_ref[k_rows, :])
    return dot_last(k_part, q_part)


def sub_blocks():
    return [(s * LANES, WINDOW + LANES) for s in range(CHUNK // LANES)]


def spread(parts):
    span = WINDOW + CHUNK
    columns = []
    for (first, rows), part in zip(sub_blocks(), parts):
        pieces = []
        if first:
            pieces.append(jnp.zeros((first, LANES), part.dtype))
        pieces.append(part)
        if span - first - rows:
            pieces.append(jnp.zeros((span - first - rows, LANES), part.dtype))
        columns.append(jnp.concatenate(pieces, axis=0) if len(pieces) > 1 else part)
    return jnp.concatenate(columns, axis=1)


def attend_kernel(q_ref, k_ref, v_ref, qdoc_ref, kdoc_ref, band_ref, o_ref, lse_ref):
    span = WINDOW + CHUNK
    for start in range(0, q_ref.shape[0], CHUNK):
        v_turned = v_ref[pl.ds(start, span), :].T
        outs = []
        for head in range(2):
            scores = masked_scores(head, start, q_ref, k_ref, qdoc_ref, kdoc_ref)
            band = band_ref[head]
            low, scale, logs = [], [], []
            for s, (first, rows) in enumerate(sub_blocks()):
                part = scores[first : first + rows, s * LANES : (s + 1) * LANES] + band
                top = jnp.max(part, axis=0, keepdims=True)
                expo = jnp.exp(part - top)
                total = jnp.sum(expo, axis=0, keepdims=True)
                low.append(expo.astype(BF16))
                scale.append(1.0 / total)
                logs.append(top + jnp.log(total))
            out = dot(v_turned[head * HEAD_DIM : (head + 1) * HEAD_DIM], spread(low))
            outs.append(out * jnp.concatenate(scale, axis=1))
            lse_ref[0, head : head + 1, pl.ds(start, CHUNK)] = jnp.concatenate(logs, axis=1)
        o_ref[pl.ds(start, CHUNK), :] = jnp.concatenate(outs, axis=0).T.astype(BF16)


def attend(queries, keys, values, query_doc, key_doc, band):
    rows, width = queries.shape
    keys_rows = keys.shape[0]
    pairs = HEADS // 2
    wide = 2 * HEAD_DIM
    return pl.pallas_call(
        attend_kernel,
        grid=(pairs,),
        in_specs=[
            pl.BlockSpec((rows, wide), lambda p: (0, p)),
            pl.BlockSpec((keys_rows, wide), lambda p: (0, p)),
            pl.BlockSpec((keys_rows, wide), lambda p: (0, p)),
            pl.BlockSpec((rows, wide), lambda p: (0, 0)),
            pl.BlockSpec((keys_rows, wide), lambda p: (0, 0)),
            pl.BlockSpec((2, WINDOW + LANES, LANES), lambda p: (p, 0, 0)),
        ],
        out_specs=[
            pl.BlockSpec((rows, wide), lambda p: (0, p)),
            pl.BlockSpec((1, 2, rows), lambda p: (p, 0, 0)),
        ],
        out_shape=[
            jax.ShapeDtypeStruct((rows, width), BF16),
            jax.ShapeDtypeStruct((pairs, 2, rows), F32),
        ],
        compiler_params=params(),
        cost_estimate=brief(),
        name="attend",
    )(queries, keys, values, query_doc, key_doc, band)


def probs_kernel(q_ref, k_ref, qdoc_ref, kdoc_ref, band_ref, lse_ref, probs_ref):
    for chunk in range(q_ref.shape[0] // CHUNK):
        start = chunk * CHUNK
        for head in range(2):
            scores = masked_scores(head, start, q_ref, k_ref, qdoc_ref, kdoc_ref)
            band = band_ref[head]
            lse = lse_ref[0, head : head + 1, pl.ds(start, CHUNK)]
            parts = []
            for s, (first, rows) in enumerate(sub_blocks()):
                lanes = slice(s * LANES, (s + 1) * LANES)
                parts.append(jnp.exp(scores[first : first + rows, lanes] + band - lse[:, lanes]).astype(BF16))
            probs_ref[head, chunk] = spread(parts)


def make_probs(queries, keys, query_doc, key_doc, band, lse):
    rows, width = queries.shape
    keys_rows = keys.shape[0]
    pairs = HEADS // 2
    wide = 2 * HEAD_DIM
    span, chunks = WINDOW + CHUNK, rows // CHUNK
    return pl.pallas_call(
        probs_kernel,
        grid=(pairs,),
        in_specs=[
            pl.BlockSpec((rows, wide), lambda p: (0, p)),
            pl.BlockSpec((keys_rows, wide), lambda p: (0, p)),
            pl.BlockSpec((rows, wide), lambda p: (0, 0)),
            pl.BlockSpec((keys_rows, wide), lambda p: (0, 0)),
            pl.BlockSpec((2, WINDOW + LANES, LANES), lambda p: (p, 0, 0)),
            pl.BlockSpec((1, 2, rows), lambda p: (p, 0, 0)),
        ],
        out_specs=pl.BlockSpec((2, chunks, span, CHUNK), lambda p: (p, 0, 0, 0)),
        out_shape=jax.ShapeDtypeStruct((HEADS, chunks, span, CHUNK), BF16),
        compiler_params=params(),
        cost_estimate=brief(),
        name="probs",
    )(queries, keys, query_doc, key_doc, band, lse)


def attend_back_kernel(
    q_ref, k_ref, v_ref, g_ref, o_ref, probs_ref, dq_ref, dk_ref, dv_ref, dist_ref, dk_sum, dv_sum, dband
):
    span = WINDOW + CHUNK
    dk_sum[...] = jnp.zeros_like(dk_sum)
    dv_sum[...] = jnp.zeros_like(dv_sum)
    for chunk in range(q_ref.shape[0] // CHUNK):
        start = chunk * CHUNK
        q_rows, k_rows = pl.ds(start, CHUNK), pl.ds(start, span)
        k_turned = k_ref[k_rows, :].T
        product = (g_ref[q_rows, :].astype(F32) * o_ref[q_rows, :].astype(F32)).T
        dq_parts = []
        for head in range(2):
            mine = head_lanes(head)
            zero = jnp.zeros((), BF16)
            g_part = jnp.where(mine, g_ref[q_rows, :], zero)
            q_part = jnp.where(mine, q_ref[q_rows, :], zero)
            prob_grad = dot_last(v_ref[k_rows, :], g_part)
            delta = jnp.sum(product[head * HEAD_DIM : (head + 1) * HEAD_DIM], axis=0, keepdims=True)
            grad_low, grad_sum = [], None
            for s, (first, rows) in enumerate(sub_blocks()):
                lanes = slice(s * LANES, (s + 1) * LANES)
                probs = probs_ref[head, chunk, first : first + rows, lanes].astype(F32)
                grad = probs * (prob_grad[first : first + rows, lanes] - delta[:, lanes])
                grad_low.append(grad.astype(BF16))
                grad_sum = grad if grad_sum is None else grad_sum + grad
            if chunk == 0:
                dband[head] = grad_sum
            else:
                dband[head] = dband[head] + grad_sum
            grads = spread(grad_low)
            dk_sum[k_rows, :] += dot(grads, q_part)
            dv_sum[k_rows, :] += dot(probs_ref[head, chunk], g_part)
            dq_parts.append(dot(k_turned[head * HEAD_DIM : (head + 1) * HEAD_DIM], grads))
        turned = jnp.concatenate(dq_parts, axis=0).T
        dq_ref[q_rows, :] = (turned * HEAD_DIM ** (-0.5)).astype(BF16)
    dk_ref[...] = dk_sum[...].astype(BF16)
    dv_ref[...] = dv_sum[...].astype(BF16)
    for head in range(2):
        dist_ref[0, head : head + 1, :] = sum_band(dband.at[head])


def attend_back(queries, keys, values, grad, out, probs):
    rows, width = queries.shape
    keys_rows = keys.shape[0]
    pairs = HEADS // 2
    wide = 2 * HEAD_DIM
    q_spec = pl.BlockSpec((rows, wide), lambda p: (0, p))
    k_spec = pl.BlockSpec((keys_rows, wide), lambda p: (0, p))
    return pl.pallas_call(
        attend_back_kernel,
        grid=(pairs,),
        in_specs=[
            q_spec,
            k_spec,
            k_spec,
            q_spec,
            q_spec,
            pl.BlockSpec((2,) + probs.shape[1:], lambda p: (p, 0, 0, 0)),
        ],
        out_specs=[q_spec, k_spec, k_spec, pl.BlockSpec((1, 2, WINDOW), lambda p: (p, 0, 0))],
        out_shape=[
            jax.ShapeDtypeStruct((rows, width), BF16),
            jax.ShapeDtypeStruct((keys_rows, width), BF16),
            jax.ShapeDtypeStruct((keys_rows, width), BF16),
            jax.ShapeDtypeStruct((pairs, 2, WINDOW), F32),
        ],
        scratch_shapes=[
            pltpu.VMEM((keys_rows, wide), F32),
            pltpu.VMEM((keys_rows, wide), F32),
            pltpu.VMEM((2, WINDOW + LANES, LANES), F32),
        ],
        compiler_params=params(),
        cost_estimate=pl.CostEstimate(
            flops=20 * rows * WINDOW * width * 2, bytes_accessed=2**20, transcendentals=0
        ),
        name="attend_back",
    )(queries, keys, values, grad, out, probs)


def down_blocks(units, width, count):
    held, share = width // count, units // count
    extra = share - held
    wide = width * extra // held
    blocks = []
    for z in range(count):
        blocks.append(((z * held, 0), (z * share, 0), (held, width)))
        for m in range(held // extra):
            blocks.append(((z * held + m * extra, width), (z * share + held, m * wide), (extra, wide)))
    return blocks


def pack_down(down, held):
    extra, width = down.shape[0] - held, down.shape[1]
    wide = width * extra // held
    rest = [down[held:, m * wide : (m + 1) * wide] for m in range(held // extra)]
    return jnp.concatenate([down[:held], jnp.concatenate(rest, axis=0)], axis=1)


def unpack_down(packed, size, width):
    held = packed.shape[0]
    extra = size - held
    rest = [packed[m * extra : (m + 1) * extra, width:] for m in range(held // extra)]
    return jnp.concatenate([packed[:, :width], jnp.concatenate(rest, axis=1)], axis=0)


def expert_kernel(first, last, units, count, parts, *refs):
    refs = list(refs)
    take = lambda: refs.pop(0)
    x_ref = take()
    pieces = [take() for _ in range(parts)]
    if first or last:
        c_ref, names_ref, router_ref = take(), take(), take()
    if not first:
        low_ref, made_in, back_in = take(), take(), take()
    if last and not first:
        gate_in = take()
    hidden_ref, dboth_ref = take(), take()
    if first:
        low_out = take()
    if first and not last:
        gate_out = take()
    made_ref, back_ref = take(), take()
    if last:
        drouter_ref = take()
    chunk_ref, down_s, sems = take(), take(), take()
    rows, width = x_ref.shape
    held = width // count
    index = lax.axis_index("ctx")

    def slot(z):
        return chunk_ref.at[z * held : (z + 1) * held]

    @pl.when(pl.program_id(0) == 0)
    def _():
        if parts == 1:
            for z in range(count):
                pltpu.make_async_copy(pieces[0].at[z * held : (z + 1) * held], slot(z), sems.at[z]).start()
        for z in range(count if parts > 1 else 0):
            for here in range(count):
                hop = abs(here - z)
                source = pieces[0 if hop == 0 else 2 * hop - 1 if z < here else 2 * hop]

                @pl.when(index == here)
                def _(source=source, z=z):
                    pltpu.make_async_copy(source, slot(z), sems.at[z]).start()

        for z in range(count):
            pltpu.make_async_copy(pieces[0].at[:held], slot(z), sems.at[z]).wait()

    x = x_ref[...]
    own = lax.broadcasted_iota(jnp.int32, (1, LANES), 1) == lax.axis_index("exp")
    if first:
        names = names_ref[...].astype(F32)
        logits = dot_last(x, router_ref[...]) * names
        mine = jnp.sum(jnp.where(own, logits, 0.0), axis=1, keepdims=True)
        theirs = jnp.sum(jnp.where(own, 0.0, logits), axis=1, keepdims=True)
        gate = jax.nn.sigmoid(mine - theirs)
        low_out[...] = (gate * c_ref[...].astype(F32)).astype(BF16)
        if not last:
            gate_out[...] = jnp.broadcast_to(gate, (rows, LANES))
        low_ref = low_out
    elif last:
        gate = gate_in[...][:, :1]
    @pl.when(pl.program_id(0) == 0)
    def _():
        for (row, column), (to_row, to_column), (high, wide) in down_blocks(units, width, count):
            from_columns = slice(2 * units + column, 2 * units + column + wide)
            down_s[to_row : to_row + high, to_column : to_column + wide] = chunk_ref[row : row + high, from_columns]

    for start in range(0, units, FF_TILE):
        stop = min(start + FF_TILE, units)
        at, up_at = slice(start, stop), slice(units + start, units + stop)
        gate_pre = dot(x, chunk_ref[:, at])
        up_pre = dot(x, chunk_ref[:, up_at])
        hidden_grad = dot_last(low_ref[...], down_s[at, :])
        root = 0.7978845608028654
        square = gate_pre * gate_pre
        bent = jnp.tanh(gate_pre * (root + root * 0.044715 * square))
        half = 0.5 * (1.0 + bent)
        act = gate_pre * half
        slope = half + 0.5 * gate_pre * (1.0 - bent * bent) * (root + 3.0 * root * 0.044715 * square)
        hidden_ref[:, at] = (act * up_pre).astype(BF16)
        dboth_ref[:, at] = (hidden_grad * up_pre * slope).astype(BF16)
        dboth_ref[:, up_at] = (hidden_grad * act).astype(BF16)
    made = dot(hidden_ref[...], down_s[...])
    back = dot_last(dboth_ref[...], chunk_ref[:, : 2 * units])
    if not first:
        made = made + made_in[...]
        back = back + back_in[...]
    if last:
        made = made.astype(BF16).astype(F32)
        names = names_ref[...].astype(F32)
        push = jnp.sum(c_ref[...].astype(F32) * made, axis=1, keepdims=True)
        push = push * gate * (1.0 - gate)
        logits_grad = push * jnp.where(own, names, -names)
        high = logits_grad.astype(BF16)
        low = (logits_grad - high.astype(F32)).astype(BF16)
        made = gate * made
        back = back + dot(high, router_ref[...]) + dot(low, router_ref[...])
        turned = x.T
        update = dot(turned, high) + dot(turned, low)

        @pl.when(pl.program_id(0) == 0)
        def _():
            drouter_ref[...] = update

        @pl.when(pl.program_id(0) > 0)
        def _():
            drouter_ref[...] += update

    made_ref[...] = made.astype(made_ref.dtype)
    back_ref[...] = back.astype(back_ref.dtype)


def run_expert(first, last, units, count, x, pieces, extras, carried):
    rows, width = x.shape
    whole = lambda i: (0, 0)
    step = lambda i: (i, 0)
    wide = pl.BlockSpec((ROW_TILE, width), step)
    thin = pl.BlockSpec((ROW_TILE, LANES), step)
    struct = jax.ShapeDtypeStruct
    early, router = extras
    operands = [x] + pieces
    in_specs = [wide] + [pl.BlockSpec(memory_space=pl.ANY)] * len(pieces)
    if first or last:
        operands += [early, early, router]
        names = pl.BlockSpec((ROW_TILE, LANES), lambda i: (i, width // LANES))
        in_specs += [wide, names, pl.BlockSpec((LANES, width), whole)]
    if not first:
        low, made, back, gate = carried
        operands += [low, made, back]
        in_specs += [wide, wide, wide]
        if last:
            operands.append(gate)
            in_specs.append(thin)
    out_shape = [struct((rows, units), BF16), struct((rows, 2 * units), BF16)]
    out_specs = [pl.BlockSpec((ROW_TILE, units), step), pl.BlockSpec((ROW_TILE, 2 * units), step)]
    if first:
        out_shape.append(struct((rows, width), BF16))
        out_specs.append(wide)
        if not last:
            out_shape.append(struct((rows, LANES), F32))
            out_specs.append(thin)
    kept = BF16 if last else F32
    out_shape += [struct((rows, width), kept), struct((rows, width), kept)]
    out_specs += [wide, wide]
    if last:
        out_shape.append(struct((width, LANES), F32))
        out_specs.append(pl.BlockSpec((width, LANES), whole))
    outs = list(
        pl.pallas_call(
            functools.partial(expert_kernel, first, last, units, count, len(pieces)),
            grid=(rows // ROW_TILE,),
            in_specs=in_specs,
            out_specs=out_specs,
            out_shape=out_shape,
            scratch_shapes=[
                pltpu.VMEM((width, pieces[0].shape[1]), BF16),
                pltpu.VMEM((units, width), BF16),
                pltpu.SemaphoreType.DMA((count,)),
            ],
            compiler_params=params(),
            cost_estimate=brief(),
            name="expert",
        )(*operands)
    )
    hidden, dboth = outs[:2]
    if first:
        low = outs[2]
        gate = None if last else outs[3]
    if last:
        made, back, drouter = outs[-3:]
        return hidden, dboth, (low, made, back, gate), drouter
    made, back = outs[-2:]
    return hidden, dboth, (low, made, back, gate), None


def expert_weights_kernel(
    units, count, x_ref, low_ref, dboth_ref, hidden_ref, grad_ref, x_turned, hidden_turned, rest
):
    step = pl.program_id(0)
    tile = low_ref.shape[1]
    width = x_ref.shape[1]
    both_steps, down_steps = 2 * units // tile, width // tile

    @pl.when(step == 0)
    def _():
        x_turned[...] = x_ref[...].T

    @pl.when(step < both_steps)
    def _():
        grad_ref[...] = dot(x_turned[...], dboth_ref[...]).astype(BF16)

    @pl.when(step == both_steps)
    def _():
        hidden_turned[...] = hidden_ref[...].T

    for place in range(down_steps):

        @pl.when(step == both_steps + place)
        def _(place=place):
            total = dot(hidden_turned[...], low_ref[...]).astype(BF16)
            first = place * tile
            for (row, column), (from_row, from_column), (high, wide) in down_blocks(units, width, count):
                if column == 0:
                    grad_ref[row : row + high, :] = total[from_row : from_row + high]
                    continue
                low, top = max(first, from_column), min(first + tile, from_column + wide)
                if low < top:
                    rest[row : row + high, low - from_column : top - from_column] = total[
                        from_row : from_row + high, low - first : top - first
                    ]

    for place in range(rest.shape[1] // tile):

        @pl.when(step == both_steps + down_steps + place)
        def _(place=place):
            grad_ref[...] = rest[:, place * tile : (place + 1) * tile]


def expert_weights(units, count, x, low, dboth, hidden, long=False):
    rows, width = x.shape
    tile = 512
    extra_steps = -(-(units - width) // tile)
    both_steps, down_steps = 2 * units // tile, width // tile
    whole = lambda i: (0, 0)
    work = pl.CostEstimate(flops=6 * rows * width * units, bytes_accessed=2**20, transcendentals=0)
    return pl.pallas_call(
        functools.partial(expert_weights_kernel, units, count),
        grid=(both_steps + down_steps + extra_steps,),
        in_specs=[
            pl.BlockSpec((rows, width), whole),
            pl.BlockSpec((rows, tile), lambda i: (0, jnp.clip(i - both_steps, 0, down_steps - 1))),
            pl.BlockSpec((rows, tile), lambda i: (0, jnp.minimum(i, both_steps - 1))),
            pl.BlockSpec((rows, units), whole),
        ],
        out_specs=pl.BlockSpec((width, tile), lambda i: (0, i)),
        out_shape=jax.ShapeDtypeStruct((width, 3 * units), BF16),
        scratch_shapes=[
            pltpu.VMEM((width, rows), BF16),
            pltpu.VMEM((units, rows), BF16),
            pltpu.VMEM((width, extra_steps * tile), BF16),
        ],
        compiler_params=params(),
        cost_estimate=work if long else brief(),
        name="expert_weights",
    )(x, low, dboth, hidden)


def expert_sums_kernel(sizes, count, own_ref, up_ref, down_ref, last_ref, gate_out, up_out, down_out):
    held, width = own_ref.shape[0], down_out.shape[1]
    extras = [size - held for size in sizes]
    tile = min(extras)
    for first in range(0, held, tile):
        rows = slice(first, first + tile)
        totals = (
            own_ref[rows, :].astype(F32) + up_ref[rows, :].astype(F32) + down_ref[rows, :].astype(F32),
            last_ref[rows, :].astype(F32),
        )
        for out, part in ((gate_out, 0), (up_out, 1)):
            pieces = []
            for z in range(count):
                for size, total in zip(sizes, totals):
                    at = part * size * count + z * size
                    pieces.append(total[:, at : at + size])
            out[rows, :] = jnp.concatenate(pieces, axis=1)
        start = 0
        for size, extra, total in zip(sizes, extras, totals):
            wide = width * extra // held
            at = 2 * size * count
            down_out[start + first : start + first + tile, :] = total[:, at : at + width]
            to, columns = start + held + first % extra, first // extra * wide
            down_out[to : to + tile, columns : columns + wide] = total[:, at + width :]
            start += size


def expert_sums(sizes, count, own, up, down, last):
    held = own.shape[0]
    units = sum(sizes)
    struct = jax.ShapeDtypeStruct
    width = held * count
    return pl.pallas_call(
        functools.partial(expert_sums_kernel, sizes, count),
        in_specs=[pl.BlockSpec(memory_space=pltpu.VMEM)] * 4,
        out_specs=[pl.BlockSpec(memory_space=pltpu.VMEM)] * 3,
        out_shape=[
            struct((held, units * count), F32),
            struct((held, units * count), F32),
            struct((units, width), F32),
        ],
        compiler_params=params(),
        cost_estimate=brief(),
        name="expert_sums",
    )(own, up, down, last)


def ctx_moves(distance):
    devices = range(lax.axis_size("ctx"))
    return [(i - distance, i) for i in devices if i - distance in devices]


def together(*values):
    return lax.optimization_barrier(values)


def gather_ctx(piece):
    count, index, size = lax.axis_size("ctx"), lax.axis_index("ctx"), piece.shape[0]
    full = jnp.zeros((count * size,) + piece.shape[1:], piece.dtype)
    place = lambda buffer, part, at: lax.dynamic_update_slice_in_dim(buffer, part, at * size, 0)
    full = place(full, piece, index)
    up = down = piece
    for hop in range(1, count):
        up, down = shift_ctx(up, 1), shift_ctx(down, -1)
        for part, at, held in ((up, index - hop, index >= hop), (down, index + hop, index + hop < count)):
            at = jnp.clip(at, 0, count - 1)
            old = lax.dynamic_slice_in_dim(full, at * size, size, 0)
            full = place(full, jnp.where(held, part, old), at)
    return full


def gather_hop(up, down, hop):
    count = lax.axis_size("ctx")
    route = [(i, i + 1) for i in range(hop - 1, count - 1)]
    back = [(count - 1 - i, count - 1 - j) for i, j in route]
    return lax.ppermute(up, "ctx", route), lax.ppermute(down, "ctx", back)


def scatter_add(parts, hop, up=None, down=None):
    count, index = lax.axis_size("ctx"), lax.axis_index("ctx")

    def part(at):
        return lax.dynamic_index_in_dim(parts, jnp.clip(at, 0, count - 1), 0, keepdims=False).astype(F32)

    distance = count - hop
    mine_up, mine_down = part(index + distance), part(index - distance)
    if up is not None:
        mine_up, mine_down = mine_up + up.astype(F32), mine_down + down.astype(F32)
    return mine_up.astype(BF16), mine_down.astype(BF16)


def scatter_hop(up, down, hop):
    count = lax.axis_size("ctx")
    route = [(i, i + 1) for i in range(hop)]
    back = [(count - 1 - i, count - 1 - j) for i, j in route]
    return lax.ppermute(up, "ctx", route), lax.ppermute(down, "ctx", back)


def scatter_end(parts, up, down):
    own = lax.dynamic_index_in_dim(parts, lax.axis_index("ctx"), 0, keepdims=False).astype(F32)
    return own + up.astype(F32) + down.astype(F32)


def swap_exp(block, bit):
    return lax.ppermute(block, "exp", [(i, i ^ bit) for i in range(lax.axis_size("exp"))])


def bit_set(bit):
    return (lax.axis_index("exp") // bit) % 2 == 1


def exp_bits():
    size, bits = lax.axis_size("exp"), []
    while 1 << len(bits) < size:
        bits.append(1 << len(bits))
    return bits


def routes_exp():
    bits = exp_bits()
    return bits[1:], bits[:0:-1]


def spread_exp(column, then):
    count = column.shape[0]
    halves = [column[None, : count // 2], column[None, count // 2 :]]
    for step, bits in enumerate(zip(*routes_exp())):
        others = [swap_exp(half, bit) for half, bit in zip(halves, bits)]
        if step == 0:
            others = then(others)
        for place, (half, other, bit) in enumerate(zip(halves, others, bits)):
            halves[place] = jnp.where(
                bit_set(bit), jnp.concatenate([other, half]), jnp.concatenate([half, other])
            )
    return halves


def spread_core(halves):
    bits = exp_bits()
    done = []
    for half, order in zip(halves, routes_exp()):
        other = swap_exp(half, 1)
        mine_first = bit_set(1)
        pair = jnp.stack([jnp.where(mine_first, other, half), jnp.where(mine_first, half, other)])
        pair = pair.reshape((2,) + (2,) * len(order) + half.shape[1:])
        axes = [1 + order[::-1].index(bit) for bit in bits[:0:-1]] + [0]
        axes = [len(axes)] + axes + list(range(len(axes) + 1, pair.ndim))
        pair = pair.transpose(axes)
        done.append(pair.reshape((half.shape[1], 1 << len(bits)) + half.shape[2:]))
    return done


def join_weights(done, first, rows):
    width = done[0].shape[-1]
    return jnp.concatenate([half[:, :, first : first + rows].reshape(-1, width) for half in done])


def scatter_exp(keep, other):
    count, bits = lax.axis_size("ctx"), exp_bits()
    chip = (keep.astype(F32) + other.astype(F32)).astype(BF16)
    chip = chip.reshape((count, -1) + chip.shape[1:])
    sums = []
    for half, order in zip((chip[: count // 2], chip[count // 2 :]), routes_exp()):
        half = half.reshape((count // 2,) + (2,) * (len(bits) - 1) + half.shape[2:])
        left = bits[:0:-1]
        for bit in order:
            axis = 1 + left.index(bit)
            low = lax.index_in_dim(half, 0, axis, keepdims=False)
            high = lax.index_in_dim(half, 1, axis, keepdims=False)
            keep = jnp.where(bit_set(bit), high, low)
            send = jnp.where(bit_set(bit), low, high)
            half = (keep.astype(F32) + swap_exp(send, bit).astype(F32)).astype(BF16)
            left = [b for b in left if b != bit]
        sums.append(half)
    return jnp.concatenate(sums)


def normed_grad_kernel(
    halo_steps, x_ref, q_ref, k_ref, v_ref, wq_ref, wk_ref, wv_ref, halo_ref, own_ref, gain_ref, total
):
    step = pl.program_id(0)
    total[...] = dot_last(k_ref[...], wk_ref[...]) + dot_last(v_ref[...], wv_ref[...])

    @pl.when(step >= halo_steps)
    def _():
        total[...] += dot_last(q_ref[...], wq_ref[...])
        own_ref[...] = total[...]

    @pl.when(step < halo_steps)
    def _():
        halo_ref[...] = total[...].astype(BF16)

    x = x_ref[...].astype(F32)
    unit = x * lax.rsqrt(jnp.mean(x * x, axis=1, keepdims=True) + EPSILON)
    update = jnp.sum((total[...] * unit).reshape(-1, 8, x.shape[1]), axis=0)

    @pl.when(step == 0)
    def _():
        gain_ref[...] = update

    @pl.when(step > 0)
    def _():
        gain_ref[...] += update


def normed_grad_of(inputs_all, query_grad, key_grad, value_grad, full_query, full_key, full_value):
    all_rows, width = key_grad.shape
    own = query_grad.shape[0]
    tile = 256
    halo_steps = (all_rows - own) // tile
    row = lambda i: (i, 0)
    late = lambda i: (jnp.maximum(i - halo_steps, 0), 0)
    whole = lambda i: (0, 0)
    block = (tile, width)
    weight = pl.BlockSpec((width, width), whole, pipeline_mode=pl.Buffered(1))
    return pl.pallas_call(
        functools.partial(normed_grad_kernel, halo_steps),
        grid=(all_rows // tile,),
        in_specs=[
            pl.BlockSpec(block, row),
            pl.BlockSpec(block, late),
            pl.BlockSpec(block, row),
            pl.BlockSpec(block, row),
            weight,
            weight,
            weight,
        ],
        out_specs=[
            pl.BlockSpec(block, lambda i: (jnp.minimum(i, halo_steps - 1), 0)),
            pl.BlockSpec(block, late),
            pl.BlockSpec((8, width), whole),
        ],
        out_shape=[
            jax.ShapeDtypeStruct((all_rows - own, width), BF16),
            jax.ShapeDtypeStruct((own, width), F32),
            jax.ShapeDtypeStruct((8, width), F32),
        ],
        scratch_shapes=[pltpu.VMEM(block, F32)],
        compiler_params=params(),
        cost_estimate=brief(),
        name="normed_grad",
    )(inputs_all, query_grad, key_grad, value_grad, full_query, full_key, full_value)


def slab_kernel(part, x_ref, q_ref, k_ref, v_ref, o_ref, g_ref, tail_ref, keep_ref, send_ref, x_turned, o_turned, total):
    core = lax.rem(lax.axis_index("exp"), 2)
    own = q_ref.shape[0]

    @pl.when(pl.program_id(0) == 0)
    def _():
        x_turned[...] = x_ref[...].T
        o_turned[...] = o_ref[...].T

    for place, (left, right) in enumerate(
        (
            (x_turned[:, x_turned.shape[1] - own :], q_ref[...]),
            (x_turned[...], k_ref[...]),
            (x_turned[...], v_ref[...]),
            (o_turned[...], g_ref[...]),
        )
    ):
        total[...] = dot(left, right)
        rows = slice(place * part, (place + 1) * part)
        for slab in range(keep_ref.shape[0]):
            first = 2 * slab * part
            keep_ref[slab, rows, :] = total[pl.ds(first + core * part, part), :].astype(BF16)
            send_ref[slab, rows, :] = total[pl.ds(first + (1 - core) * part, part), :].astype(BF16)
    for slab in range(keep_ref.shape[0]):
        keep_ref[slab, 4 * part :, :] = tail_ref[2 * slab + core]
        send_ref[slab, 4 * part :, :] = tail_ref[2 * slab + 1 - core]


def make_slabs(normed_all, query_grad, key_grad, value_grad, attended, branch_grad, tail):
    devices, extra, width = tail.shape
    all_rows, own = normed_all.shape[0], query_grad.shape[0]
    part, tile = width // devices, 256
    slab_rows = 4 * part + extra
    whole = lambda i: (0, 0)
    column = lambda i: (0, i)
    out = pl.BlockSpec((devices // 2, slab_rows, tile), lambda i: (0, 0, i))
    shape = jax.ShapeDtypeStruct((devices // 2, slab_rows, width), BF16)
    return pl.pallas_call(
        functools.partial(slab_kernel, part),
        grid=(width // tile,),
        in_specs=[
            pl.BlockSpec((all_rows, width), whole),
            pl.BlockSpec((own, tile), column),
            pl.BlockSpec((all_rows, tile), column),
            pl.BlockSpec((all_rows, tile), column),
            pl.BlockSpec((own, width), whole),
            pl.BlockSpec((own, tile), column),
            pl.BlockSpec((devices, extra, tile), lambda i: (0, 0, i)),
        ],
        out_specs=[out, out],
        out_shape=[shape, shape],
        scratch_shapes=[
            pltpu.VMEM((width, all_rows), BF16),
            pltpu.VMEM((width, own), BF16),
            pltpu.VMEM((width, tile), F32),
        ],
        compiler_params=params(),
        cost_estimate=brief(),
        name="slabs",
    )(normed_all, query_grad, key_grad, value_grad, attended, branch_grad, tail)


def exchange(blocks):
    return lax.all_to_all(blocks, "exp", split_axis=0, concat_axis=0, tiled=True)


def body(
    tokens,
    w_query,
    w_key,
    w_value,
    w_out,
    w_router,
    gain_attn,
    gain_mlp,
    pos_bias,
    exp_gate,
    exp_up,
    exp_down,
    doc_lengths,
    bucket_of,
    expert_ids,
    cotangent,
):
    both = ("ctx", "exp")
    own_tokens = tokens[0]
    rows, width = own_tokens.shape
    experts = w_router.shape[1]
    capacity = (5 * TOP * rows + 4 * experts - 1) // (4 * experts)
    reach = (WINDOW + rows - 2) // rows
    scale = HEAD_DIM ** (-0.5)
    ctx_index, ctx_count = lax.axis_index("ctx"), lax.axis_size("ctx")
    exp_index = lax.axis_index("exp")
    part = w_query.shape[0]
    bias_part = pos_bias.shape[0]
    devices = width // part

    expert_range = jnp.arange(experts, dtype=jnp.int32)
    named = jnp.any(expert_ids[0][:, :, None] == expert_range, axis=1)
    named_low = named.astype(BF16)
    step = jnp.arange(rows, dtype=jnp.int32)
    earlier = (step[:, None] > step[None, :]).astype(BF16)
    slots = dot(earlier, named_low).astype(jnp.int32)
    slots = jnp.where(named, slots, -1).T
    routes = (slots[:, None, :] == jnp.arange(capacity, dtype=jnp.int32)[None, :, None]).astype(BF16)
    routes = routes.reshape(experts * capacity, rows)

    names = jnp.pad(named_low, ((0, 0), (0, LANES - experts)))
    early = dot(routes, jnp.concatenate([cotangent[0], names], axis=1)).astype(BF16)
    early = exchange(early.reshape(experts, capacity, width + LANES)).reshape(-1, width + LANES)

    held, share = exp_gate.shape[1], exp_down.shape[1]
    sizes = (share * 5 // 11, share * 6 // 11)
    packed, first = [], 0
    for size in sizes:
        columns = [slice(z * share + first, z * share + first + size) for z in range(ctx_count)]
        parts = [weight[0][:, at] for weight in (exp_gate, exp_up) for at in columns]
        packed.append(jnp.concatenate(parts + [pack_down(exp_down[0][first : first + size], held)], axis=1))
        first += size

    small = jnp.concatenate([w_router.reshape(-1), gain_attn, gain_mlp, pos_bias])
    small = jnp.pad(small, (0, width - small.shape[0]))[None]
    small = lax.all_gather(jnp.pad(small, ((0, 15), (0, 0))), both, axis=0)[:, 0]
    at = part * experts
    full_router = small[:, :at].reshape(width, experts)
    full_gain_attn = small[:, at : at + part].reshape(width).astype(F32)
    full_gain_mlp = small[:, at + part : at + 2 * part].reshape(width).astype(F32)
    table = small[:, at + 2 * part : at + 2 * part + bias_part].reshape(HEADS, BUCKETS)
    column = gather_ctx(jnp.concatenate([w_query, w_key, w_value, w_out], axis=0)[None])
    halo = [shift_ctx(own_tokens, 1), own_tokens]
    column, halo[0], early, packed[0] = together(column, halo[0], early, packed[0])
    for _ in range(1, reach):
        halo.insert(0, shift_ctx(halo[0], 1))
    onehot_bucket = (bucket_of[None, :] == jnp.arange(BUCKETS, dtype=jnp.int32)[:, None]).astype(BF16)
    band = make_band(dot(table, onehot_bucket))

    def then(others):
        *others, halo[0], packed[0] = together(*others, halo[0], packed[0])
        return others

    *halves, band = together(*spread_exp(column, then), band)
    chunk0 = lax.all_gather(packed[0], "ctx", axis=0, tiled=True)
    dense = spread_core(halves)
    full_query, full_key, full_value, full_out = (join_weights(dense, i * part, part) for i in range(4))
    tokens_all = jnp.concatenate(halo, axis=0)
    inputs_all = tokens_all.astype(F32)
    inputs = own_tokens.astype(F32)

    ends = jnp.cumsum(doc_lengths[0])

    def documents(positions):
        return jnp.sum((positions[:, None] >= ends[None, :]).astype(jnp.int32), axis=1)[:, None]

    feature = (jnp.arange(2 * HEAD_DIM, dtype=jnp.int32) % HEAD_DIM)[None, :]
    docs = doc_lengths.shape[1] + 1
    query_pos = ctx_index * rows + step
    key_pos = (ctx_index - reach) * rows + jnp.arange((reach + 1) * rows, dtype=jnp.int32)
    query_doc = (feature == documents(query_pos)).astype(BF16)
    same = (feature == documents(key_pos)) & (key_pos[:, None] >= 0)
    key_doc = jnp.where(same | (feature >= docs), 0.0, NEGATIVE).astype(BF16)

    normed_all = norm_rows(inputs_all, full_gain_attn).astype(BF16)
    normed = normed_all[reach * rows :]
    queries = (dot(normed, full_query).astype(BF16)) * jnp.asarray(scale, BF16)
    keys = dot(normed_all, full_key).astype(BF16)
    values = dot(normed_all, full_value).astype(BF16)
    attended, lse = attend(queries, keys, values, query_doc, key_doc, band)
    middle = inputs + dot(attended, full_out)
    normed_mlp = norm_rows(middle, full_gain_mlp).astype(BF16)

    sent = dot(routes, normed_mlp).astype(BF16)
    arrived = exchange(sent.reshape(experts, capacity, width)).reshape(-1, width)
    router_turned = jnp.pad(full_router.T, ((0, LANES - experts), (0, 0)))
    extras = (early, router_turned)
    units0, units1 = (size * ctx_count for size in sizes)
    arrived, packed[1], chunk0 = together(arrived, packed[1], chunk0)
    up, down = gather_hop(packed[1], packed[1], 1)
    hidden, dboth, carried, _ = run_expert(True, False, units0, ctx_count, arrived, [chunk0], extras, None)
    grad0 = expert_weights(units0, ctx_count, arrived, carried[0], dboth, hidden)
    pieces, sent = [packed[1]], (None, None)
    probs = make_probs(queries, keys, query_doc, key_doc, band, lse)
    for hop in range(1, ctx_count):
        if hop == 1:
            up, down, grad0 = together(up, down, grad0)
            parts0 = grad0.reshape(ctx_count, held, -1)
        else:
            up, down = gather_hop(up, down, hop)
            sent = scatter_hop(*scatter_add(parts0, hop - 1, *sent), hop - 1)
            up, down, probs, *sent = together(up, down, probs, *sent)
        pieces += [up, down]
    arrived, *sent = together(arrived, *scatter_add(parts0, ctx_count - 1, *sent))
    sent = scatter_hop(*sent, ctx_count - 1)
    hidden, dboth, carried, router_grad = run_expert(
        False, True, units1, ctx_count, arrived, pieces, extras, carried
    )
    low, made, back, _ = carried
    hidden, dboth, low, made, back, *sent = together(hidden, dboth, low, made, back, *sent)
    grad1 = expert_weights(units1, ctx_count, arrived, low, dboth, hidden, True)
    total1 = lax.psum_scatter(grad1, "ctx", scatter_dimension=0, tiled=True)
    back = exchange(back.reshape(experts, capacity, width)).reshape(-1, width)

    upstream = cotangent[0].astype(F32)
    normed_mlp_grad = dot_rows(routes, back)
    _, second_pull = jax.vjp(norm_rows, middle, full_gain_mlp)
    middle_norm_grad, gain_mlp_grad = second_pull(normed_mlp_grad)
    middle_grad = upstream + middle_norm_grad
    branch_grad = middle_grad.astype(BF16)
    attended_grad = dot_last(branch_grad, full_out).astype(BF16)
    made, attended_grad = together(made, attended_grad)
    made = exchange(made.reshape(experts, capacity, width)).reshape(-1, width)
    query_grad, key_grad, value_grad, dist_grad = attend_back(
        queries, keys, values, attended_grad, attended, probs
    )
    bias_grad = jnp.dot(
        dist_grad.reshape(HEADS, WINDOW), onehot_bucket.T.astype(F32), precision=lax.Precision.HIGHEST
    )

    halo_grad, own_grad, gain_attn_grad = normed_grad_of(
        tokens_all, query_grad, key_grad, value_grad, full_query, full_key, full_value
    )
    gain_attn_grad = jnp.sum(gain_attn_grad, axis=0)

    tail = jnp.concatenate(
        [
            router_grad[:, :experts].reshape(devices, -1),
            gain_attn_grad.reshape(devices, part),
            gain_mlp_grad.reshape(devices, part),
            bias_grad.reshape(devices, bias_part),
        ],
        axis=1,
    ).astype(BF16)
    tail = jnp.pad(tail[:, None, :], ((0, 0), (0, 15), (0, width - tail.shape[1])))
    query_grad, made = together(query_grad, made)
    output = (middle + dot_rows(routes, made)).astype(BF16)
    keep, send = make_slabs(normed_all, query_grad, key_grad, value_grad, attended, branch_grad, tail)
    other = swap_exp(send, 1)
    parts = scatter_exp(keep, other)
    pieces = [halo_grad[place * rows : (place + 1) * rows] for place in range(reach)]
    returning = shift_ctx(pieces[0], -1)
    for piece in pieces[1:]:
        parts, returning = together(parts, returning)
        returning = shift_ctx((piece.astype(F32) + returning.astype(F32)).astype(BF16), -1)
    own0 = lax.dynamic_index_in_dim(parts0, ctx_index, 0, keepdims=False)
    expert_grads = expert_sums(sizes, ctx_count, own0, *sent, total1)
    sent = (None, None)
    for hop in range(1, ctx_count):
        sent = scatter_add(parts, hop, *sent)
        sent = scatter_hop(*sent, hop)
        if hop == 1:
            *sent, grad_gate, grad_up, grad_down = together(*sent, *expert_grads)
    sums = scatter_end(parts, *sent)
    _, own_pull = jax.vjp(norm_rows, inputs, full_gain_attn)
    input_grad = middle_grad + own_pull(own_grad + returning.astype(F32))[0]
    tail = sums[4 * part]
    at = part * experts
    return (
        output[None],
        input_grad[None],
        sums[:part],
        sums[part : 2 * part],
        sums[2 * part : 3 * part],
        sums[3 * part : 4 * part],
        tail[:at].reshape(part, experts),
        tail[at : at + part],
        tail[at + part : at + 2 * part],
        tail[at + 2 * part : at + 2 * part + bias_part],
        grad_gate[None],
        grad_up[None],
        grad_down[None],
    )


def solution(mesh):
    rows3 = P("exp", "ctx", None)
    dense2 = P(("ctx", "exp"), None)
    dense1 = P(("ctx", "exp"))
    return jax.shard_map(
        body,
        mesh=mesh,
        in_specs=(
            rows3,
            dense2,
            dense2,
            dense2,
            dense2,
            dense2,
            dense1,
            dense1,
            dense1,
            rows3,
            rows3,
            rows3,
            P("exp", None),
            P(),
            rows3,
            rows3,
        ),
        out_specs=(
            rows3,
            rows3,
            dense2,
            dense2,
            dense2,
            dense2,
            dense2,
            dense1,
            dense1,
            dense1,
            rows3,
            rows3,
            rows3,
        ),
        check_vma=False,
    )
```

```python
import functools

import jax
import jax.numpy as jnp
from jax import lax
from jax.experimental import pallas as pl
from jax.experimental.pallas import tpu as pltpu
from jax.sharding import PartitionSpec as P

HEADS = 16
HEAD_DIM = 64
BUCKETS = 32
TOP = 2
WINDOW = 1024

EPSILON = 1e-06
NEGATIVE = -1e30
LANES = 128
CHUNK = 256
FF_TILE = 512
ROW_TILE = 256
VMEM_LIMIT = 58 * 2**20
BF16 = jnp.bfloat16
F32 = jnp.float32


def shift_ctx(block, distance):
    devices = range(lax.axis_size("ctx"))
    route = [(i - distance, i) for i in devices if i - distance in devices]
    return lax.ppermute(block, "ctx", route)


def norm_rows(values, gain):
    return values * lax.rsqrt(jnp.mean(values * values, axis=-1, keepdims=True) + EPSILON) * gain


def dot(left, right):
    return jnp.dot(left, right, preferred_element_type=F32)


def dot_rows(left, right):
    return lax.dot_general(left, right, (((0,), (0,)), ((), ())), preferred_element_type=F32)


def dot_last(left, right):
    return lax.dot_general(left, right, (((1,), (1,)), ((), ())), preferred_element_type=F32)


def params(**more):
    return pltpu.CompilerParams(vmem_limit_bytes=VMEM_LIMIT, **more)


def brief():
    return pl.CostEstimate(flops=2**20, bytes_accessed=2**20, transcendentals=0)


def band_kernel(bias_ref, band_ref):
    blocks = WINDOW // LANES
    size = (blocks + 2) * LANES
    for head in range(bias_ref.shape[0]):
        row = jnp.broadcast_to(bias_ref[head : head + 1, :], (8, size))
        eight = pltpu.roll(row, 0, 1, stride=1, stride_axis=0)
        for group in range(LANES // 8):
            wide = pltpu.roll(eight, 8 * group, 1) if group else eight
            for a in range(blocks + 1):
                first = a * LANES + group * 8
                at = (blocks + 1 - a) * LANES
                band_ref[head, first : first + 8, :] = wide[:, at : at + LANES]


def make_band(bias_dist):
    group = 8
    edge = jnp.full((HEADS, LANES), NEGATIVE, F32)
    padded = jnp.concatenate([edge, bias_dist, edge], axis=1)
    return pl.pallas_call(
        band_kernel,
        grid=(HEADS // group,),
        in_specs=[pl.BlockSpec((group, WINDOW + 2 * LANES), lambda h: (h, 0))],
        out_specs=pl.BlockSpec((group, WINDOW + LANES, LANES), lambda h: (h, 0, 0)),
        out_shape=jax.ShapeDtypeStruct((HEADS, WINDOW + LANES, LANES), F32),
        compiler_params=params(),
        cost_estimate=brief(),
        name="bias_band",
    )(padded)


def sum_band(band_ref):
    blocks = WINDOW // LANES
    size = (blocks + 2) * LANES
    row = lax.broadcasted_iota(jnp.int32, (8, 1), 0)
    edge = jnp.zeros((8, LANES), F32)
    total = None
    for group in range(LANES // 8):
        pieces = [edge]
        for a in range(blocks, -1, -1):
            first = a * LANES + group * 8
            pieces.append(band_ref[first : first + 8, :])
        wide = jnp.concatenate(pieces, axis=1)
        if group:
            wide = pltpu.roll(wide, size - 8 * group, 1)
        total = wide if total is None else total + wide
    dist = jnp.zeros_like(total)
    for r in range(8):
        turned = pltpu.roll(total, size - r, 1) if r else total
        dist = dist + jnp.where(row == r, turned, 0.0)
    return jnp.sum(dist, axis=0, keepdims=True)[:, LANES : LANES + WINDOW]


def head_lanes(head):
    lane = lax.broadcasted_iota(jnp.int32, (1, 2 * HEAD_DIM), 1)
    return (lane >= head * HEAD_DIM) & (lane < (head + 1) * HEAD_DIM)


def masked_scores(head, start, q_ref, k_ref, qdoc_ref, kdoc_ref):
    span = WINDOW + CHUNK
    mine = head_lanes(head)
    q_rows, k_rows = pl.ds(start, CHUNK), pl.ds(start, span)
    q_part = jnp.where(mine, q_ref[q_rows, :], qdoc_ref[q_rows, :])
    k_part = jnp.where(mine, k_ref[k_rows, :], kdoc_ref[k_rows, :])
    return dot_last(k_part, q_part)


def sub_blocks():
    return [(s * LANES, WINDOW + LANES) for s in range(CHUNK // LANES)]


def spread(parts):
    span = WINDOW + CHUNK
    columns = []
    for (first, rows), part in zip(sub_blocks(), parts):
        pieces = []
        if first:
            pieces.append(jnp.zeros((first, LANES), part.dtype))
        pieces.append(part)
        if span - first - rows:
            pieces.append(jnp.zeros((span - first - rows, LANES), part.dtype))
        columns.append(jnp.concatenate(pieces, axis=0) if len(pieces) > 1 else part)
    return jnp.concatenate(columns, axis=1)


def attend_kernel(q_ref, k_ref, v_ref, qdoc_ref, kdoc_ref, band_ref, o_ref, lse_ref):
    span = WINDOW + CHUNK
    for start in range(0, q_ref.shape[0], CHUNK):
        v_turned = v_ref[pl.ds(start, span), :].T
        outs = []
        for head in range(2):
            scores = masked_scores(head, start, q_ref, k_ref, qdoc_ref, kdoc_ref)
            band = band_ref[head]
            low, scale, logs = [], [], []
            for s, (first, rows) in enumerate(sub_blocks()):
                part = scores[first : first + rows, s * LANES : (s + 1) * LANES] + band
                top = jnp.max(part, axis=0, keepdims=True)
                expo = jnp.exp(part - top)
                total = jnp.sum(expo, axis=0, keepdims=True)
                low.append(expo.astype(BF16))
                scale.append(1.0 / total)
                logs.append(top + jnp.log(total))
            out = dot(v_turned[head * HEAD_DIM : (head + 1) * HEAD_DIM], spread(low))
            outs.append(out * jnp.concatenate(scale, axis=1))
            lse_ref[0, head : head + 1, pl.ds(start, CHUNK)] = jnp.concatenate(logs, axis=1)
        o_ref[pl.ds(start, CHUNK), :] = jnp.concatenate(outs, axis=0).T.astype(BF16)


def attend(queries, keys, values, query_doc, key_doc, band):
    rows, width = queries.shape
    keys_rows = keys.shape[0]
    pairs = HEADS // 2
    wide = 2 * HEAD_DIM
    return pl.pallas_call(
        attend_kernel,
        grid=(pairs,),
        in_specs=[
            pl.BlockSpec((rows, wide), lambda p: (0, p)),
            pl.BlockSpec((keys_rows, wide), lambda p: (0, p)),
            pl.BlockSpec((keys_rows, wide), lambda p: (0, p)),
            pl.BlockSpec((rows, wide), lambda p: (0, 0)),
            pl.BlockSpec((keys_rows, wide), lambda p: (0, 0)),
            pl.BlockSpec((2, WINDOW + LANES, LANES), lambda p: (p, 0, 0)),
        ],
        out_specs=[
            pl.BlockSpec((rows, wide), lambda p: (0, p)),
            pl.BlockSpec((1, 2, rows), lambda p: (p, 0, 0)),
        ],
        out_shape=[
            jax.ShapeDtypeStruct((rows, width), BF16),
            jax.ShapeDtypeStruct((pairs, 2, rows), F32),
        ],
        compiler_params=params(),
        cost_estimate=brief(),
        name="attend",
    )(queries, keys, values, query_doc, key_doc, band)


def probs_kernel(q_ref, k_ref, qdoc_ref, kdoc_ref, band_ref, lse_ref, probs_ref):
    for chunk in range(q_ref.shape[0] // CHUNK):
        start = chunk * CHUNK
        for head in range(2):
            scores = masked_scores(head, start, q_ref, k_ref, qdoc_ref, kdoc_ref)
            band = band_ref[head]
            lse = lse_ref[0, head : head + 1, pl.ds(start, CHUNK)]
            parts = []
            for s, (first, rows) in enumerate(sub_blocks()):
                lanes = slice(s * LANES, (s + 1) * LANES)
                parts.append(jnp.exp(scores[first : first + rows, lanes] + band - lse[:, lanes]).astype(BF16))
            probs_ref[head, chunk] = spread(parts)


def make_probs(queries, keys, query_doc, key_doc, band, lse):
    rows, width = queries.shape
    keys_rows = keys.shape[0]
    pairs = HEADS // 2
    wide = 2 * HEAD_DIM
    span, chunks = WINDOW + CHUNK, rows // CHUNK
    return pl.pallas_call(
        probs_kernel,
        grid=(pairs,),
        in_specs=[
            pl.BlockSpec((rows, wide), lambda p: (0, p)),
            pl.BlockSpec((keys_rows, wide), lambda p: (0, p)),
            pl.BlockSpec((rows, wide), lambda p: (0, 0)),
            pl.BlockSpec((keys_rows, wide), lambda p: (0, 0)),
            pl.BlockSpec((2, WINDOW + LANES, LANES), lambda p: (p, 0, 0)),
            pl.BlockSpec((1, 2, rows), lambda p: (p, 0, 0)),
        ],
        out_specs=pl.BlockSpec((2, chunks, span, CHUNK), lambda p: (p, 0, 0, 0)),
        out_shape=jax.ShapeDtypeStruct((HEADS, chunks, span, CHUNK), BF16),
        compiler_params=params(),
        cost_estimate=brief(),
        name="probs",
    )(queries, keys, query_doc, key_doc, band, lse)


def attend_back_kernel(
    q_ref, k_ref, v_ref, g_ref, o_ref, probs_ref, dq_ref, dk_ref, dv_ref, dist_ref, dk_sum, dv_sum, dband
):
    span = WINDOW + CHUNK
    dk_sum[...] = jnp.zeros_like(dk_sum)
    dv_sum[...] = jnp.zeros_like(dv_sum)
    for chunk in range(q_ref.shape[0] // CHUNK):
        start = chunk * CHUNK
        q_rows, k_rows = pl.ds(start, CHUNK), pl.ds(start, span)
        k_turned = k_ref[k_rows, :].T
        product = (g_ref[q_rows, :].astype(F32) * o_ref[q_rows, :].astype(F32)).T
        dq_parts = []
        for head in range(2):
            mine = head_lanes(head)
            zero = jnp.zeros((), BF16)
            g_part = jnp.where(mine, g_ref[q_rows, :], zero)
            q_part = jnp.where(mine, q_ref[q_rows, :], zero)
            prob_grad = dot_last(v_ref[k_rows, :], g_part)
            delta = jnp.sum(product[head * HEAD_DIM : (head + 1) * HEAD_DIM], axis=0, keepdims=True)
            grad_low, grad_sum = [], None
            for s, (first, rows) in enumerate(sub_blocks()):
                lanes = slice(s * LANES, (s + 1) * LANES)
                probs = probs_ref[head, chunk, first : first + rows, lanes].astype(F32)
                grad = probs * (prob_grad[first : first + rows, lanes] - delta[:, lanes])
                grad_low.append(grad.astype(BF16))
                grad_sum = grad if grad_sum is None else grad_sum + grad
            if chunk == 0:
                dband[head] = grad_sum
            else:
                dband[head] = dband[head] + grad_sum
            grads = spread(grad_low)
            dk_sum[k_rows, :] += dot(grads, q_part)
            dv_sum[k_rows, :] += dot(probs_ref[head, chunk], g_part)
            dq_parts.append(dot(k_turned[head * HEAD_DIM : (head + 1) * HEAD_DIM], grads))
        turned = jnp.concatenate(dq_parts, axis=0).T
        dq_ref[q_rows, :] = (turned * HEAD_DIM ** (-0.5)).astype(BF16)
    dk_ref[...] = dk_sum[...].astype(BF16)
    dv_ref[...] = dv_sum[...].astype(BF16)
    for head in range(2):
        dist_ref[0, head : head + 1, :] = sum_band(dband.at[head])


def attend_back(queries, keys, values, grad, out, probs):
    rows, width = queries.shape
    keys_rows = keys.shape[0]
    pairs = HEADS // 2
    wide = 2 * HEAD_DIM
    q_spec = pl.BlockSpec((rows, wide), lambda p: (0, p))
    k_spec = pl.BlockSpec((keys_rows, wide), lambda p: (0, p))
    return pl.pallas_call(
        attend_back_kernel,
        grid=(pairs,),
        in_specs=[
            q_spec,
            k_spec,
            k_spec,
            q_spec,
            q_spec,
            pl.BlockSpec((2,) + probs.shape[1:], lambda p: (p, 0, 0, 0)),
        ],
        out_specs=[q_spec, k_spec, k_spec, pl.BlockSpec((1, 2, WINDOW), lambda p: (p, 0, 0))],
        out_shape=[
            jax.ShapeDtypeStruct((rows, width), BF16),
            jax.ShapeDtypeStruct((keys_rows, width), BF16),
            jax.ShapeDtypeStruct((keys_rows, width), BF16),
            jax.ShapeDtypeStruct((pairs, 2, WINDOW), F32),
        ],
        scratch_shapes=[
            pltpu.VMEM((keys_rows, wide), F32),
            pltpu.VMEM((keys_rows, wide), F32),
            pltpu.VMEM((2, WINDOW + LANES, LANES), F32),
        ],
        compiler_params=params(),
        cost_estimate=pl.CostEstimate(
            flops=20 * rows * WINDOW * width * 2, bytes_accessed=2**20, transcendentals=0
        ),
        name="attend_back",
    )(queries, keys, values, grad, out, probs)


def down_blocks(units, width, count):
    held, share = width // count, units // count
    extra = share - held
    wide = width * extra // held
    blocks = []
    for z in range(count):
        blocks.append(((z * held, 0), (z * share, 0), (held, width)))
        for m in range(held // extra):
            blocks.append(((z * held + m * extra, width), (z * share + held, m * wide), (extra, wide)))
    return blocks


def pack_down(down, held):
    extra, width = down.shape[0] - held, down.shape[1]
    wide = width * extra // held
    rest = [down[held:, m * wide : (m + 1) * wide] for m in range(held // extra)]
    return jnp.concatenate([down[:held], jnp.concatenate(rest, axis=0)], axis=1)


def unpack_down(packed, size, width):
    held = packed.shape[0]
    extra = size - held
    rest = [packed[m * extra : (m + 1) * extra, width:] for m in range(held // extra)]
    return jnp.concatenate([packed[:, :width], jnp.concatenate(rest, axis=1)], axis=0)


def expert_kernel(first, last, units, count, parts, *refs):
    refs = list(refs)
    take = lambda: refs.pop(0)
    x_ref = take()
    pieces = [take() for _ in range(parts)]
    if first or last:
        c_ref, names_ref, router_ref = take(), take(), take()
    if not first:
        low_ref, made_in, back_in = take(), take(), take()
    if last and not first:
        gate_in = take()
    hidden_ref, dboth_ref = take(), take()
    if first:
        low_out = take()
    if first and not last:
        gate_out = take()
    made_ref, back_ref = take(), take()
    if last:
        drouter_ref = take()
    chunk_ref, down_s, sems = take(), take(), take()
    rows, width = x_ref.shape
    held = width // count
    index = lax.axis_index("ctx")

    def slot(z):
        return chunk_ref.at[z * held : (z + 1) * held]

    @pl.when(pl.program_id(0) == 0)
    def _():
        if parts == 1:
            for z in range(count):
                pltpu.make_async_copy(pieces[0].at[z * held : (z + 1) * held], slot(z), sems.at[z]).start()
        for z in range(count if parts > 1 else 0):
            for here in range(count):
                hop = abs(here - z)
                source = pieces[0 if hop == 0 else 2 * hop - 1 if z < here else 2 * hop]

                @pl.when(index == here)
                def _(source=source, z=z):
                    pltpu.make_async_copy(source, slot(z), sems.at[z]).start()

        for z in range(count):
            pltpu.make_async_copy(pieces[0].at[:held], slot(z), sems.at[z]).wait()

    x = x_ref[...]
    own = lax.broadcasted_iota(jnp.int32, (1, LANES), 1) == lax.axis_index("exp")
    if first:
        names = names_ref[...].astype(F32)
        logits = dot_last(x, router_ref[...]) * names
        mine = jnp.sum(jnp.where(own, logits, 0.0), axis=1, keepdims=True)
        theirs = jnp.sum(jnp.where(own, 0.0, logits), axis=1, keepdims=True)
        gate = jax.nn.sigmoid(mine - theirs)
        low_out[...] = (gate * c_ref[...].astype(F32)).astype(BF16)
        if not last:
            gate_out[...] = jnp.broadcast_to(gate, (rows, LANES))
        low_ref = low_out
    elif last:
        gate = gate_in[...][:, :1]
    @pl.when(pl.program_id(0) == 0)
    def _():
        for (row, column), (to_row, to_column), (high, wide) in down_blocks(units, width, count):
            from_columns = slice(2 * units + column, 2 * units + column + wide)
            down_s[to_row : to_row + high, to_column : to_column + wide] = chunk_ref[row : row + high, from_columns]

    for start in range(0, units, FF_TILE):
        stop = min(start + FF_TILE, units)
        at, up_at = slice(start, stop), slice(units + start, units + stop)
        gate_pre = dot(x, chunk_ref[:, at])
        up_pre = dot(x, chunk_ref[:, up_at])
        hidden_grad = dot_last(low_ref[...], down_s[at, :])
        root = 0.7978845608028654
        square = gate_pre * gate_pre
        bent = jnp.tanh(gate_pre * (root + root * 0.044715 * square))
        half = 0.5 * (1.0 + bent)
        act = gate_pre * half
        slope = half + 0.5 * gate_pre * (1.0 - bent * bent) * (root + 3.0 * root * 0.044715 * square)
        hidden_ref[:, at] = (act * up_pre).astype(BF16)
        dboth_ref[:, at] = (hidden_grad * up_pre * slope).astype(BF16)
        dboth_ref[:, up_at] = (hidden_grad * act).astype(BF16)
    made = dot(hidden_ref[...], down_s[...])
    back = dot_last(dboth_ref[...], chunk_ref[:, : 2 * units])
    if not first:
        made = made + made_in[...]
        back = back + back_in[...]
    if last:
        made = made.astype(BF16).astype(F32)
        names = names_ref[...].astype(F32)
        push = jnp.sum(c_ref[...].astype(F32) * made, axis=1, keepdims=True)
        push = push * gate * (1.0 - gate)
        logits_grad = push * jnp.where(own, names, -names)
        high = logits_grad.astype(BF16)
        low = (logits_grad - high.astype(F32)).astype(BF16)
        made = gate * made
        back = back + dot(high, router_ref[...]) + dot(low, router_ref[...])
        turned = x.T
        update = dot(turned, high) + dot(turned, low)

        @pl.when(pl.program_id(0) == 0)
        def _():
            drouter_ref[...] = update

        @pl.when(pl.program_id(0) > 0)
        def _():
            drouter_ref[...] += update

    made_ref[...] = made.astype(made_ref.dtype)
    back_ref[...] = back.astype(back_ref.dtype)


def run_expert(first, last, units, count, x, pieces, extras, carried):
    rows, width = x.shape
    whole = lambda i: (0, 0)
    step = lambda i: (i, 0)
    wide = pl.BlockSpec((ROW_TILE, width), step)
    thin = pl.BlockSpec((ROW_TILE, LANES), step)
    struct = jax.ShapeDtypeStruct
    early, router = extras
    operands = [x] + pieces
    in_specs = [wide] + [pl.BlockSpec(memory_space=pl.ANY)] * len(pieces)
    if first or last:
        operands += [early, early, router]
        names = pl.BlockSpec((ROW_TILE, LANES), lambda i: (i, width // LANES))
        in_specs += [wide, names, pl.BlockSpec((LANES, width), whole)]
    if not first:
        low, made, back, gate = carried
        operands += [low, made, back]
        in_specs += [wide, wide, wide]
        if last:
            operands.append(gate)
            in_specs.append(thin)
    out_shape = [struct((rows, units), BF16), struct((rows, 2 * units), BF16)]
    out_specs = [pl.BlockSpec((ROW_TILE, units), step), pl.BlockSpec((ROW_TILE, 2 * units), step)]
    if first:
        out_shape.append(struct((rows, width), BF16))
        out_specs.append(wide)
        if not last:
            out_shape.append(struct((rows, LANES), F32))
            out_specs.append(thin)
    kept = BF16 if last else F32
    out_shape += [struct((rows, width), kept), struct((rows, width), kept)]
    out_specs += [wide, wide]
    if last:
        out_shape.append(struct((width, LANES), F32))
        out_specs.append(pl.BlockSpec((width, LANES), whole))
    outs = list(
        pl.pallas_call(
            functools.partial(expert_kernel, first, last, units, count, len(pieces)),
            grid=(rows // ROW_TILE,),
            in_specs=in_specs,
            out_specs=out_specs,
            out_shape=out_shape,
            scratch_shapes=[
                pltpu.VMEM((width, pieces[0].shape[1]), BF16),
                pltpu.VMEM((units, width), BF16),
                pltpu.SemaphoreType.DMA((count,)),
            ],
            compiler_params=params(),
            cost_estimate=brief(),
            name="expert",
        )(*operands)
    )
    hidden, dboth = outs[:2]
    if first:
        low = outs[2]
        gate = None if last else outs[3]
    if last:
        made, back, drouter = outs[-3:]
        return hidden, dboth, (low, made, back, gate), drouter
    made, back = outs[-2:]
    return hidden, dboth, (low, made, back, gate), None


def expert_weights_kernel(
    units, count, x_ref, low_ref, dboth_ref, hidden_ref, grad_ref, x_turned, hidden_turned, rest
):
    step = pl.program_id(0)
    tile = low_ref.shape[1]
    width = x_ref.shape[1]
    both_steps, down_steps = 2 * units // tile, width // tile

    @pl.when(step == 0)
    def _():
        x_turned[...] = x_ref[...].T

    @pl.when(step < both_steps)
    def _():
        grad_ref[...] = dot(x_turned[...], dboth_ref[...]).astype(BF16)

    @pl.when(step == both_steps)
    def _():
        hidden_turned[...] = hidden_ref[...].T

    for place in range(down_steps):

        @pl.when(step == both_steps + place)
        def _(place=place):
            total = dot(hidden_turned[...], low_ref[...]).astype(BF16)
            first = place * tile
            for (row, column), (from_row, from_column), (high, wide) in down_blocks(units, width, count):
                if column == 0:
                    grad_ref[row : row + high, :] = total[from_row : from_row + high]
                    continue
                low, top = max(first, from_column), min(first + tile, from_column + wide)
                if low < top:
                    rest[row : row + high, low - from_column : top - from_column] = total[
                        from_row : from_row + high, low - first : top - first
                    ]

    for place in range(rest.shape[1] // tile):

        @pl.when(step == both_steps + down_steps + place)
        def _(place=place):
            grad_ref[...] = rest[:, place * tile : (place + 1) * tile]


def expert_weights(units, count, x, low, dboth, hidden, long=False):
    rows, width = x.shape
    tile = 512
    extra_steps = -(-(units - width) // tile)
    both_steps, down_steps = 2 * units // tile, width // tile
    whole = lambda i: (0, 0)
    work = pl.CostEstimate(flops=6 * rows * width * units, bytes_accessed=2**20, transcendentals=0)
    return pl.pallas_call(
        functools.partial(expert_weights_kernel, units, count),
        grid=(both_steps + down_steps + extra_steps,),
        in_specs=[
            pl.BlockSpec((rows, width), whole),
            pl.BlockSpec((rows, tile), lambda i: (0, jnp.clip(i - both_steps, 0, down_steps - 1))),
            pl.BlockSpec((rows, tile), lambda i: (0, jnp.minimum(i, both_steps - 1))),
            pl.BlockSpec((rows, units), whole),
        ],
        out_specs=pl.BlockSpec((width, tile), lambda i: (0, i)),
        out_shape=jax.ShapeDtypeStruct((width, 3 * units), BF16),
        scratch_shapes=[
            pltpu.VMEM((width, rows), BF16),
            pltpu.VMEM((units, rows), BF16),
            pltpu.VMEM((width, extra_steps * tile), BF16),
        ],
        compiler_params=params(),
        cost_estimate=work if long else brief(),
        name="expert_weights",
    )(x, low, dboth, hidden)


def expert_sums_kernel(sizes, count, own_ref, up_ref, down_ref, last_ref, gate_out, up_out, down_out):
    held, width = own_ref.shape[0], down_out.shape[1]
    extras = [size - held for size in sizes]
    tile = min(extras)
    for first in range(0, held, tile):
        rows = slice(first, first + tile)
        totals = (
            own_ref[rows, :].astype(F32) + up_ref[rows, :].astype(F32) + down_ref[rows, :].astype(F32),
            last_ref[rows, :].astype(F32),
        )
        for out, part in ((gate_out, 0), (up_out, 1)):
            pieces = []
            for z in range(count):
                for size, total in zip(sizes, totals):
                    at = part * size * count + z * size
                    pieces.append(total[:, at : at + size])
            out[rows, :] = jnp.concatenate(pieces, axis=1)
        start = 0
        for size, extra, total in zip(sizes, extras, totals):
            wide = width * extra // held
            at = 2 * size * count
            down_out[start + first : start + first + tile, :] = total[:, at : at + width]
            to, columns = start + held + first % extra, first // extra * wide
            down_out[to : to + tile, columns : columns + wide] = total[:, at + width :]
            start += size


def expert_sums(sizes, count, own, up, down, last):
    held = own.shape[0]
    units = sum(sizes)
    struct = jax.ShapeDtypeStruct
    width = held * count
    return pl.pallas_call(
        functools.partial(expert_sums_kernel, sizes, count),
        in_specs=[pl.BlockSpec(memory_space=pltpu.VMEM)] * 4,
        out_specs=[pl.BlockSpec(memory_space=pltpu.VMEM)] * 3,
        out_shape=[
            struct((held, units * count), F32),
            struct((held, units * count), F32),
            struct((units, width), F32),
        ],
        compiler_params=params(),
        cost_estimate=brief(),
        name="expert_sums",
    )(own, up, down, last)


def ctx_moves(distance):
    devices = range(lax.axis_size("ctx"))
    return [(i - distance, i) for i in devices if i - distance in devices]


def together(*values):
    return lax.optimization_barrier(values)


def gather_ctx(piece):
    count, index, size = lax.axis_size("ctx"), lax.axis_index("ctx"), piece.shape[0]
    full = jnp.zeros((count * size,) + piece.shape[1:], piece.dtype)
    place = lambda buffer, part, at: lax.dynamic_update_slice_in_dim(buffer, part, at * size, 0)
    full = place(full, piece, index)
    up = down = piece
    for hop in range(1, count):
        up, down = shift_ctx(up, 1), shift_ctx(down, -1)
        for part, at, held in ((up, index - hop, index >= hop), (down, index + hop, index + hop < count)):
            at = jnp.clip(at, 0, count - 1)
            old = lax.dynamic_slice_in_dim(full, at * size, size, 0)
            full = place(full, jnp.where(held, part, old), at)
    return full


def gather_hop(up, down, hop):
    count = lax.axis_size("ctx")
    route = [(i, i + 1) for i in range(hop - 1, count - 1)]
    back = [(count - 1 - i, count - 1 - j) for i, j in route]
    return lax.ppermute(up, "ctx", route), lax.ppermute(down, "ctx", back)


def scatter_add(parts, hop, up=None, down=None):
    count, index = lax.axis_size("ctx"), lax.axis_index("ctx")

    def part(at):
        return lax.dynamic_index_in_dim(parts, jnp.clip(at, 0, count - 1), 0, keepdims=False).astype(F32)

    distance = count - hop
    if hop == 1:
        return parts[count - 1].astype(BF16), parts[0].astype(BF16)
    mine_up, mine_down = part(index + distance), part(index - distance)
    if up is not None:
        mine_up, mine_down = mine_up + up.astype(F32), mine_down + down.astype(F32)
    return mine_up.astype(BF16), mine_down.astype(BF16)


def scatter_hop(up, down, hop):
    count = lax.axis_size("ctx")
    route = [(i, i + 1) for i in range(hop)]
    back = [(count - 1 - i, count - 1 - j) for i, j in route]
    return lax.ppermute(up, "ctx", route), lax.ppermute(down, "ctx", back)


def scatter_end(parts, up, down):
    own = lax.dynamic_index_in_dim(parts, lax.axis_index("ctx"), 0, keepdims=False).astype(F32)
    return own + up.astype(F32) + down.astype(F32)


def swap_exp(block, bit):
    return lax.ppermute(block, "exp", [(i, i ^ bit) for i in range(lax.axis_size("exp"))])


def bit_set(bit):
    return (lax.axis_index("exp") // bit) % 2 == 1


def exp_bits():
    size, bits = lax.axis_size("exp"), []
    while 1 << len(bits) < size:
        bits.append(1 << len(bits))
    return bits


def routes_exp():
    bits = exp_bits()
    return bits[1:], bits[:0:-1]


def spread_exp(column, then):
    count = column.shape[0]
    halves = [column[None, : count // 2], column[None, count // 2 :]]
    for step, bits in enumerate(zip(*routes_exp())):
        others = [swap_exp(half, bit) for half, bit in zip(halves, bits)]
        if step == 0:
            others = then(others)
        for place, (half, other, bit) in enumerate(zip(halves, others, bits)):
            halves[place] = jnp.where(
                bit_set(bit), jnp.concatenate([other, half]), jnp.concatenate([half, other])
            )
    return halves


def spread_core(halves):
    bits = exp_bits()
    done = []
    for half, order in zip(halves, routes_exp()):
        other = swap_exp(half, 1)
        mine_first = bit_set(1)
        pair = jnp.stack([jnp.where(mine_first, other, half), jnp.where(mine_first, half, other)])
        pair = pair.reshape((2,) + (2,) * len(order) + half.shape[1:])
        axes = [1 + order[::-1].index(bit) for bit in bits[:0:-1]] + [0]
        axes = [len(axes)] + axes + list(range(len(axes) + 1, pair.ndim))
        pair = pair.transpose(axes)
        done.append(pair.reshape((half.shape[1], 1 << len(bits)) + half.shape[2:]))
    return done


def join_weights(done, first, rows):
    width = done[0].shape[-1]
    return jnp.concatenate([half[:, :, first : first + rows].reshape(-1, width) for half in done])


def scatter_exp(keep, other):
    count, bits = lax.axis_size("ctx"), exp_bits()
    chip = (keep.astype(F32) + other.astype(F32)).astype(BF16)
    chip = chip.reshape((count, -1) + chip.shape[1:])
    sums = []
    for half, order in zip((chip[: count // 2], chip[count // 2 :]), routes_exp()):
        half = half.reshape((count // 2,) + (2,) * (len(bits) - 1) + half.shape[2:])
        left = bits[:0:-1]
        for bit in order:
            axis = 1 + left.index(bit)
            low = lax.index_in_dim(half, 0, axis, keepdims=False)
            high = lax.index_in_dim(half, 1, axis, keepdims=False)
            keep = jnp.where(bit_set(bit), high, low)
            send = jnp.where(bit_set(bit), low, high)
            half = (keep.astype(F32) + swap_exp(send, bit).astype(F32)).astype(BF16)
            left = [b for b in left if b != bit]
        sums.append(half)
    return jnp.concatenate(sums)


def normed_grad_kernel(
    halo_steps, x_ref, q_ref, k_ref, v_ref, wq_ref, wk_ref, wv_ref, halo_ref, own_ref, gain_ref, total
):
    step = pl.program_id(0)
    total[...] = dot_last(k_ref[...], wk_ref[...]) + dot_last(v_ref[...], wv_ref[...])

    @pl.when(step >= halo_steps)
    def _():
        total[...] += dot_last(q_ref[...], wq_ref[...])
        own_ref[...] = total[...]

    @pl.when(step < halo_steps)
    def _():
        halo_ref[...] = total[...].astype(BF16)

    x = x_ref[...].astype(F32)
    unit = x * lax.rsqrt(jnp.mean(x * x, axis=1, keepdims=True) + EPSILON)
    update = jnp.sum((total[...] * unit).reshape(-1, 8, x.shape[1]), axis=0)

    @pl.when(step == 0)
    def _():
        gain_ref[...] = update

    @pl.when(step > 0)
    def _():
        gain_ref[...] += update


def normed_grad_of(inputs_all, query_grad, key_grad, value_grad, full_query, full_key, full_value):
    all_rows, width = key_grad.shape
    own = query_grad.shape[0]
    tile = 256
    halo_steps = (all_rows - own) // tile
    row = lambda i: (i, 0)
    late = lambda i: (jnp.maximum(i - halo_steps, 0), 0)
    whole = lambda i: (0, 0)
    block = (tile, width)
    weight = pl.BlockSpec((width, width), whole, pipeline_mode=pl.Buffered(1))
    return pl.pallas_call(
        functools.partial(normed_grad_kernel, halo_steps),
        grid=(all_rows // tile,),
        in_specs=[
            pl.BlockSpec(block, row),
            pl.BlockSpec(block, late),
            pl.BlockSpec(block, row),
            pl.BlockSpec(block, row),
            weight,
            weight,
            weight,
        ],
        out_specs=[
            pl.BlockSpec(block, lambda i: (jnp.minimum(i, halo_steps - 1), 0)),
            pl.BlockSpec(block, late),
            pl.BlockSpec((8, width), whole),
        ],
        out_shape=[
            jax.ShapeDtypeStruct((all_rows - own, width), BF16),
            jax.ShapeDtypeStruct((own, width), F32),
            jax.ShapeDtypeStruct((8, width), F32),
        ],
        scratch_shapes=[pltpu.VMEM(block, F32)],
        compiler_params=params(),
        cost_estimate=brief(),
        name="normed_grad",
    )(inputs_all, query_grad, key_grad, value_grad, full_query, full_key, full_value)


def slab_kernel(part, x_ref, q_ref, k_ref, v_ref, o_ref, g_ref, tail_ref, keep_ref, send_ref, x_turned, o_turned, total):
    core = lax.rem(lax.axis_index("exp"), 2)
    own = q_ref.shape[0]

    @pl.when(pl.program_id(0) == 0)
    def _():
        x_turned[...] = x_ref[...].T
        o_turned[...] = o_ref[...].T

    for place, (left, right) in enumerate(
        (
            (x_turned[:, x_turned.shape[1] - own :], q_ref[...]),
            (x_turned[...], k_ref[...]),
            (x_turned[...], v_ref[...]),
            (o_turned[...], g_ref[...]),
        )
    ):
        total[...] = dot(left, right)
        rows = slice(place * part, (place + 1) * part)
        for slab in range(keep_ref.shape[0]):
            first = 2 * slab * part
            keep_ref[slab, rows, :] = total[pl.ds(first + core * part, part), :].astype(BF16)
            send_ref[slab, rows, :] = total[pl.ds(first + (1 - core) * part, part), :].astype(BF16)
    for slab in range(keep_ref.shape[0]):
        keep_ref[slab, 4 * part :, :] = tail_ref[2 * slab + core]
        send_ref[slab, 4 * part :, :] = tail_ref[2 * slab + 1 - core]


def make_slabs(normed_all, query_grad, key_grad, value_grad, attended, branch_grad, tail):
    devices, extra, width = tail.shape
    all_rows, own = normed_all.shape[0], query_grad.shape[0]
    part, tile = width // devices, 256
    slab_rows = 4 * part + extra
    whole = lambda i: (0, 0)
    column = lambda i: (0, i)
    out = pl.BlockSpec((devices // 2, slab_rows, tile), lambda i: (0, 0, i))
    shape = jax.ShapeDtypeStruct((devices // 2, slab_rows, width), BF16)
    return pl.pallas_call(
        functools.partial(slab_kernel, part),
        grid=(width // tile,),
        in_specs=[
            pl.BlockSpec((all_rows, width), whole),
            pl.BlockSpec((own, tile), column),
            pl.BlockSpec((all_rows, tile), column),
            pl.BlockSpec((all_rows, tile), column),
            pl.BlockSpec((own, width), whole),
            pl.BlockSpec((own, tile), column),
            pl.BlockSpec((devices, extra, tile), lambda i: (0, 0, i)),
        ],
        out_specs=[out, out],
        out_shape=[shape, shape],
        scratch_shapes=[
            pltpu.VMEM((width, all_rows), BF16),
            pltpu.VMEM((width, own), BF16),
            pltpu.VMEM((width, tile), F32),
        ],
        compiler_params=params(),
        cost_estimate=brief(),
        name="slabs",
    )(normed_all, query_grad, key_grad, value_grad, attended, branch_grad, tail)


def exchange(blocks):
    return lax.all_to_all(blocks, "exp", split_axis=0, concat_axis=0, tiled=True)


def body(
    tokens,
    w_query,
    w_key,
    w_value,
    w_out,
    w_router,
    gain_attn,
    gain_mlp,
    pos_bias,
    exp_gate,
    exp_up,
    exp_down,
    doc_lengths,
    bucket_of,
    expert_ids,
    cotangent,
):
    both = ("ctx", "exp")
    own_tokens = tokens[0]
    rows, width = own_tokens.shape
    experts = w_router.shape[1]
    capacity = (5 * TOP * rows + 4 * experts - 1) // (4 * experts)
    reach = (WINDOW + rows - 2) // rows
    scale = HEAD_DIM ** (-0.5)
    ctx_index, ctx_count = lax.axis_index("ctx"), lax.axis_size("ctx")
    exp_index = lax.axis_index("exp")
    part = w_query.shape[0]
    bias_part = pos_bias.shape[0]
    devices = width // part

    expert_range = jnp.arange(experts, dtype=jnp.int32)
    named = jnp.any(expert_ids[0][:, :, None] == expert_range, axis=1)
    named_low = named.astype(BF16)
    step = jnp.arange(rows, dtype=jnp.int32)
    earlier = (step[:, None] > step[None, :]).astype(BF16)
    slots = dot(earlier, named_low).astype(jnp.int32)
    slots = jnp.where(named, slots, -1).T
    routes = (slots[:, None, :] == jnp.arange(capacity, dtype=jnp.int32)[None, :, None]).astype(BF16)
    routes = routes.reshape(experts * capacity, rows)

    names = jnp.pad(named_low, ((0, 0), (0, LANES - experts)))
    early = dot(routes, jnp.concatenate([cotangent[0], names], axis=1)).astype(BF16)
    early = exchange(early.reshape(experts, capacity, width + LANES)).reshape(-1, width + LANES)

    held, share = exp_gate.shape[1], exp_down.shape[1]
    sizes = (share * 5 // 11, share * 6 // 11)
    packed, first = [], 0
    for size in sizes:
        columns = [slice(z * share + first, z * share + first + size) for z in range(ctx_count)]
        parts = [weight[0][:, at] for weight in (exp_gate, exp_up) for at in columns]
        packed.append(jnp.concatenate(parts + [pack_down(exp_down[0][first : first + size], held)], axis=1))
        first += size

    small = jnp.concatenate([w_router.reshape(-1), gain_attn, gain_mlp, pos_bias])
    small = jnp.pad(small, (0, width - small.shape[0]))[None]
    small = lax.all_gather(jnp.pad(small, ((0, 15), (0, 0))), both, axis=0)[:, 0]
    at = part * experts
    full_router = small[:, :at].reshape(width, experts)
    full_gain_attn = small[:, at : at + part].reshape(width).astype(F32)
    full_gain_mlp = small[:, at + part : at + 2 * part].reshape(width).astype(F32)
    table = small[:, at + 2 * part : at + 2 * part + bias_part].reshape(HEADS, BUCKETS)
    column = gather_ctx(jnp.concatenate([w_query, w_key, w_value, w_out], axis=0)[None])
    halo = [shift_ctx(own_tokens, 1), own_tokens]
    column, halo[0], early, packed[0] = together(column, halo[0], early, packed[0])
    for _ in range(1, reach):
        halo.insert(0, shift_ctx(halo[0], 1))
    onehot_bucket = (bucket_of[None, :] == jnp.arange(BUCKETS, dtype=jnp.int32)[:, None]).astype(BF16)
    band = make_band(dot(table, onehot_bucket))

    def then(others):
        *others, halo[0], packed[0] = together(*others, halo[0], packed[0])
        return others

    *halves, band = together(*spread_exp(column, then), band)
    chunk0 = lax.all_gather(packed[0], "ctx", axis=0, tiled=True)
    dense = spread_core(halves)
    full_query, full_key, full_value, full_out = (join_weights(dense, i * part, part) for i in range(4))
    tokens_all = jnp.concatenate(halo, axis=0)
    inputs_all = tokens_all.astype(F32)
    inputs = own_tokens.astype(F32)

    ends = jnp.cumsum(doc_lengths[0])

    def documents(positions):
        return jnp.sum((positions[:, None] >= ends[None, :]).astype(jnp.int32), axis=1)[:, None]

    feature = (jnp.arange(2 * HEAD_DIM, dtype=jnp.int32) % HEAD_DIM)[None, :]
    docs = doc_lengths.shape[1] + 1
    query_pos = ctx_index * rows + step
    key_pos = (ctx_index - reach) * rows + jnp.arange((reach + 1) * rows, dtype=jnp.int32)
    query_doc = (feature == documents(query_pos)).astype(BF16)
    same = (feature == documents(key_pos)) & (key_pos[:, None] >= 0)
    key_doc = jnp.where(same | (feature >= docs), 0.0, NEGATIVE).astype(BF16)

    normed_all = norm_rows(inputs_all, full_gain_attn).astype(BF16)
    normed = normed_all[reach * rows :]
    queries = (dot(normed, full_query).astype(BF16)) * jnp.asarray(scale, BF16)
    keys = dot(normed_all, full_key).astype(BF16)
    values = dot(normed_all, full_value).astype(BF16)
    attended, lse = attend(queries, keys, values, query_doc, key_doc, band)
    middle = inputs + dot(attended, full_out)
    normed_mlp = norm_rows(middle, full_gain_mlp).astype(BF16)

    sent = dot(routes, normed_mlp).astype(BF16)
    arrived = exchange(sent.reshape(experts, capacity, width)).reshape(-1, width)
    router_turned = jnp.pad(full_router.T, ((0, LANES - experts), (0, 0)))
    extras = (early, router_turned)
    units0, units1 = (size * ctx_count for size in sizes)
    arrived, packed[1], chunk0 = together(arrived, packed[1], chunk0)
    up, down = gather_hop(packed[1], packed[1], 1)
    hidden, dboth, carried, _ = run_expert(True, False, units0, ctx_count, arrived, [chunk0], extras, None)
    grad0 = expert_weights(units0, ctx_count, arrived, carried[0], dboth, hidden)
    pieces, sent = [packed[1]], (None, None)
    probs = make_probs(queries, keys, query_doc, key_doc, band, lse)
    for hop in range(1, ctx_count):
        if hop == 1:
            up, down, grad0 = together(up, down, grad0)
            parts0 = grad0.reshape(ctx_count, held, -1)
        else:
            up, down = gather_hop(up, down, hop)
            sent = scatter_hop(*scatter_add(parts0, hop - 1, *sent), hop - 1)
            up, down, probs, *sent = together(up, down, probs, *sent)
        pieces += [up, down]
    arrived, *sent = together(arrived, *scatter_add(parts0, ctx_count - 1, *sent))
    sent = scatter_hop(*sent, ctx_count - 1)
    hidden, dboth, carried, router_grad = run_expert(
        False, True, units1, ctx_count, arrived, pieces, extras, carried
    )
    low, made, back, _ = carried
    hidden, dboth, low, made, back, *sent = together(hidden, dboth, low, made, back, *sent)
    grad1 = expert_weights(units1, ctx_count, arrived, low, dboth, hidden, True)
    back, grad1 = together(back, grad1)
    total1 = lax.psum_scatter(grad1, "ctx", scatter_dimension=0, tiled=True)
    back = exchange(back.reshape(experts, capacity, width)).reshape(-1, width)

    upstream = cotangent[0].astype(F32)
    normed_mlp_grad = dot_rows(routes, back)
    _, second_pull = jax.vjp(norm_rows, middle, full_gain_mlp)
    middle_norm_grad, gain_mlp_grad = second_pull(normed_mlp_grad)
    middle_grad = upstream + middle_norm_grad
    branch_grad = middle_grad.astype(BF16)
    attended_grad = dot_last(branch_grad, full_out).astype(BF16)
    made, attended_grad = together(made, attended_grad)
    made = exchange(made.reshape(experts, capacity, width)).reshape(-1, width)
    query_grad, key_grad, value_grad, dist_grad = attend_back(
        queries, keys, values, attended_grad, attended, probs
    )
    bias_grad = jnp.dot(
        dist_grad.reshape(HEADS, WINDOW), onehot_bucket.T.astype(F32), precision=lax.Precision.HIGHEST
    )

    halo_grad, own_grad, gain_attn_grad = normed_grad_of(
        tokens_all, query_grad, key_grad, value_grad, full_query, full_key, full_value
    )
    gain_attn_grad = jnp.sum(gain_attn_grad, axis=0)

    tail = jnp.concatenate(
        [
            router_grad[:, :experts].reshape(devices, -1),
            gain_attn_grad.reshape(devices, part),
            gain_mlp_grad.reshape(devices, part),
            bias_grad.reshape(devices, bias_part),
        ],
        axis=1,
    ).astype(BF16)
    tail = jnp.pad(tail[:, None, :], ((0, 0), (0, 15), (0, width - tail.shape[1])))
    query_grad, made = together(query_grad, made)
    output = (middle + dot_rows(routes, made)).astype(BF16)
    keep, send = make_slabs(normed_all, query_grad, key_grad, value_grad, attended, branch_grad, tail)
    other = swap_exp(send, 1)
    parts = scatter_exp(keep, other)
    pieces = [halo_grad[place * rows : (place + 1) * rows] for place in range(reach)]
    returning = shift_ctx(pieces[0], -1)
    for piece in pieces[1:]:
        parts, returning, output = together(parts, returning, output)
        returning = shift_ctx((piece.astype(F32) + returning.astype(F32)).astype(BF16), -1)
    own0 = lax.dynamic_index_in_dim(parts0, ctx_index, 0, keepdims=False)
    expert_grads = expert_sums(sizes, ctx_count, own0, *sent, total1)
    sent = (None, None)
    for hop in range(1, ctx_count):
        sent = scatter_add(parts, hop, *sent)
        sent = scatter_hop(*sent, hop)
        if hop == 1:
            *sent, grad_gate, grad_up, grad_down = together(*sent, *expert_grads)
    sums = scatter_end(parts, *sent)
    _, own_pull = jax.vjp(norm_rows, inputs, full_gain_attn)
    input_grad = middle_grad + own_pull(own_grad + returning.astype(F32))[0]
    tail = sums[4 * part]
    at = part * experts
    return (
        output[None],
        input_grad[None],
        sums[:part],
        sums[part : 2 * part],
        sums[2 * part : 3 * part],
        sums[3 * part : 4 * part],
        tail[:at].reshape(part, experts),
        tail[at : at + part],
        tail[at + part : at + 2 * part],
        tail[at + 2 * part : at + 2 * part + bias_part],
        grad_gate[None],
        grad_up[None],
        grad_down[None],
    )


def solution(mesh):
    rows3 = P("exp", "ctx", None)
    dense2 = P(("ctx", "exp"), None)
    dense1 = P(("ctx", "exp"))
    return jax.shard_map(
        body,
        mesh=mesh,
        in_specs=(
            rows3,
            dense2,
            dense2,
            dense2,
            dense2,
            dense2,
            dense1,
            dense1,
            dense1,
            rows3,
            rows3,
            rows3,
            P("exp", None),
            P(),
            rows3,
            rows3,
        ),
        out_specs=(
            rows3,
            rows3,
            dense2,
            dense2,
            dense2,
            dense2,
            dense2,
            dense1,
            dense1,
            dense1,
            rows3,
            rows3,
            rows3,
        ),
        check_vma=False,
    )
```

```python
import functools

import jax
import jax.numpy as jnp
from jax import lax
from jax.experimental import pallas as pl
from jax.experimental.pallas import tpu as pltpu
from jax.sharding import PartitionSpec as P

HEADS = 16
HEAD_DIM = 64
BUCKETS = 32
TOP = 2
WINDOW = 1024

EPSILON = 1e-06
NEGATIVE = -1e30
LANES = 128
CHUNK = 256
FF_TILE = 512
ROW_TILE = 256
VMEM_LIMIT = 58 * 2**20
BF16 = jnp.bfloat16
F32 = jnp.float32


def shift_ctx(block, distance):
    devices = range(lax.axis_size("ctx"))
    route = [(i - distance, i) for i in devices if i - distance in devices]
    return lax.ppermute(block, "ctx", route)


def norm_rows(values, gain):
    return values * lax.rsqrt(jnp.mean(values * values, axis=-1, keepdims=True) + EPSILON) * gain


def dot(left, right):
    return jnp.dot(left, right, preferred_element_type=F32)


def dot_rows(left, right):
    return lax.dot_general(left, right, (((0,), (0,)), ((), ())), preferred_element_type=F32)


def dot_last(left, right):
    return lax.dot_general(left, right, (((1,), (1,)), ((), ())), preferred_element_type=F32)


def params(**more):
    return pltpu.CompilerParams(vmem_limit_bytes=VMEM_LIMIT, **more)


def brief():
    return pl.CostEstimate(flops=2**20, bytes_accessed=2**20, transcendentals=0)


def band_kernel(bias_ref, band_ref):
    blocks = WINDOW // LANES
    size = (blocks + 2) * LANES
    for head in range(bias_ref.shape[0]):
        row = jnp.broadcast_to(bias_ref[head : head + 1, :], (8, size))
        eight = pltpu.roll(row, 0, 1, stride=1, stride_axis=0)
        for group in range(LANES // 8):
            wide = pltpu.roll(eight, 8 * group, 1) if group else eight
            for a in range(blocks + 1):
                first = a * LANES + group * 8
                at = (blocks + 1 - a) * LANES
                band_ref[head, first : first + 8, :] = wide[:, at : at + LANES]


def make_band(bias_dist):
    group = 8
    edge = jnp.full((HEADS, LANES), NEGATIVE, F32)
    padded = jnp.concatenate([edge, bias_dist, edge], axis=1)
    return pl.pallas_call(
        band_kernel,
        grid=(HEADS // group,),
        in_specs=[pl.BlockSpec((group, WINDOW + 2 * LANES), lambda h: (h, 0))],
        out_specs=pl.BlockSpec((group, WINDOW + LANES, LANES), lambda h: (h, 0, 0)),
        out_shape=jax.ShapeDtypeStruct((HEADS, WINDOW + LANES, LANES), F32),
        compiler_params=params(),
        cost_estimate=brief(),
        name="bias_band",
    )(padded)


def sum_band(band_ref):
    blocks = WINDOW // LANES
    size = (blocks + 2) * LANES
    row = lax.broadcasted_iota(jnp.int32, (8, 1), 0)
    edge = jnp.zeros((8, LANES), F32)
    total = None
    for group in range(LANES // 8):
        pieces = [edge]
        for a in range(blocks, -1, -1):
            first = a * LANES + group * 8
            pieces.append(band_ref[first : first + 8, :])
        wide = jnp.concatenate(pieces, axis=1)
        if group:
            wide = pltpu.roll(wide, size - 8 * group, 1)
        total = wide if total is None else total + wide
    dist = jnp.zeros_like(total)
    for r in range(8):
        turned = pltpu.roll(total, size - r, 1) if r else total
        dist = dist + jnp.where(row == r, turned, 0.0)
    return jnp.sum(dist, axis=0, keepdims=True)[:, LANES : LANES + WINDOW]


def head_lanes(head):
    lane = lax.broadcasted_iota(jnp.int32, (1, 2 * HEAD_DIM), 1)
    return (lane >= head * HEAD_DIM) & (lane < (head + 1) * HEAD_DIM)


def masked_scores(head, start, q_ref, k_ref, qdoc_ref, kdoc_ref):
    span = WINDOW + CHUNK
    mine = head_lanes(head)
    q_rows, k_rows = pl.ds(start, CHUNK), pl.ds(start, span)
    q_part = jnp.where(mine, q_ref[q_rows, :], qdoc_ref[q_rows, :])
    k_part = jnp.where(mine, k_ref[k_rows, :], kdoc_ref[k_rows, :])
    return dot_last(k_part, q_part)


def sub_blocks():
    return [(s * LANES, WINDOW + LANES) for s in range(CHUNK // LANES)]


def spread(parts):
    span = WINDOW + CHUNK
    columns = []
    for (first, rows), part in zip(sub_blocks(), parts):
        pieces = []
        if first:
            pieces.append(jnp.zeros((first, LANES), part.dtype))
        pieces.append(part)
        if span - first - rows:
            pieces.append(jnp.zeros((span - first - rows, LANES), part.dtype))
        columns.append(jnp.concatenate(pieces, axis=0) if len(pieces) > 1 else part)
    return jnp.concatenate(columns, axis=1)


def attend_kernel(q_ref, k_ref, v_ref, qdoc_ref, kdoc_ref, band_ref, o_ref, lse_ref):
    span = WINDOW + CHUNK
    for start in range(0, q_ref.shape[0], CHUNK):
        v_turned = v_ref[pl.ds(start, span), :].T
        outs = []
        for head in range(2):
            scores = masked_scores(head, start, q_ref, k_ref, qdoc_ref, kdoc_ref)
            band = band_ref[head]
            low, scale, logs = [], [], []
            for s, (first, rows) in enumerate(sub_blocks()):
                part = scores[first : first + rows, s * LANES : (s + 1) * LANES] + band
                top = jnp.max(part, axis=0, keepdims=True)
                expo = jnp.exp(part - top)
                total = jnp.sum(expo, axis=0, keepdims=True)
                low.append(expo.astype(BF16))
                scale.append(1.0 / total)
                logs.append(top + jnp.log(total))
            out = dot(v_turned[head * HEAD_DIM : (head + 1) * HEAD_DIM], spread(low))
            outs.append(out * jnp.concatenate(scale, axis=1))
            lse_ref[0, head : head + 1, pl.ds(start, CHUNK)] = jnp.concatenate(logs, axis=1)
        o_ref[pl.ds(start, CHUNK), :] = jnp.concatenate(outs, axis=0).T.astype(BF16)


def attend(queries, keys, values, query_doc, key_doc, band):
    rows, width = queries.shape
    keys_rows = keys.shape[0]
    pairs = HEADS // 2
    wide = 2 * HEAD_DIM
    return pl.pallas_call(
        attend_kernel,
        grid=(pairs,),
        in_specs=[
            pl.BlockSpec((rows, wide), lambda p: (0, p)),
            pl.BlockSpec((keys_rows, wide), lambda p: (0, p)),
            pl.BlockSpec((keys_rows, wide), lambda p: (0, p)),
            pl.BlockSpec((rows, wide), lambda p: (0, 0)),
            pl.BlockSpec((keys_rows, wide), lambda p: (0, 0)),
            pl.BlockSpec((2, WINDOW + LANES, LANES), lambda p: (p, 0, 0)),
        ],
        out_specs=[
            pl.BlockSpec((rows, wide), lambda p: (0, p)),
            pl.BlockSpec((1, 2, rows), lambda p: (p, 0, 0)),
        ],
        out_shape=[
            jax.ShapeDtypeStruct((rows, width), BF16),
            jax.ShapeDtypeStruct((pairs, 2, rows), F32),
        ],
        compiler_params=params(),
        cost_estimate=brief(),
        name="attend",
    )(queries, keys, values, query_doc, key_doc, band)


def probs_kernel(q_ref, k_ref, qdoc_ref, kdoc_ref, band_ref, lse_ref, probs_ref):
    for chunk in range(q_ref.shape[0] // CHUNK):
        start = chunk * CHUNK
        for head in range(2):
            scores = masked_scores(head, start, q_ref, k_ref, qdoc_ref, kdoc_ref)
            band = band_ref[head]
            lse = lse_ref[0, head : head + 1, pl.ds(start, CHUNK)]
            parts = []
            for s, (first, rows) in enumerate(sub_blocks()):
                lanes = slice(s * LANES, (s + 1) * LANES)
                parts.append(jnp.exp(scores[first : first + rows, lanes] + band - lse[:, lanes]).astype(BF16))
            probs_ref[head, chunk] = spread(parts)


def make_probs(queries, keys, query_doc, key_doc, band, lse):
    rows, width = queries.shape
    keys_rows = keys.shape[0]
    pairs = HEADS // 2
    wide = 2 * HEAD_DIM
    span, chunks = WINDOW + CHUNK, rows // CHUNK
    return pl.pallas_call(
        probs_kernel,
        grid=(pairs,),
        in_specs=[
            pl.BlockSpec((rows, wide), lambda p: (0, p)),
            pl.BlockSpec((keys_rows, wide), lambda p: (0, p)),
            pl.BlockSpec((rows, wide), lambda p: (0, 0)),
            pl.BlockSpec((keys_rows, wide), lambda p: (0, 0)),
            pl.BlockSpec((2, WINDOW + LANES, LANES), lambda p: (p, 0, 0)),
            pl.BlockSpec((1, 2, rows), lambda p: (p, 0, 0)),
        ],
        out_specs=pl.BlockSpec((2, chunks, span, CHUNK), lambda p: (p, 0, 0, 0)),
        out_shape=jax.ShapeDtypeStruct((HEADS, chunks, span, CHUNK), BF16),
        compiler_params=params(),
        cost_estimate=brief(),
        name="probs",
    )(queries, keys, query_doc, key_doc, band, lse)


def attend_back_kernel(
    q_ref, k_ref, v_ref, g_ref, o_ref, probs_ref, dq_ref, dk_ref, dv_ref, dist_ref, dk_sum, dv_sum, dband
):
    span = WINDOW + CHUNK
    dk_sum[...] = jnp.zeros_like(dk_sum)
    dv_sum[...] = jnp.zeros_like(dv_sum)
    for chunk in range(q_ref.shape[0] // CHUNK):
        start = chunk * CHUNK
        q_rows, k_rows = pl.ds(start, CHUNK), pl.ds(start, span)
        k_turned = k_ref[k_rows, :].T
        product = (g_ref[q_rows, :].astype(F32) * o_ref[q_rows, :].astype(F32)).T
        dq_parts = []
        for head in range(2):
            mine = head_lanes(head)
            zero = jnp.zeros((), BF16)
            g_part = jnp.where(mine, g_ref[q_rows, :], zero)
            q_part = jnp.where(mine, q_ref[q_rows, :], zero)
            prob_grad = dot_last(v_ref[k_rows, :], g_part)
            delta = jnp.sum(product[head * HEAD_DIM : (head + 1) * HEAD_DIM], axis=0, keepdims=True)
            grad_low, grad_sum = [], None
            for s, (first, rows) in enumerate(sub_blocks()):
                lanes = slice(s * LANES, (s + 1) * LANES)
                probs = probs_ref[head, chunk, first : first + rows, lanes].astype(F32)
                grad = probs * (prob_grad[first : first + rows, lanes] - delta[:, lanes])
                grad_low.append(grad.astype(BF16))
                grad_sum = grad if grad_sum is None else grad_sum + grad
            if chunk == 0:
                dband[head] = grad_sum
            else:
                dband[head] = dband[head] + grad_sum
            grads = spread(grad_low)
            dk_sum[k_rows, :] += dot(grads, q_part)
            dv_sum[k_rows, :] += dot(probs_ref[head, chunk], g_part)
            dq_parts.append(dot(k_turned[head * HEAD_DIM : (head + 1) * HEAD_DIM], grads))
        turned = jnp.concatenate(dq_parts, axis=0).T
        dq_ref[q_rows, :] = (turned * HEAD_DIM ** (-0.5)).astype(BF16)
    dk_ref[...] = dk_sum[...].astype(BF16)
    dv_ref[...] = dv_sum[...].astype(BF16)
    for head in range(2):
        dist_ref[0, head : head + 1, :] = sum_band(dband.at[head])


def attend_back(queries, keys, values, grad, out, probs):
    rows, width = queries.shape
    keys_rows = keys.shape[0]
    pairs = HEADS // 2
    wide = 2 * HEAD_DIM
    q_spec = pl.BlockSpec((rows, wide), lambda p: (0, p))
    k_spec = pl.BlockSpec((keys_rows, wide), lambda p: (0, p))
    return pl.pallas_call(
        attend_back_kernel,
        grid=(pairs,),
        in_specs=[
            q_spec,
            k_spec,
            k_spec,
            q_spec,
            q_spec,
            pl.BlockSpec((2,) + probs.shape[1:], lambda p: (p, 0, 0, 0)),
        ],
        out_specs=[q_spec, k_spec, k_spec, pl.BlockSpec((1, 2, WINDOW), lambda p: (p, 0, 0))],
        out_shape=[
            jax.ShapeDtypeStruct((rows, width), BF16),
            jax.ShapeDtypeStruct((keys_rows, width), BF16),
            jax.ShapeDtypeStruct((keys_rows, width), BF16),
            jax.ShapeDtypeStruct((pairs, 2, WINDOW), F32),
        ],
        scratch_shapes=[
            pltpu.VMEM((keys_rows, wide), F32),
            pltpu.VMEM((keys_rows, wide), F32),
            pltpu.VMEM((2, WINDOW + LANES, LANES), F32),
        ],
        compiler_params=params(),
        cost_estimate=pl.CostEstimate(
            flops=20 * rows * WINDOW * width * 2, bytes_accessed=2**20, transcendentals=0
        ),
        name="attend_back",
    )(queries, keys, values, grad, out, probs)


def down_blocks(units, width, count):
    held, share = width // count, units // count
    extra = share - held
    wide = width * extra // held
    blocks = []
    for z in range(count):
        blocks.append(((z * held, 0), (z * share, 0), (held, width)))
        for m in range(held // extra):
            blocks.append(((z * held + m * extra, width), (z * share + held, m * wide), (extra, wide)))
    return blocks


def pack_down(down, held):
    extra, width = down.shape[0] - held, down.shape[1]
    wide = width * extra // held
    rest = [down[held:, m * wide : (m + 1) * wide] for m in range(held // extra)]
    return jnp.concatenate([down[:held], jnp.concatenate(rest, axis=0)], axis=1)


def unpack_down(packed, size, width):
    held = packed.shape[0]
    extra = size - held
    rest = [packed[m * extra : (m + 1) * extra, width:] for m in range(held // extra)]
    return jnp.concatenate([packed[:, :width], jnp.concatenate(rest, axis=1)], axis=0)


def expert_kernel(first, last, units, count, parts, *refs):
    refs = list(refs)
    take = lambda: refs.pop(0)
    x_ref = take()
    pieces = [take() for _ in range(parts)]
    if first or last:
        c_ref, names_ref, router_ref = take(), take(), take()
    if not first:
        low_ref, made_in, back_in = take(), take(), take()
    if last and not first:
        gate_in = take()
    hidden_ref, dboth_ref = take(), take()
    if first:
        low_out = take()
    if first and not last:
        gate_out = take()
    made_ref, back_ref = take(), take()
    if last:
        drouter_ref = take()
    chunk_ref, down_s, sems = take(), take(), take()
    rows, width = x_ref.shape
    held = width // count
    index = lax.axis_index("ctx")

    def slot(z):
        return chunk_ref.at[z * held : (z + 1) * held]

    @pl.when(pl.program_id(0) == 0)
    def _():
        if parts == 1:
            for z in range(count):
                pltpu.make_async_copy(pieces[0].at[z * held : (z + 1) * held], slot(z), sems.at[z]).start()
        for z in range(count if parts > 1 else 0):
            for here in range(count):
                hop = abs(here - z)
                source = pieces[0 if hop == 0 else 2 * hop - 1 if z < here else 2 * hop]

                @pl.when(index == here)
                def _(source=source, z=z):
                    pltpu.make_async_copy(source, slot(z), sems.at[z]).start()

        for z in range(count):
            pltpu.make_async_copy(pieces[0].at[:held], slot(z), sems.at[z]).wait()

    x = x_ref[...]
    own = lax.broadcasted_iota(jnp.int32, (1, LANES), 1) == lax.axis_index("exp")
    if first:
        names = names_ref[...].astype(F32)
        logits = dot_last(x, router_ref[...]) * names
        mine = jnp.sum(jnp.where(own, logits, 0.0), axis=1, keepdims=True)
        theirs = jnp.sum(jnp.where(own, 0.0, logits), axis=1, keepdims=True)
        gate = jax.nn.sigmoid(mine - theirs)
        low_out[...] = (gate * c_ref[...].astype(F32)).astype(BF16)
        if not last:
            gate_out[...] = jnp.broadcast_to(gate, (rows, LANES))
        low_ref = low_out
    elif last:
        gate = gate_in[...][:, :1]
    @pl.when(pl.program_id(0) == 0)
    def _():
        for (row, column), (to_row, to_column), (high, wide) in down_blocks(units, width, count):
            from_columns = slice(2 * units + column, 2 * units + column + wide)
            down_s[to_row : to_row + high, to_column : to_column + wide] = chunk_ref[row : row + high, from_columns]

    for start in range(0, units, FF_TILE):
        stop = min(start + FF_TILE, units)
        at, up_at = slice(start, stop), slice(units + start, units + stop)
        gate_pre = dot(x, chunk_ref[:, at])
        up_pre = dot(x, chunk_ref[:, up_at])
        hidden_grad = dot_last(low_ref[...], down_s[at, :])
        root = 0.7978845608028654
        square = gate_pre * gate_pre
        bent = jnp.tanh(gate_pre * (root + root * 0.044715 * square))
        half = 0.5 * (1.0 + bent)
        act = gate_pre * half
        slope = half + 0.5 * gate_pre * (1.0 - bent * bent) * (root + 3.0 * root * 0.044715 * square)
        hidden_ref[:, at] = (act * up_pre).astype(BF16)
        dboth_ref[:, at] = (hidden_grad * up_pre * slope).astype(BF16)
        dboth_ref[:, up_at] = (hidden_grad * act).astype(BF16)
    made = dot(hidden_ref[...], down_s[...])
    back = dot_last(dboth_ref[...], chunk_ref[:, : 2 * units])
    if not first:
        made = made + made_in[...]
        back = back + back_in[...]
    if last:
        made = made.astype(BF16).astype(F32)
        names = names_ref[...].astype(F32)
        push = jnp.sum(c_ref[...].astype(F32) * made, axis=1, keepdims=True)
        push = push * gate * (1.0 - gate)
        logits_grad = push * jnp.where(own, names, -names)
        high = logits_grad.astype(BF16)
        low = (logits_grad - high.astype(F32)).astype(BF16)
        made = gate * made
        back = back + dot(high, router_ref[...]) + dot(low, router_ref[...])
        turned = x.T
        update = dot(turned, high) + dot(turned, low)

        @pl.when(pl.program_id(0) == 0)
        def _():
            drouter_ref[...] = update

        @pl.when(pl.program_id(0) > 0)
        def _():
            drouter_ref[...] += update

    made_ref[...] = made.astype(made_ref.dtype)
    back_ref[...] = back.astype(back_ref.dtype)


def run_expert(first, last, units, count, x, pieces, extras, carried):
    rows, width = x.shape
    whole = lambda i: (0, 0)
    step = lambda i: (i, 0)
    wide = pl.BlockSpec((ROW_TILE, width), step)
    thin = pl.BlockSpec((ROW_TILE, LANES), step)
    struct = jax.ShapeDtypeStruct
    early, router = extras
    operands = [x] + pieces
    in_specs = [wide] + [pl.BlockSpec(memory_space=pl.ANY)] * len(pieces)
    if first or last:
        operands += [early, early, router]
        names = pl.BlockSpec((ROW_TILE, LANES), lambda i: (i, width // LANES))
        in_specs += [wide, names, pl.BlockSpec((LANES, width), whole)]
    if not first:
        low, made, back, gate = carried
        operands += [low, made, back]
        in_specs += [wide, wide, wide]
        if last:
            operands.append(gate)
            in_specs.append(thin)
    out_shape = [struct((rows, units), BF16), struct((rows, 2 * units), BF16)]
    out_specs = [pl.BlockSpec((ROW_TILE, units), step), pl.BlockSpec((ROW_TILE, 2 * units), step)]
    if first:
        out_shape.append(struct((rows, width), BF16))
        out_specs.append(wide)
        if not last:
            out_shape.append(struct((rows, LANES), F32))
            out_specs.append(thin)
    kept = BF16 if last else F32
    out_shape += [struct((rows, width), kept), struct((rows, width), kept)]
    out_specs += [wide, wide]
    if last:
        out_shape.append(struct((width, LANES), F32))
        out_specs.append(pl.BlockSpec((width, LANES), whole))
    outs = list(
        pl.pallas_call(
            functools.partial(expert_kernel, first, last, units, count, len(pieces)),
            grid=(rows // ROW_TILE,),
            in_specs=in_specs,
            out_specs=out_specs,
            out_shape=out_shape,
            scratch_shapes=[
                pltpu.VMEM((width, pieces[0].shape[1]), BF16),
                pltpu.VMEM((units, width), BF16),
                pltpu.SemaphoreType.DMA((count,)),
            ],
            compiler_params=params(),
            cost_estimate=brief(),
            name="expert",
        )(*operands)
    )
    hidden, dboth = outs[:2]
    if first:
        low = outs[2]
        gate = None if last else outs[3]
    if last:
        made, back, drouter = outs[-3:]
        return hidden, dboth, (low, made, back, gate), drouter
    made, back = outs[-2:]
    return hidden, dboth, (low, made, back, gate), None


def expert_weights_kernel(
    units, count, x_ref, low_ref, dboth_ref, hidden_ref, grad_ref, x_turned, hidden_turned, rest
):
    step = pl.program_id(0)
    tile = low_ref.shape[1]
    width = x_ref.shape[1]
    both_steps, down_steps = 2 * units // tile, width // tile

    @pl.when(step == 0)
    def _():
        x_turned[...] = x_ref[...].T

    @pl.when(step < both_steps)
    def _():
        grad_ref[...] = dot(x_turned[...], dboth_ref[...]).astype(BF16)

    @pl.when(step == both_steps)
    def _():
        hidden_turned[...] = hidden_ref[...].T

    for place in range(down_steps):

        @pl.when(step == both_steps + place)
        def _(place=place):
            total = dot(hidden_turned[...], low_ref[...]).astype(BF16)
            first = place * tile
            for (row, column), (from_row, from_column), (high, wide) in down_blocks(units, width, count):
                if column == 0:
                    grad_ref[row : row + high, :] = total[from_row : from_row + high]
                    continue
                low, top = max(first, from_column), min(first + tile, from_column + wide)
                if low < top:
                    rest[row : row + high, low - from_column : top - from_column] = total[
                        from_row : from_row + high, low - first : top - first
                    ]

    for place in range(rest.shape[1] // tile):

        @pl.when(step == both_steps + down_steps + place)
        def _(place=place):
            grad_ref[...] = rest[:, place * tile : (place + 1) * tile]


def expert_weights(units, count, x, low, dboth, hidden, long=False):
    rows, width = x.shape
    tile = 512
    extra_steps = -(-(units - width) // tile)
    both_steps, down_steps = 2 * units // tile, width // tile
    whole = lambda i: (0, 0)
    work = pl.CostEstimate(flops=6 * rows * width * units, bytes_accessed=2**20, transcendentals=0)
    return pl.pallas_call(
        functools.partial(expert_weights_kernel, units, count),
        grid=(both_steps + down_steps + extra_steps,),
        in_specs=[
            pl.BlockSpec((rows, width), whole),
            pl.BlockSpec((rows, tile), lambda i: (0, jnp.clip(i - both_steps, 0, down_steps - 1))),
            pl.BlockSpec((rows, tile), lambda i: (0, jnp.minimum(i, both_steps - 1))),
            pl.BlockSpec((rows, units), whole),
        ],
        out_specs=pl.BlockSpec((width, tile), lambda i: (0, i)),
        out_shape=jax.ShapeDtypeStruct((width, 3 * units), BF16),
        scratch_shapes=[
            pltpu.VMEM((width, rows), BF16),
            pltpu.VMEM((units, rows), BF16),
            pltpu.VMEM((width, extra_steps * tile), BF16),
        ],
        compiler_params=params(),
        cost_estimate=work if long else brief(),
        name="expert_weights",
    )(x, low, dboth, hidden)


def expert_sums_kernel(sizes, count, own_ref, up_ref, down_ref, last_ref, gate_out, up_out, down_out):
    held, width = own_ref.shape[0], down_out.shape[1]
    extras = [size - held for size in sizes]
    tile = min(extras)
    for first in range(0, held, tile):
        rows = slice(first, first + tile)
        totals = (
            own_ref[rows, :].astype(F32) + up_ref[rows, :].astype(F32) + down_ref[rows, :].astype(F32),
            last_ref[rows, :].astype(F32),
        )
        for out, part in ((gate_out, 0), (up_out, 1)):
            pieces = []
            for z in range(count):
                for size, total in zip(sizes, totals):
                    at = part * size * count + z * size
                    pieces.append(total[:, at : at + size])
            out[rows, :] = jnp.concatenate(pieces, axis=1)
        start = 0
        for size, extra, total in zip(sizes, extras, totals):
            wide = width * extra // held
            at = 2 * size * count
            down_out[start + first : start + first + tile, :] = total[:, at : at + width]
            to, columns = start + held + first % extra, first // extra * wide
            down_out[to : to + tile, columns : columns + wide] = total[:, at + width :]
            start += size


def expert_sums(sizes, count, own, up, down, last):
    held = own.shape[0]
    units = sum(sizes)
    struct = jax.ShapeDtypeStruct
    width = held * count
    return pl.pallas_call(
        functools.partial(expert_sums_kernel, sizes, count),
        in_specs=[pl.BlockSpec(memory_space=pltpu.VMEM)] * 4,
        out_specs=[pl.BlockSpec(memory_space=pltpu.VMEM)] * 3,
        out_shape=[
            struct((held, units * count), F32),
            struct((held, units * count), F32),
            struct((units, width), F32),
        ],
        compiler_params=params(),
        cost_estimate=brief(),
        name="expert_sums",
    )(own, up, down, last)


def ctx_moves(distance):
    devices = range(lax.axis_size("ctx"))
    return [(i - distance, i) for i in devices if i - distance in devices]


def together(*values):
    return lax.optimization_barrier(values)


def gather_ctx(piece):
    count, index, size = lax.axis_size("ctx"), lax.axis_index("ctx"), piece.shape[0]
    full = jnp.zeros((count * size,) + piece.shape[1:], piece.dtype)
    place = lambda buffer, part, at: lax.dynamic_update_slice_in_dim(buffer, part, at * size, 0)
    full = place(full, piece, index)
    up = down = piece
    for hop in range(1, count):
        up, down = shift_ctx(up, 1), shift_ctx(down, -1)
        for part, at, held in ((up, index - hop, index >= hop), (down, index + hop, index + hop < count)):
            at = jnp.clip(at, 0, count - 1)
            old = lax.dynamic_slice_in_dim(full, at * size, size, 0)
            full = place(full, jnp.where(held, part, old), at)
    return full


def gather_hop(up, down, hop):
    count = lax.axis_size("ctx")
    route = [(i, i + 1) for i in range(hop - 1, count - 1)]
    back = [(count - 1 - i, count - 1 - j) for i, j in route]
    return lax.ppermute(up, "ctx", route), lax.ppermute(down, "ctx", back)


def scatter_add(parts, hop, up=None, down=None):
    count, index = lax.axis_size("ctx"), lax.axis_index("ctx")

    def part(at):
        return lax.dynamic_index_in_dim(parts, jnp.clip(at, 0, count - 1), 0, keepdims=False).astype(F32)

    distance = count - hop
    if hop == 1:
        return parts[count - 1].astype(BF16), parts[0].astype(BF16)
    mine_up, mine_down = part(index + distance), part(index - distance)
    if up is not None:
        mine_up, mine_down = mine_up + up.astype(F32), mine_down + down.astype(F32)
    return mine_up.astype(BF16), mine_down.astype(BF16)


def scatter_hop(up, down, hop):
    count = lax.axis_size("ctx")
    route = [(i, i + 1) for i in range(hop)]
    back = [(count - 1 - i, count - 1 - j) for i, j in route]
    return lax.ppermute(up, "ctx", route), lax.ppermute(down, "ctx", back)


def scatter_end(parts, up, down):
    own = lax.dynamic_index_in_dim(parts, lax.axis_index("ctx"), 0, keepdims=False).astype(F32)
    return own + up.astype(F32) + down.astype(F32)


def swap_exp(block, bit):
    return lax.ppermute(block, "exp", [(i, i ^ bit) for i in range(lax.axis_size("exp"))])


def bit_set(bit):
    return (lax.axis_index("exp") // bit) % 2 == 1


def exp_bits():
    size, bits = lax.axis_size("exp"), []
    while 1 << len(bits) < size:
        bits.append(1 << len(bits))
    return bits


def routes_exp():
    bits = exp_bits()
    return bits[1:], bits[:0:-1]


def spread_exp(column, then):
    count = column.shape[0]
    halves = [column[None, : count // 2], column[None, count // 2 :]]
    for step, bits in enumerate(zip(*routes_exp())):
        others = [swap_exp(half, bit) for half, bit in zip(halves, bits)]
        if step == 0:
            others = then(others)
        for place, (half, other, bit) in enumerate(zip(halves, others, bits)):
            halves[place] = jnp.where(
                bit_set(bit), jnp.concatenate([other, half]), jnp.concatenate([half, other])
            )
    return halves


def spread_core(halves):
    bits = exp_bits()
    done = []
    for half, order in zip(halves, routes_exp()):
        other = swap_exp(half, 1)
        mine_first = bit_set(1)
        pair = jnp.stack([jnp.where(mine_first, other, half), jnp.where(mine_first, half, other)])
        pair = pair.reshape((2,) + (2,) * len(order) + half.shape[1:])
        axes = [1 + order[::-1].index(bit) for bit in bits[:0:-1]] + [0]
        axes = [len(axes)] + axes + list(range(len(axes) + 1, pair.ndim))
        pair = pair.transpose(axes)
        done.append(pair.reshape((half.shape[1], 1 << len(bits)) + half.shape[2:]))
    return done


def join_weights(done, first, rows):
    width = done[0].shape[-1]
    return jnp.concatenate([half[:, :, first : first + rows].reshape(-1, width) for half in done])


def scatter_exp(keep, other):
    count, bits = lax.axis_size("ctx"), exp_bits()
    chip = (keep.astype(F32) + other.astype(F32)).astype(BF16)
    chip = chip.reshape((count, -1) + chip.shape[1:])
    sums = []
    for half, order in zip((chip[: count // 2], chip[count // 2 :]), routes_exp()):
        half = half.reshape((count // 2,) + (2,) * (len(bits) - 1) + half.shape[2:])
        left = bits[:0:-1]
        for bit in order:
            axis = 1 + left.index(bit)
            low = lax.index_in_dim(half, 0, axis, keepdims=False)
            high = lax.index_in_dim(half, 1, axis, keepdims=False)
            keep = jnp.where(bit_set(bit), high, low)
            send = jnp.where(bit_set(bit), low, high)
            half = (keep.astype(F32) + swap_exp(send, bit).astype(F32)).astype(BF16)
            left = [b for b in left if b != bit]
        sums.append(half)
    return jnp.concatenate(sums)


def normed_grad_kernel(
    halo_steps, x_ref, q_ref, k_ref, v_ref, wq_ref, wk_ref, wv_ref, halo_ref, own_ref, gain_ref, total
):
    step = pl.program_id(0)
    total[...] = dot_last(k_ref[...], wk_ref[...]) + dot_last(v_ref[...], wv_ref[...])

    @pl.when(step >= halo_steps)
    def _():
        total[...] += dot_last(q_ref[...], wq_ref[...])
        own_ref[...] = total[...]

    @pl.when(step < halo_steps)
    def _():
        halo_ref[...] = total[...].astype(BF16)

    x = x_ref[...].astype(F32)
    unit = x * lax.rsqrt(jnp.mean(x * x, axis=1, keepdims=True) + EPSILON)
    update = jnp.sum((total[...] * unit).reshape(-1, 8, x.shape[1]), axis=0)

    @pl.when(step == 0)
    def _():
        gain_ref[...] = update

    @pl.when(step > 0)
    def _():
        gain_ref[...] += update


def normed_grad_of(inputs_all, query_grad, key_grad, value_grad, full_query, full_key, full_value):
    all_rows, width = key_grad.shape
    own = query_grad.shape[0]
    tile = 256
    halo_steps = (all_rows - own) // tile
    row = lambda i: (i, 0)
    late = lambda i: (jnp.maximum(i - halo_steps, 0), 0)
    whole = lambda i: (0, 0)
    block = (tile, width)
    weight = pl.BlockSpec((width, width), whole, pipeline_mode=pl.Buffered(1))
    return pl.pallas_call(
        functools.partial(normed_grad_kernel, halo_steps),
        grid=(all_rows // tile,),
        in_specs=[
            pl.BlockSpec(block, row),
            pl.BlockSpec(block, late),
            pl.BlockSpec(block, row),
            pl.BlockSpec(block, row),
            weight,
            weight,
            weight,
        ],
        out_specs=[
            pl.BlockSpec(block, lambda i: (jnp.minimum(i, halo_steps - 1), 0)),
            pl.BlockSpec(block, late),
            pl.BlockSpec((8, width), whole),
        ],
        out_shape=[
            jax.ShapeDtypeStruct((all_rows - own, width), BF16),
            jax.ShapeDtypeStruct((own, width), F32),
            jax.ShapeDtypeStruct((8, width), F32),
        ],
        scratch_shapes=[pltpu.VMEM(block, F32)],
        compiler_params=params(),
        cost_estimate=brief(),
        name="normed_grad",
    )(inputs_all, query_grad, key_grad, value_grad, full_query, full_key, full_value)


def slab_kernel(part, x_ref, q_ref, k_ref, v_ref, o_ref, g_ref, tail_ref, keep_ref, send_ref, x_turned, o_turned, total):
    core = lax.rem(lax.axis_index("exp"), 2)
    own = q_ref.shape[0]

    @pl.when(pl.program_id(0) == 0)
    def _():
        x_turned[...] = x_ref[...].T
        o_turned[...] = o_ref[...].T

    for place, (left, right) in enumerate(
        (
            (x_turned[:, x_turned.shape[1] - own :], q_ref[...]),
            (x_turned[...], k_ref[...]),
            (x_turned[...], v_ref[...]),
            (o_turned[...], g_ref[...]),
        )
    ):
        total[...] = dot(left, right)
        rows = slice(place * part, (place + 1) * part)
        for slab in range(keep_ref.shape[0]):
            first = 2 * slab * part
            keep_ref[slab, rows, :] = total[pl.ds(first + core * part, part), :].astype(BF16)
            send_ref[slab, rows, :] = total[pl.ds(first + (1 - core) * part, part), :].astype(BF16)
    for slab in range(keep_ref.shape[0]):
        keep_ref[slab, 4 * part :, :] = tail_ref[2 * slab + core]
        send_ref[slab, 4 * part :, :] = tail_ref[2 * slab + 1 - core]


def make_slabs(normed_all, query_grad, key_grad, value_grad, attended, branch_grad, tail):
    devices, extra, width = tail.shape
    all_rows, own = normed_all.shape[0], query_grad.shape[0]
    part, tile = width // devices, 256
    slab_rows = 4 * part + extra
    whole = lambda i: (0, 0)
    column = lambda i: (0, i)
    out = pl.BlockSpec((devices // 2, slab_rows, tile), lambda i: (0, 0, i))
    shape = jax.ShapeDtypeStruct((devices // 2, slab_rows, width), BF16)
    return pl.pallas_call(
        functools.partial(slab_kernel, part),
        grid=(width // tile,),
        in_specs=[
            pl.BlockSpec((all_rows, width), whole),
            pl.BlockSpec((own, tile), column),
            pl.BlockSpec((all_rows, tile), column),
            pl.BlockSpec((all_rows, tile), column),
            pl.BlockSpec((own, width), whole),
            pl.BlockSpec((own, tile), column),
            pl.BlockSpec((devices, extra, tile), lambda i: (0, 0, i)),
        ],
        out_specs=[out, out],
        out_shape=[shape, shape],
        scratch_shapes=[
            pltpu.VMEM((width, all_rows), BF16),
            pltpu.VMEM((width, own), BF16),
            pltpu.VMEM((width, tile), F32),
        ],
        compiler_params=params(),
        cost_estimate=brief(),
        name="slabs",
    )(normed_all, query_grad, key_grad, value_grad, attended, branch_grad, tail)


def exchange(blocks):
    return lax.all_to_all(blocks, "exp", split_axis=0, concat_axis=0, tiled=True)


def body(
    tokens,
    w_query,
    w_key,
    w_value,
    w_out,
    w_router,
    gain_attn,
    gain_mlp,
    pos_bias,
    exp_gate,
    exp_up,
    exp_down,
    doc_lengths,
    bucket_of,
    expert_ids,
    cotangent,
):
    both = ("ctx", "exp")
    own_tokens = tokens[0]
    rows, width = own_tokens.shape
    experts = w_router.shape[1]
    capacity = (5 * TOP * rows + 4 * experts - 1) // (4 * experts)
    reach = (WINDOW + rows - 2) // rows
    scale = HEAD_DIM ** (-0.5)
    ctx_index, ctx_count = lax.axis_index("ctx"), lax.axis_size("ctx")
    exp_index = lax.axis_index("exp")
    part = w_query.shape[0]
    bias_part = pos_bias.shape[0]
    devices = width // part

    expert_range = jnp.arange(experts, dtype=jnp.int32)
    named = jnp.any(expert_ids[0][:, :, None] == expert_range, axis=1)
    named_low = named.astype(BF16)
    step = jnp.arange(rows, dtype=jnp.int32)
    earlier = (step[:, None] > step[None, :]).astype(BF16)
    slots = dot(earlier, named_low).astype(jnp.int32)
    slots = jnp.where(named, slots, -1).T
    routes = (slots[:, None, :] == jnp.arange(capacity, dtype=jnp.int32)[None, :, None]).astype(BF16)
    routes = routes.reshape(experts * capacity, rows)

    names = jnp.pad(named_low, ((0, 0), (0, LANES - experts)))
    early = dot(routes, jnp.concatenate([cotangent[0], names], axis=1)).astype(BF16)
    early = exchange(early.reshape(experts, capacity, width + LANES)).reshape(-1, width + LANES)

    held, share = exp_gate.shape[1], exp_down.shape[1]
    sizes = (share * 5 // 11, share * 6 // 11)
    packed, first = [], 0
    for size in sizes:
        columns = [slice(z * share + first, z * share + first + size) for z in range(ctx_count)]
        parts = [weight[0][:, at] for weight in (exp_gate, exp_up) for at in columns]
        packed.append(jnp.concatenate(parts + [pack_down(exp_down[0][first : first + size], held)], axis=1))
        first += size

    small = jnp.concatenate([w_router.reshape(-1), gain_attn, gain_mlp, pos_bias])
    small = jnp.pad(small, (0, width - small.shape[0]))[None]
    small = lax.all_gather(jnp.pad(small, ((0, 15), (0, 0))), both, axis=0)[:, 0]
    at = part * experts
    full_router = small[:, :at].reshape(width, experts)
    full_gain_attn = small[:, at : at + part].reshape(width).astype(F32)
    full_gain_mlp = small[:, at + part : at + 2 * part].reshape(width).astype(F32)
    table = small[:, at + 2 * part : at + 2 * part + bias_part].reshape(HEADS, BUCKETS)
    column = gather_ctx(jnp.concatenate([w_query, w_key, w_value, w_out], axis=0)[None])
    halo = [shift_ctx(own_tokens, 1), own_tokens]
    column, halo[0], early, packed[0] = together(column, halo[0], early, packed[0])
    for _ in range(1, reach):
        halo.insert(0, shift_ctx(halo[0], 1))
    onehot_bucket = (bucket_of[None, :] == jnp.arange(BUCKETS, dtype=jnp.int32)[:, None]).astype(BF16)
    band = make_band(dot(table, onehot_bucket))

    def then(others):
        *others, halo[0], packed[0] = together(*others, halo[0], packed[0])
        return others

    *halves, band = together(*spread_exp(column, then), band)
    chunk0 = lax.all_gather(packed[0], "ctx", axis=0, tiled=True)
    dense = spread_core(halves)
    full_query, full_key, full_value, full_out = (join_weights(dense, i * part, part) for i in range(4))
    tokens_all = jnp.concatenate(halo, axis=0)
    inputs_all = tokens_all.astype(F32)
    inputs = own_tokens.astype(F32)

    ends = jnp.cumsum(doc_lengths[0])

    def documents(positions):
        return jnp.sum((positions[:, None] >= ends[None, :]).astype(jnp.int32), axis=1)[:, None]

    feature = (jnp.arange(2 * HEAD_DIM, dtype=jnp.int32) % HEAD_DIM)[None, :]
    docs = doc_lengths.shape[1] + 1
    query_pos = ctx_index * rows + step
    key_pos = (ctx_index - reach) * rows + jnp.arange((reach + 1) * rows, dtype=jnp.int32)
    query_doc = (feature == documents(query_pos)).astype(BF16)
    same = (feature == documents(key_pos)) & (key_pos[:, None] >= 0)
    key_doc = jnp.where(same | (feature >= docs), 0.0, NEGATIVE).astype(BF16)

    normed_all = norm_rows(inputs_all, full_gain_attn).astype(BF16)
    normed = normed_all[reach * rows :]
    queries = (dot(normed, full_query).astype(BF16)) * jnp.asarray(scale, BF16)
    keys = dot(normed_all, full_key).astype(BF16)
    values = dot(normed_all, full_value).astype(BF16)
    attended, lse = attend(queries, keys, values, query_doc, key_doc, band)
    middle = inputs + dot(attended, full_out)
    normed_mlp = norm_rows(middle, full_gain_mlp).astype(BF16)

    sent = dot(routes, normed_mlp).astype(BF16)
    arrived = exchange(sent.reshape(experts, capacity, width)).reshape(-1, width)
    router_turned = jnp.pad(full_router.T, ((0, LANES - experts), (0, 0)))
    extras = (early, router_turned)
    units0, units1 = (size * ctx_count for size in sizes)
    arrived, packed[1], chunk0 = together(arrived, packed[1], chunk0)
    up, down = gather_hop(packed[1], packed[1], 1)
    hidden, dboth, carried, _ = run_expert(True, False, units0, ctx_count, arrived, [chunk0], extras, None)
    grad0 = expert_weights(units0, ctx_count, arrived, carried[0], dboth, hidden)
    pieces, sent = [packed[1]], (None, None)
    probs = make_probs(queries, keys, query_doc, key_doc, band, lse)
    for hop in range(1, ctx_count):
        if hop == 1:
            up, down, grad0 = together(up, down, grad0)
            parts0 = grad0.reshape(ctx_count, held, -1)
        else:
            up, down = gather_hop(up, down, hop)
            sent = scatter_hop(*scatter_add(parts0, hop - 1, *sent), hop - 1)
            up, down, probs, *sent = together(up, down, probs, *sent)
        pieces += [up, down]
    arrived, *sent = together(arrived, *scatter_add(parts0, ctx_count - 1, *sent))
    sent = scatter_hop(*sent, ctx_count - 1)
    hidden, dboth, carried, router_grad = run_expert(
        False, True, units1, ctx_count, arrived, pieces, extras, carried
    )
    low, made, back, _ = carried
    hidden, dboth, low, made, back, *sent = together(hidden, dboth, low, made, back, *sent)
    grad1 = expert_weights(units1, ctx_count, arrived, low, dboth, hidden, True)
    back, grad1 = together(back, grad1)
    total1 = lax.psum_scatter(grad1, "ctx", scatter_dimension=0, tiled=True)
    back = exchange(back.reshape(experts, capacity, width)).reshape(-1, width)

    upstream = cotangent[0].astype(F32)
    normed_mlp_grad = dot_rows(routes, back)
    _, second_pull = jax.vjp(norm_rows, middle, full_gain_mlp)
    middle_norm_grad, gain_mlp_grad = second_pull(normed_mlp_grad)
    middle_grad = upstream + middle_norm_grad
    branch_grad = middle_grad.astype(BF16)
    attended_grad = dot_last(branch_grad, full_out).astype(BF16)
    made, attended_grad = together(made, attended_grad)
    made = exchange(made.reshape(experts, capacity, width)).reshape(-1, width)
    query_grad, key_grad, value_grad, dist_grad = attend_back(
        queries, keys, values, attended_grad, attended, probs
    )
    bias_grad = jnp.dot(
        dist_grad.reshape(HEADS, WINDOW), onehot_bucket.T.astype(F32), precision=lax.Precision.HIGHEST
    )

    halo_grad, own_grad, gain_attn_grad = normed_grad_of(
        tokens_all, query_grad, key_grad, value_grad, full_query, full_key, full_value
    )
    gain_attn_grad = jnp.sum(gain_attn_grad, axis=0)

    tail = jnp.concatenate(
        [
            router_grad[:, :experts].reshape(devices, -1),
            gain_attn_grad.reshape(devices, part),
            gain_mlp_grad.reshape(devices, part),
            bias_grad.reshape(devices, bias_part),
        ],
        axis=1,
    ).astype(BF16)
    tail = jnp.pad(tail[:, None, :], ((0, 0), (0, 15), (0, width - tail.shape[1])))
    query_grad, made = together(query_grad, made)
    output = (middle + dot_rows(routes, made)).astype(BF16)
    keep, send = make_slabs(normed_all, query_grad, key_grad, value_grad, attended, branch_grad, tail)
    other = swap_exp(send, 1)
    parts = scatter_exp(keep, other)
    pieces = [halo_grad[place * rows : (place + 1) * rows] for place in range(reach)]
    returning = shift_ctx(pieces[0], -1)
    for piece in pieces[1:]:
        parts, returning, output = together(parts, returning, output)
        returning = shift_ctx((piece.astype(F32) + returning.astype(F32)).astype(BF16), -1)
    own0 = lax.dynamic_index_in_dim(parts0, ctx_index, 0, keepdims=False)
    expert_grads = expert_sums(sizes, ctx_count, own0, *sent, total1)
    sent = (None, None)
    for hop in range(1, ctx_count):
        sent = scatter_add(parts, hop, *sent)
        sent = scatter_hop(*sent, hop)
        if hop == min(2, ctx_count - 1):
            *sent, grad_gate, grad_up, grad_down = together(*sent, *expert_grads)
    sums = scatter_end(parts, *sent)
    _, own_pull = jax.vjp(norm_rows, inputs, full_gain_attn)
    input_grad = middle_grad + own_pull(own_grad + returning.astype(F32))[0]
    tail = sums[4 * part]
    at = part * experts
    return (
        output[None],
        input_grad[None],
        sums[:part],
        sums[part : 2 * part],
        sums[2 * part : 3 * part],
        sums[3 * part : 4 * part],
        tail[:at].reshape(part, experts),
        tail[at : at + part],
        tail[at + part : at + 2 * part],
        tail[at + 2 * part : at + 2 * part + bias_part],
        grad_gate[None],
        grad_up[None],
        grad_down[None],
    )


def solution(mesh):
    rows3 = P("exp", "ctx", None)
    dense2 = P(("ctx", "exp"), None)
    dense1 = P(("ctx", "exp"))
    return jax.shard_map(
        body,
        mesh=mesh,
        in_specs=(
            rows3,
            dense2,
            dense2,
            dense2,
            dense2,
            dense2,
            dense1,
            dense1,
            dense1,
            rows3,
            rows3,
            rows3,
            P("exp", None),
            P(),
            rows3,
            rows3,
        ),
        out_specs=(
            rows3,
            rows3,
            dense2,
            dense2,
            dense2,
            dense2,
            dense2,
            dense1,
            dense1,
            dense1,
            rows3,
            rows3,
            rows3,
        ),
        check_vma=False,
    )
```

```python
import functools

import jax
import jax.numpy as jnp
from jax import lax
from jax.experimental import pallas as pl
from jax.experimental.pallas import tpu as pltpu
from jax.sharding import PartitionSpec as P

HEADS = 16
HEAD_DIM = 64
BUCKETS = 32
TOP = 2
WINDOW = 1024

EPSILON = 1e-06
NEGATIVE = -1e30
LANES = 128
CHUNK = 256
FF_TILE = 512
ROW_TILE = 256
VMEM_LIMIT = 58 * 2**20
BF16 = jnp.bfloat16
F32 = jnp.float32


def shift_ctx(block, distance):
    devices = range(lax.axis_size("ctx"))
    route = [(i - distance, i) for i in devices if i - distance in devices]
    return lax.ppermute(block, "ctx", route)


def norm_rows(values, gain):
    return values * lax.rsqrt(jnp.mean(values * values, axis=-1, keepdims=True) + EPSILON) * gain


def dot(left, right):
    return jnp.dot(left, right, preferred_element_type=F32)


def dot_rows(left, right):
    return lax.dot_general(left, right, (((0,), (0,)), ((), ())), preferred_element_type=F32)


def dot_last(left, right):
    return lax.dot_general(left, right, (((1,), (1,)), ((), ())), preferred_element_type=F32)


def params(**more):
    return pltpu.CompilerParams(vmem_limit_bytes=VMEM_LIMIT, **more)


def brief():
    return pl.CostEstimate(flops=2**20, bytes_accessed=2**20, transcendentals=0)


def band_kernel(bias_ref, band_ref):
    blocks = WINDOW // LANES
    size = (blocks + 2) * LANES
    for head in range(bias_ref.shape[0]):
        row = jnp.broadcast_to(bias_ref[head : head + 1, :], (8, size))
        eight = pltpu.roll(row, 0, 1, stride=1, stride_axis=0)
        for group in range(LANES // 8):
            wide = pltpu.roll(eight, 8 * group, 1) if group else eight
            for a in range(blocks + 1):
                first = a * LANES + group * 8
                at = (blocks + 1 - a) * LANES
                band_ref[head, first : first + 8, :] = wide[:, at : at + LANES]


def make_band(bias_dist):
    group = 8
    edge = jnp.full((HEADS, LANES), NEGATIVE, F32)
    padded = jnp.concatenate([edge, bias_dist, edge], axis=1)
    return pl.pallas_call(
        band_kernel,
        grid=(HEADS // group,),
        in_specs=[pl.BlockSpec((group, WINDOW + 2 * LANES), lambda h: (h, 0))],
        out_specs=pl.BlockSpec((group, WINDOW + LANES, LANES), lambda h: (h, 0, 0)),
        out_shape=jax.ShapeDtypeStruct((HEADS, WINDOW + LANES, LANES), F32),
        compiler_params=params(),
        cost_estimate=brief(),
        name="bias_band",
    )(padded)


def sum_band(band_ref):
    blocks = WINDOW // LANES
    size = (blocks + 2) * LANES
    row = lax.broadcasted_iota(jnp.int32, (8, 1), 0)
    edge = jnp.zeros((8, LANES), F32)
    total = None
    for group in range(LANES // 8):
        pieces = [edge]
        for a in range(blocks, -1, -1):
            first = a * LANES + group * 8
            pieces.append(band_ref[first : first + 8, :])
        wide = jnp.concatenate(pieces, axis=1)
        if group:
            wide = pltpu.roll(wide, size - 8 * group, 1)
        total = wide if total is None else total + wide
    dist = jnp.zeros_like(total)
    for r in range(8):
        turned = pltpu.roll(total, size - r, 1) if r else total
        dist = dist + jnp.where(row == r, turned, 0.0)
    return jnp.sum(dist, axis=0, keepdims=True)[:, LANES : LANES + WINDOW]


def head_lanes(head):
    lane = lax.broadcasted_iota(jnp.int32, (1, 2 * HEAD_DIM), 1)
    return (lane >= head * HEAD_DIM) & (lane < (head + 1) * HEAD_DIM)


def masked_scores(head, start, q_ref, k_ref, qdoc_ref, kdoc_ref):
    span = WINDOW + CHUNK
    mine = head_lanes(head)
    q_rows, k_rows = pl.ds(start, CHUNK), pl.ds(start, span)
    q_part = jnp.where(mine, q_ref[q_rows, :], qdoc_ref[q_rows, :])
    k_part = jnp.where(mine, k_ref[k_rows, :], kdoc_ref[k_rows, :])
    return dot_last(k_part, q_part)


def sub_blocks():
    return [(s * LANES, WINDOW + LANES) for s in range(CHUNK // LANES)]


def spread(parts):
    span = WINDOW + CHUNK
    columns = []
    for (first, rows), part in zip(sub_blocks(), parts):
        pieces = []
        if first:
            pieces.append(jnp.zeros((first, LANES), part.dtype))
        pieces.append(part)
        if span - first - rows:
            pieces.append(jnp.zeros((span - first - rows, LANES), part.dtype))
        columns.append(jnp.concatenate(pieces, axis=0) if len(pieces) > 1 else part)
    return jnp.concatenate(columns, axis=1)


def attend_kernel(q_ref, k_ref, v_ref, qdoc_ref, kdoc_ref, band_ref, o_ref, lse_ref):
    span = WINDOW + CHUNK
    for start in range(0, q_ref.shape[0], CHUNK):
        v_turned = v_ref[pl.ds(start, span), :].T
        outs = []
        for head in range(2):
            scores = masked_scores(head, start, q_ref, k_ref, qdoc_ref, kdoc_ref)
            band = band_ref[head]
            low, scale, logs = [], [], []
            for s, (first, rows) in enumerate(sub_blocks()):
                part = scores[first : first + rows, s * LANES : (s + 1) * LANES] + band
                top = jnp.max(part, axis=0, keepdims=True)
                expo = jnp.exp(part - top)
                total = jnp.sum(expo, axis=0, keepdims=True)
                low.append(expo.astype(BF16))
                scale.append(1.0 / total)
                logs.append(top + jnp.log(total))
            out = dot(v_turned[head * HEAD_DIM : (head + 1) * HEAD_DIM], spread(low))
            outs.append(out * jnp.concatenate(scale, axis=1))
            lse_ref[0, head : head + 1, pl.ds(start, CHUNK)] = jnp.concatenate(logs, axis=1)
        o_ref[pl.ds(start, CHUNK), :] = jnp.concatenate(outs, axis=0).T.astype(BF16)


def attend(queries, keys, values, query_doc, key_doc, band):
    rows, width = queries.shape
    keys_rows = keys.shape[0]
    pairs = HEADS // 2
    wide = 2 * HEAD_DIM
    return pl.pallas_call(
        attend_kernel,
        grid=(pairs,),
        in_specs=[
            pl.BlockSpec((rows, wide), lambda p: (0, p)),
            pl.BlockSpec((keys_rows, wide), lambda p: (0, p)),
            pl.BlockSpec((keys_rows, wide), lambda p: (0, p)),
            pl.BlockSpec((rows, wide), lambda p: (0, 0)),
            pl.BlockSpec((keys_rows, wide), lambda p: (0, 0)),
            pl.BlockSpec((2, WINDOW + LANES, LANES), lambda p: (p, 0, 0)),
        ],
        out_specs=[
            pl.BlockSpec((rows, wide), lambda p: (0, p)),
            pl.BlockSpec((1, 2, rows), lambda p: (p, 0, 0)),
        ],
        out_shape=[
            jax.ShapeDtypeStruct((rows, width), BF16),
            jax.ShapeDtypeStruct((pairs, 2, rows), F32),
        ],
        compiler_params=params(),
        cost_estimate=brief(),
        name="attend",
    )(queries, keys, values, query_doc, key_doc, band)


def probs_kernel(q_ref, k_ref, qdoc_ref, kdoc_ref, band_ref, lse_ref, probs_ref):
    for chunk in range(q_ref.shape[0] // CHUNK):
        start = chunk * CHUNK
        for head in range(2):
            scores = masked_scores(head, start, q_ref, k_ref, qdoc_ref, kdoc_ref)
            band = band_ref[head]
            lse = lse_ref[0, head : head + 1, pl.ds(start, CHUNK)]
            parts = []
            for s, (first, rows) in enumerate(sub_blocks()):
                lanes = slice(s * LANES, (s + 1) * LANES)
                parts.append(jnp.exp(scores[first : first + rows, lanes] + band - lse[:, lanes]).astype(BF16))
            probs_ref[head, chunk] = spread(parts)


def make_probs(queries, keys, query_doc, key_doc, band, lse):
    rows, width = queries.shape
    keys_rows = keys.shape[0]
    pairs = HEADS // 2
    wide = 2 * HEAD_DIM
    span, chunks = WINDOW + CHUNK, rows // CHUNK
    return pl.pallas_call(
        probs_kernel,
        grid=(pairs,),
        in_specs=[
            pl.BlockSpec((rows, wide), lambda p: (0, p)),
            pl.BlockSpec((keys_rows, wide), lambda p: (0, p)),
            pl.BlockSpec((rows, wide), lambda p: (0, 0)),
            pl.BlockSpec((keys_rows, wide), lambda p: (0, 0)),
            pl.BlockSpec((2, WINDOW + LANES, LANES), lambda p: (p, 0, 0)),
            pl.BlockSpec((1, 2, rows), lambda p: (p, 0, 0)),
        ],
        out_specs=pl.BlockSpec((2, chunks, span, CHUNK), lambda p: (p, 0, 0, 0)),
        out_shape=jax.ShapeDtypeStruct((HEADS, chunks, span, CHUNK), BF16),
        compiler_params=params(),
        cost_estimate=brief(),
        name="probs",
    )(queries, keys, query_doc, key_doc, band, lse)


def attend_back_kernel(
    q_ref, k_ref, v_ref, g_ref, o_ref, probs_ref, dq_ref, dk_ref, dv_ref, dist_ref, dk_sum, dv_sum, dband
):
    span = WINDOW + CHUNK
    dk_sum[...] = jnp.zeros_like(dk_sum)
    dv_sum[...] = jnp.zeros_like(dv_sum)
    for chunk in range(q_ref.shape[0] // CHUNK):
        start = chunk * CHUNK
        q_rows, k_rows = pl.ds(start, CHUNK), pl.ds(start, span)
        k_turned = k_ref[k_rows, :].T
        product = (g_ref[q_rows, :].astype(F32) * o_ref[q_rows, :].astype(F32)).T
        dq_parts = []
        for head in range(2):
            mine = head_lanes(head)
            zero = jnp.zeros((), BF16)
            g_part = jnp.where(mine, g_ref[q_rows, :], zero)
            q_part = jnp.where(mine, q_ref[q_rows, :], zero)
            prob_grad = dot_last(v_ref[k_rows, :], g_part)
            delta = jnp.sum(product[head * HEAD_DIM : (head + 1) * HEAD_DIM], axis=0, keepdims=True)
            grad_low, grad_sum = [], None
            for s, (first, rows) in enumerate(sub_blocks()):
                lanes = slice(s * LANES, (s + 1) * LANES)
                probs = probs_ref[head, chunk, first : first + rows, lanes].astype(F32)
                grad = probs * (prob_grad[first : first + rows, lanes] - delta[:, lanes])
                grad_low.append(grad.astype(BF16))
                grad_sum = grad if grad_sum is None else grad_sum + grad
            if chunk == 0:
                dband[head] = grad_sum
            else:
                dband[head] = dband[head] + grad_sum
            grads = spread(grad_low)
            dk_sum[k_rows, :] += dot(grads, q_part)
            dv_sum[k_rows, :] += dot(probs_ref[head, chunk], g_part)
            dq_parts.append(dot(k_turned[head * HEAD_DIM : (head + 1) * HEAD_DIM], grads))
        turned = jnp.concatenate(dq_parts, axis=0).T
        dq_ref[q_rows, :] = (turned * HEAD_DIM ** (-0.5)).astype(BF16)
    dk_ref[...] = dk_sum[...].astype(BF16)
    dv_ref[...] = dv_sum[...].astype(BF16)
    for head in range(2):
        dist_ref[0, head : head + 1, :] = sum_band(dband.at[head])


def attend_back(queries, keys, values, grad, out, probs):
    rows, width = queries.shape
    keys_rows = keys.shape[0]
    pairs = HEADS // 2
    wide = 2 * HEAD_DIM
    q_spec = pl.BlockSpec((rows, wide), lambda p: (0, p))
    k_spec = pl.BlockSpec((keys_rows, wide), lambda p: (0, p))
    return pl.pallas_call(
        attend_back_kernel,
        grid=(pairs,),
        in_specs=[
            q_spec,
            k_spec,
            k_spec,
            q_spec,
            q_spec,
            pl.BlockSpec((2,) + probs.shape[1:], lambda p: (p, 0, 0, 0)),
        ],
        out_specs=[q_spec, k_spec, k_spec, pl.BlockSpec((1, 2, WINDOW), lambda p: (p, 0, 0))],
        out_shape=[
            jax.ShapeDtypeStruct((rows, width), BF16),
            jax.ShapeDtypeStruct((keys_rows, width), BF16),
            jax.ShapeDtypeStruct((keys_rows, width), BF16),
            jax.ShapeDtypeStruct((pairs, 2, WINDOW), F32),
        ],
        scratch_shapes=[
            pltpu.VMEM((keys_rows, wide), F32),
            pltpu.VMEM((keys_rows, wide), F32),
            pltpu.VMEM((2, WINDOW + LANES, LANES), F32),
        ],
        compiler_params=params(),
        cost_estimate=pl.CostEstimate(
            flops=20 * rows * WINDOW * width * 2, bytes_accessed=2**20, transcendentals=0
        ),
        name="attend_back",
    )(queries, keys, values, grad, out, probs)


def down_blocks(units, width, count):
    held, share = width // count, units // count
    extra = share - held
    wide = width * extra // held
    blocks = []
    for z in range(count):
        blocks.append(((z * held, 0), (z * share, 0), (held, width)))
        for m in range(held // extra):
            blocks.append(((z * held + m * extra, width), (z * share + held, m * wide), (extra, wide)))
    return blocks


def pack_down(down, held):
    extra, width = down.shape[0] - held, down.shape[1]
    wide = width * extra // held
    rest = [down[held:, m * wide : (m + 1) * wide] for m in range(held // extra)]
    return jnp.concatenate([down[:held], jnp.concatenate(rest, axis=0)], axis=1)


def unpack_down(packed, size, width):
    held = packed.shape[0]
    extra = size - held
    rest = [packed[m * extra : (m + 1) * extra, width:] for m in range(held // extra)]
    return jnp.concatenate([packed[:, :width], jnp.concatenate(rest, axis=1)], axis=0)


def expert_kernel(first, last, units, count, parts, *refs):
    refs = list(refs)
    take = lambda: refs.pop(0)
    x_ref = take()
    pieces = [take() for _ in range(parts)]
    if first or last:
        c_ref, names_ref, router_ref = take(), take(), take()
    if not first:
        low_ref, made_in, back_in = take(), take(), take()
    if last and not first:
        gate_in = take()
    hidden_ref, dboth_ref = take(), take()
    if first:
        low_out = take()
    if first and not last:
        gate_out = take()
    made_ref, back_ref = take(), take()
    if last:
        drouter_ref = take()
    chunk_ref, down_s, sems = take(), take(), take()
    rows, width = x_ref.shape
    held = width // count
    index = lax.axis_index("ctx")

    def slot(z):
        return chunk_ref.at[z * held : (z + 1) * held]

    @pl.when(pl.program_id(0) == 0)
    def _():
        if parts == 1:
            for z in range(count):
                pltpu.make_async_copy(pieces[0].at[z * held : (z + 1) * held], slot(z), sems.at[z]).start()
        for z in range(count if parts > 1 else 0):
            for here in range(count):
                hop = abs(here - z)
                source = pieces[0 if hop == 0 else 2 * hop - 1 if z < here else 2 * hop]

                @pl.when(index == here)
                def _(source=source, z=z):
                    pltpu.make_async_copy(source, slot(z), sems.at[z]).start()

        for z in range(count):
            pltpu.make_async_copy(pieces[0].at[:held], slot(z), sems.at[z]).wait()

    x = x_ref[...]
    own = lax.broadcasted_iota(jnp.int32, (1, LANES), 1) == lax.axis_index("exp")
    if first:
        names = names_ref[...].astype(F32)
        logits = dot_last(x, router_ref[...]) * names
        mine = jnp.sum(jnp.where(own, logits, 0.0), axis=1, keepdims=True)
        theirs = jnp.sum(jnp.where(own, 0.0, logits), axis=1, keepdims=True)
        gate = jax.nn.sigmoid(mine - theirs)
        low_out[...] = (gate * c_ref[...].astype(F32)).astype(BF16)
        if not last:
            gate_out[...] = jnp.broadcast_to(gate, (rows, LANES))
        low_ref = low_out
    elif last:
        gate = gate_in[...][:, :1]
    @pl.when(pl.program_id(0) == 0)
    def _():
        for (row, column), (to_row, to_column), (high, wide) in down_blocks(units, width, count):
            from_columns = slice(2 * units + column, 2 * units + column + wide)
            down_s[to_row : to_row + high, to_column : to_column + wide] = chunk_ref[row : row + high, from_columns]

    for start in range(0, units, FF_TILE):
        stop = min(start + FF_TILE, units)
        at, up_at = slice(start, stop), slice(units + start, units + stop)
        gate_pre = dot(x, chunk_ref[:, at])
        up_pre = dot(x, chunk_ref[:, up_at])
        hidden_grad = dot_last(low_ref[...], down_s[at, :])
        root = 0.7978845608028654
        square = gate_pre * gate_pre
        bent = jnp.tanh(gate_pre * (root + root * 0.044715 * square))
        half = 0.5 * (1.0 + bent)
        act = gate_pre * half
        slope = half + 0.5 * gate_pre * (1.0 - bent * bent) * (root + 3.0 * root * 0.044715 * square)
        hidden_ref[:, at] = (act * up_pre).astype(BF16)
        dboth_ref[:, at] = (hidden_grad * up_pre * slope).astype(BF16)
        dboth_ref[:, up_at] = (hidden_grad * act).astype(BF16)
    made = dot(hidden_ref[...], down_s[...])
    back = dot_last(dboth_ref[...], chunk_ref[:, : 2 * units])
    if not first:
        made = made + made_in[...]
        back = back + back_in[...]
    if last:
        made = made.astype(BF16).astype(F32)
        names = names_ref[...].astype(F32)
        push = jnp.sum(c_ref[...].astype(F32) * made, axis=1, keepdims=True)
        push = push * gate * (1.0 - gate)
        logits_grad = push * jnp.where(own, names, -names)
        high = logits_grad.astype(BF16)
        low = (logits_grad - high.astype(F32)).astype(BF16)
        made = gate * made
        back = back + dot(high, router_ref[...]) + dot(low, router_ref[...])
        turned = x.T
        update = dot(turned, high) + dot(turned, low)

        @pl.when(pl.program_id(0) == 0)
        def _():
            drouter_ref[...] = update

        @pl.when(pl.program_id(0) > 0)
        def _():
            drouter_ref[...] += update

    made_ref[...] = made.astype(made_ref.dtype)
    back_ref[...] = back.astype(back_ref.dtype)


def run_expert(first, last, units, count, x, pieces, extras, carried):
    rows, width = x.shape
    whole = lambda i: (0, 0)
    step = lambda i: (i, 0)
    wide = pl.BlockSpec((ROW_TILE, width), step)
    thin = pl.BlockSpec((ROW_TILE, LANES), step)
    struct = jax.ShapeDtypeStruct
    early, router = extras
    operands = [x] + pieces
    in_specs = [wide] + [pl.BlockSpec(memory_space=pl.ANY)] * len(pieces)
    if first or last:
        operands += [early, early, router]
        names = pl.BlockSpec((ROW_TILE, LANES), lambda i: (i, width // LANES))
        in_specs += [wide, names, pl.BlockSpec((LANES, width), whole)]
    if not first:
        low, made, back, gate = carried
        operands += [low, made, back]
        in_specs += [wide, wide, wide]
        if last:
            operands.append(gate)
            in_specs.append(thin)
    out_shape = [struct((rows, units), BF16), struct((rows, 2 * units), BF16)]
    out_specs = [pl.BlockSpec((ROW_TILE, units), step), pl.BlockSpec((ROW_TILE, 2 * units), step)]
    if first:
        out_shape.append(struct((rows, width), BF16))
        out_specs.append(wide)
        if not last:
            out_shape.append(struct((rows, LANES), F32))
            out_specs.append(thin)
    kept = BF16 if last else F32
    out_shape += [struct((rows, width), kept), struct((rows, width), kept)]
    out_specs += [wide, wide]
    if last:
        out_shape.append(struct((width, LANES), F32))
        out_specs.append(pl.BlockSpec((width, LANES), whole))
    outs = list(
        pl.pallas_call(
            functools.partial(expert_kernel, first, last, units, count, len(pieces)),
            grid=(rows // ROW_TILE,),
            in_specs=in_specs,
            out_specs=out_specs,
            out_shape=out_shape,
            scratch_shapes=[
                pltpu.VMEM((width, pieces[0].shape[1]), BF16),
                pltpu.VMEM((units, width), BF16),
                pltpu.SemaphoreType.DMA((count,)),
            ],
            compiler_params=params(),
            cost_estimate=brief(),
            name="expert",
        )(*operands)
    )
    hidden, dboth = outs[:2]
    if first:
        low = outs[2]
        gate = None if last else outs[3]
    if last:
        made, back, drouter = outs[-3:]
        return hidden, dboth, (low, made, back, gate), drouter
    made, back = outs[-2:]
    return hidden, dboth, (low, made, back, gate), None


def expert_weights_kernel(
    units, count, x_ref, low_ref, dboth_ref, hidden_ref, grad_ref, x_turned, hidden_turned, rest
):
    step = pl.program_id(0)
    tile = low_ref.shape[1]
    width = x_ref.shape[1]
    both_steps, down_steps = 2 * units // tile, width // tile

    @pl.when(step == 0)
    def _():
        x_turned[...] = x_ref[...].T

    @pl.when(step < both_steps)
    def _():
        grad_ref[...] = dot(x_turned[...], dboth_ref[...]).astype(BF16)

    @pl.when(step == both_steps)
    def _():
        hidden_turned[...] = hidden_ref[...].T

    for place in range(down_steps):

        @pl.when(step == both_steps + place)
        def _(place=place):
            total = dot(hidden_turned[...], low_ref[...]).astype(BF16)
            first = place * tile
            for (row, column), (from_row, from_column), (high, wide) in down_blocks(units, width, count):
                if column == 0:
                    grad_ref[row : row + high, :] = total[from_row : from_row + high]
                    continue
                low, top = max(first, from_column), min(first + tile, from_column + wide)
                if low < top:
                    rest[row : row + high, low - from_column : top - from_column] = total[
                        from_row : from_row + high, low - first : top - first
                    ]

    for place in range(rest.shape[1] // tile):

        @pl.when(step == both_steps + down_steps + place)
        def _(place=place):
            grad_ref[...] = rest[:, place * tile : (place + 1) * tile]


def expert_weights(units, count, x, low, dboth, hidden, long=False):
    rows, width = x.shape
    tile = 512
    extra_steps = -(-(units - width) // tile)
    both_steps, down_steps = 2 * units // tile, width // tile
    whole = lambda i: (0, 0)
    work = pl.CostEstimate(flops=6 * rows * width * units, bytes_accessed=2**20, transcendentals=0)
    return pl.pallas_call(
        functools.partial(expert_weights_kernel, units, count),
        grid=(both_steps + down_steps + extra_steps,),
        in_specs=[
            pl.BlockSpec((rows, width), whole),
            pl.BlockSpec((rows, tile), lambda i: (0, jnp.clip(i - both_steps, 0, down_steps - 1))),
            pl.BlockSpec((rows, tile), lambda i: (0, jnp.minimum(i, both_steps - 1))),
            pl.BlockSpec((rows, units), whole),
        ],
        out_specs=pl.BlockSpec((width, tile), lambda i: (0, i)),
        out_shape=jax.ShapeDtypeStruct((width, 3 * units), BF16),
        scratch_shapes=[
            pltpu.VMEM((width, rows), BF16),
            pltpu.VMEM((units, rows), BF16),
            pltpu.VMEM((width, extra_steps * tile), BF16),
        ],
        compiler_params=params(),
        cost_estimate=work if long else brief(),
        name="expert_weights",
    )(x, low, dboth, hidden)


def expert_sums_kernel(sizes, count, own_ref, up_ref, down_ref, last_ref, gate_out, up_out, down_out):
    held, width = own_ref.shape[0], down_out.shape[1]
    extras = [size - held for size in sizes]
    tile = min(extras)
    for first in range(0, held, tile):
        rows = slice(first, first + tile)
        totals = (
            own_ref[rows, :].astype(F32) + up_ref[rows, :].astype(F32) + down_ref[rows, :].astype(F32),
            last_ref[rows, :].astype(F32),
        )
        for out, part in ((gate_out, 0), (up_out, 1)):
            pieces = []
            for z in range(count):
                for size, total in zip(sizes, totals):
                    at = part * size * count + z * size
                    pieces.append(total[:, at : at + size])
            out[rows, :] = jnp.concatenate(pieces, axis=1)
        start = 0
        for size, extra, total in zip(sizes, extras, totals):
            wide = width * extra // held
            at = 2 * size * count
            down_out[start + first : start + first + tile, :] = total[:, at : at + width]
            to, columns = start + held + first % extra, first // extra * wide
            down_out[to : to + tile, columns : columns + wide] = total[:, at + width :]
            start += size


def expert_sums(sizes, count, own, up, down, last):
    held = own.shape[0]
    units = sum(sizes)
    struct = jax.ShapeDtypeStruct
    width = held * count
    return pl.pallas_call(
        functools.partial(expert_sums_kernel, sizes, count),
        in_specs=[pl.BlockSpec(memory_space=pltpu.VMEM)] * 4,
        out_specs=[pl.BlockSpec(memory_space=pltpu.VMEM)] * 3,
        out_shape=[
            struct((held, units * count), F32),
            struct((held, units * count), F32),
            struct((units, width), F32),
        ],
        compiler_params=params(),
        cost_estimate=brief(),
        name="expert_sums",
    )(own, up, down, last)


def ctx_moves(distance):
    devices = range(lax.axis_size("ctx"))
    return [(i - distance, i) for i in devices if i - distance in devices]


def together(*values):
    return lax.optimization_barrier(values)


def gather_ctx(piece):
    count, index, size = lax.axis_size("ctx"), lax.axis_index("ctx"), piece.shape[0]
    full = jnp.zeros((count * size,) + piece.shape[1:], piece.dtype)
    place = lambda buffer, part, at: lax.dynamic_update_slice_in_dim(buffer, part, at * size, 0)
    full = place(full, piece, index)
    up = down = piece
    for hop in range(1, count):
        up, down = shift_ctx(up, 1), shift_ctx(down, -1)
        for part, at, held in ((up, index - hop, index >= hop), (down, index + hop, index + hop < count)):
            at = jnp.clip(at, 0, count - 1)
            old = lax.dynamic_slice_in_dim(full, at * size, size, 0)
            full = place(full, jnp.where(held, part, old), at)
    return full


def gather_hop(up, down, hop):
    count = lax.axis_size("ctx")
    route = [(i, i + 1) for i in range(hop - 1, count - 1)]
    back = [(count - 1 - i, count - 1 - j) for i, j in route]
    return lax.ppermute(up, "ctx", route), lax.ppermute(down, "ctx", back)


def scatter_add(parts, hop, up=None, down=None):
    count, index = lax.axis_size("ctx"), lax.axis_index("ctx")

    def part(at):
        return lax.dynamic_index_in_dim(parts, jnp.clip(at, 0, count - 1), 0, keepdims=False).astype(F32)

    distance = count - hop
    mine_up, mine_down = part(index + distance), part(index - distance)
    if up is not None:
        mine_up, mine_down = mine_up + up.astype(F32), mine_down + down.astype(F32)
    return mine_up.astype(BF16), mine_down.astype(BF16)


def scatter_hop(up, down, hop):
    count = lax.axis_size("ctx")
    route = [(i, i + 1) for i in range(hop)]
    back = [(count - 1 - i, count - 1 - j) for i, j in route]
    return lax.ppermute(up, "ctx", route), lax.ppermute(down, "ctx", back)


def scatter_end(parts, up, down):
    own = lax.dynamic_index_in_dim(parts, lax.axis_index("ctx"), 0, keepdims=False).astype(F32)
    return own + up.astype(F32) + down.astype(F32)


def swap_exp(block, bit):
    return lax.ppermute(block, "exp", [(i, i ^ bit) for i in range(lax.axis_size("exp"))])


def bit_set(bit):
    return (lax.axis_index("exp") // bit) % 2 == 1


def exp_bits():
    size, bits = lax.axis_size("exp"), []
    while 1 << len(bits) < size:
        bits.append(1 << len(bits))
    return bits


def routes_exp():
    bits = exp_bits()
    return bits[1:], bits[:0:-1]


def spread_exp(column, then):
    count = column.shape[0]
    halves = [column[None, : count // 2], column[None, count // 2 :]]
    for step, bits in enumerate(zip(*routes_exp())):
        others = [swap_exp(half, bit) for half, bit in zip(halves, bits)]
        if step == 0:
            others = then(others)
        for place, (half, other, bit) in enumerate(zip(halves, others, bits)):
            halves[place] = jnp.where(
                bit_set(bit), jnp.concatenate([other, half]), jnp.concatenate([half, other])
            )
    return halves


def spread_core(halves):
    bits = exp_bits()
    done = []
    for half, order in zip(halves, routes_exp()):
        other = swap_exp(half, 1)
        mine_first = bit_set(1)
        pair = jnp.stack([jnp.where(mine_first, other, half), jnp.where(mine_first, half, other)])
        pair = pair.reshape((2,) + (2,) * len(order) + half.shape[1:])
        axes = [1 + order[::-1].index(bit) for bit in bits[:0:-1]] + [0]
        axes = [len(axes)] + axes + list(range(len(axes) + 1, pair.ndim))
        pair = pair.transpose(axes)
        done.append(pair.reshape((half.shape[1], 1 << len(bits)) + half.shape[2:]))
    return done


def join_weights(done, first, rows):
    width = done[0].shape[-1]
    return jnp.concatenate([half[:, :, first : first + rows].reshape(-1, width) for half in done])


def scatter_exp(keep, other):
    count, bits = lax.axis_size("ctx"), exp_bits()
    chip = (keep.astype(F32) + other.astype(F32)).astype(BF16)
    chip = chip.reshape((count, -1) + chip.shape[1:])
    sums = []
    for half, order in zip((chip[: count // 2], chip[count // 2 :]), routes_exp()):
        half = half.reshape((count // 2,) + (2,) * (len(bits) - 1) + half.shape[2:])
        left = bits[:0:-1]
        for bit in order:
            axis = 1 + left.index(bit)
            low = lax.index_in_dim(half, 0, axis, keepdims=False)
            high = lax.index_in_dim(half, 1, axis, keepdims=False)
            keep = jnp.where(bit_set(bit), high, low)
            send = jnp.where(bit_set(bit), low, high)
            half = (keep.astype(F32) + swap_exp(send, bit).astype(F32)).astype(BF16)
            left = [b for b in left if b != bit]
        sums.append(half)
    return jnp.concatenate(sums)


def normed_grad_kernel(
    halo_steps, x_ref, q_ref, k_ref, v_ref, wq_ref, wk_ref, wv_ref, halo_ref, own_ref, gain_ref, total
):
    step = pl.program_id(0)
    total[...] = dot_last(k_ref[...], wk_ref[...]) + dot_last(v_ref[...], wv_ref[...])

    @pl.when(step >= halo_steps)
    def _():
        total[...] += dot_last(q_ref[...], wq_ref[...])
        own_ref[...] = total[...]

    @pl.when(step < halo_steps)
    def _():
        halo_ref[...] = total[...].astype(BF16)

    x = x_ref[...].astype(F32)
    unit = x * lax.rsqrt(jnp.mean(x * x, axis=1, keepdims=True) + EPSILON)
    update = jnp.sum((total[...] * unit).reshape(-1, 8, x.shape[1]), axis=0)

    @pl.when(step == 0)
    def _():
        gain_ref[...] = update

    @pl.when(step > 0)
    def _():
        gain_ref[...] += update


def normed_grad_of(inputs_all, query_grad, key_grad, value_grad, full_query, full_key, full_value):
    all_rows, width = key_grad.shape
    own = query_grad.shape[0]
    tile = 256
    halo_steps = (all_rows - own) // tile
    row = lambda i: (i, 0)
    late = lambda i: (jnp.maximum(i - halo_steps, 0), 0)
    whole = lambda i: (0, 0)
    block = (tile, width)
    weight = pl.BlockSpec((width, width), whole, pipeline_mode=pl.Buffered(1))
    return pl.pallas_call(
        functools.partial(normed_grad_kernel, halo_steps),
        grid=(all_rows // tile,),
        in_specs=[
            pl.BlockSpec(block, row),
            pl.BlockSpec(block, late),
            pl.BlockSpec(block, row),
            pl.BlockSpec(block, row),
            weight,
            weight,
            weight,
        ],
        out_specs=[
            pl.BlockSpec(block, lambda i: (jnp.minimum(i, halo_steps - 1), 0)),
            pl.BlockSpec(block, late),
            pl.BlockSpec((8, width), whole),
        ],
        out_shape=[
            jax.ShapeDtypeStruct((all_rows - own, width), BF16),
            jax.ShapeDtypeStruct((own, width), F32),
            jax.ShapeDtypeStruct((8, width), F32),
        ],
        scratch_shapes=[pltpu.VMEM(block, F32)],
        compiler_params=params(),
        cost_estimate=brief(),
        name="normed_grad",
    )(inputs_all, query_grad, key_grad, value_grad, full_query, full_key, full_value)


def slab_kernel(part, x_ref, q_ref, k_ref, v_ref, o_ref, g_ref, tail_ref, keep_ref, send_ref, x_turned, o_turned, total):
    core = lax.rem(lax.axis_index("exp"), 2)
    own = q_ref.shape[0]

    @pl.when(pl.program_id(0) == 0)
    def _():
        x_turned[...] = x_ref[...].T
        o_turned[...] = o_ref[...].T

    for place, (left, right) in enumerate(
        (
            (x_turned[:, x_turned.shape[1] - own :], q_ref[...]),
            (x_turned[...], k_ref[...]),
            (x_turned[...], v_ref[...]),
            (o_turned[...], g_ref[...]),
        )
    ):
        total[...] = dot(left, right)
        rows = slice(place * part, (place + 1) * part)
        for slab in range(keep_ref.shape[0]):
            first = 2 * slab * part
            keep_ref[slab, rows, :] = total[pl.ds(first + core * part, part), :].astype(BF16)
            send_ref[slab, rows, :] = total[pl.ds(first + (1 - core) * part, part), :].astype(BF16)
    for slab in range(keep_ref.shape[0]):
        keep_ref[slab, 4 * part :, :] = tail_ref[2 * slab + core]
        send_ref[slab, 4 * part :, :] = tail_ref[2 * slab + 1 - core]


def make_slabs(normed_all, query_grad, key_grad, value_grad, attended, branch_grad, tail):
    devices, extra, width = tail.shape
    all_rows, own = normed_all.shape[0], query_grad.shape[0]
    part, tile = width // devices, 256
    slab_rows = 4 * part + extra
    whole = lambda i: (0, 0)
    column = lambda i: (0, i)
    out = pl.BlockSpec((devices // 2, slab_rows, tile), lambda i: (0, 0, i))
    shape = jax.ShapeDtypeStruct((devices // 2, slab_rows, width), BF16)
    return pl.pallas_call(
        functools.partial(slab_kernel, part),
        grid=(width // tile,),
        in_specs=[
            pl.BlockSpec((all_rows, width), whole),
            pl.BlockSpec((own, tile), column),
            pl.BlockSpec((all_rows, tile), column),
            pl.BlockSpec((all_rows, tile), column),
            pl.BlockSpec((own, width), whole),
            pl.BlockSpec((own, tile), column),
            pl.BlockSpec((devices, extra, tile), lambda i: (0, 0, i)),
        ],
        out_specs=[out, out],
        out_shape=[shape, shape],
        scratch_shapes=[
            pltpu.VMEM((width, all_rows), BF16),
            pltpu.VMEM((width, own), BF16),
            pltpu.VMEM((width, tile), F32),
        ],
        compiler_params=params(),
        cost_estimate=brief(),
        name="slabs",
    )(normed_all, query_grad, key_grad, value_grad, attended, branch_grad, tail)


def exchange(blocks):
    return lax.all_to_all(blocks, "exp", split_axis=0, concat_axis=0, tiled=True)


def body(
    tokens,
    w_query,
    w_key,
    w_value,
    w_out,
    w_router,
    gain_attn,
    gain_mlp,
    pos_bias,
    exp_gate,
    exp_up,
    exp_down,
    doc_lengths,
    bucket_of,
    expert_ids,
    cotangent,
):
    both = ("ctx", "exp")
    own_tokens = tokens[0]
    rows, width = own_tokens.shape
    experts = w_router.shape[1]
    capacity = (5 * TOP * rows + 4 * experts - 1) // (4 * experts)
    reach = (WINDOW + rows - 2) // rows
    scale = HEAD_DIM ** (-0.5)
    ctx_index, ctx_count = lax.axis_index("ctx"), lax.axis_size("ctx")
    exp_index = lax.axis_index("exp")
    part = w_query.shape[0]
    bias_part = pos_bias.shape[0]
    devices = width // part

    expert_range = jnp.arange(experts, dtype=jnp.int32)
    named = jnp.any(expert_ids[0][:, :, None] == expert_range, axis=1)
    named_low = named.astype(BF16)
    step = jnp.arange(rows, dtype=jnp.int32)
    earlier = (step[:, None] > step[None, :]).astype(BF16)
    slots = dot(earlier, named_low).astype(jnp.int32)
    slots = jnp.where(named, slots, -1).T
    routes = (slots[:, None, :] == jnp.arange(capacity, dtype=jnp.int32)[None, :, None]).astype(BF16)
    routes = routes.reshape(experts * capacity, rows)

    names = jnp.pad(named_low, ((0, 0), (0, LANES - experts)))
    early = dot(routes, jnp.concatenate([cotangent[0], names], axis=1)).astype(BF16)
    early = exchange(early.reshape(experts, capacity, width + LANES)).reshape(-1, width + LANES)

    held, share = exp_gate.shape[1], exp_down.shape[1]
    sizes = (share * 5 // 11, share * 6 // 11)
    packed, first = [], 0
    for size in sizes:
        columns = [slice(z * share + first, z * share + first + size) for z in range(ctx_count)]
        parts = [weight[0][:, at] for weight in (exp_gate, exp_up) for at in columns]
        packed.append(jnp.concatenate(parts + [pack_down(exp_down[0][first : first + size], held)], axis=1))
        first += size

    small = jnp.concatenate([w_router.reshape(-1), gain_attn, gain_mlp, pos_bias])
    small = jnp.pad(small, (0, width - small.shape[0]))[None]
    small = lax.all_gather(jnp.pad(small, ((0, 15), (0, 0))), both, axis=0)[:, 0]
    at = part * experts
    full_router = small[:, :at].reshape(width, experts)
    full_gain_attn = small[:, at : at + part].reshape(width).astype(F32)
    full_gain_mlp = small[:, at + part : at + 2 * part].reshape(width).astype(F32)
    table = small[:, at + 2 * part : at + 2 * part + bias_part].reshape(HEADS, BUCKETS)
    column = gather_ctx(jnp.concatenate([w_query, w_key, w_value, w_out], axis=0)[None])
    halo = [shift_ctx(own_tokens, 1), own_tokens]
    column, halo[0], early, packed[0] = together(column, halo[0], early, packed[0])
    for _ in range(1, reach):
        halo.insert(0, shift_ctx(halo[0], 1))
    onehot_bucket = (bucket_of[None, :] == jnp.arange(BUCKETS, dtype=jnp.int32)[:, None]).astype(BF16)
    band = make_band(dot(table, onehot_bucket))

    def then(others):
        *others, halo[0], packed[0] = together(*others, halo[0], packed[0])
        return others

    *halves, band = together(*spread_exp(column, then), band)
    chunk0 = lax.all_gather(packed[0], "ctx", axis=0, tiled=True)
    dense = spread_core(halves)
    full_query, full_key, full_value, full_out = (join_weights(dense, i * part, part) for i in range(4))
    tokens_all = jnp.concatenate(halo, axis=0)
    inputs_all = tokens_all.astype(F32)
    inputs = own_tokens.astype(F32)

    ends = jnp.cumsum(doc_lengths[0])

    def documents(positions):
        return jnp.sum((positions[:, None] >= ends[None, :]).astype(jnp.int32), axis=1)[:, None]

    feature = (jnp.arange(2 * HEAD_DIM, dtype=jnp.int32) % HEAD_DIM)[None, :]
    docs = doc_lengths.shape[1] + 1
    query_pos = ctx_index * rows + step
    key_pos = (ctx_index - reach) * rows + jnp.arange((reach + 1) * rows, dtype=jnp.int32)
    query_doc = (feature == documents(query_pos)).astype(BF16)
    same = (feature == documents(key_pos)) & (key_pos[:, None] >= 0)
    key_doc = jnp.where(same | (feature >= docs), 0.0, NEGATIVE).astype(BF16)

    normed_all = norm_rows(inputs_all, full_gain_attn).astype(BF16)
    normed = normed_all[reach * rows :]
    queries = (dot(normed, full_query).astype(BF16)) * jnp.asarray(scale, BF16)
    keys = dot(normed_all, full_key).astype(BF16)
    values = dot(normed_all, full_value).astype(BF16)
    attended, lse = attend(queries, keys, values, query_doc, key_doc, band)
    middle = inputs + dot(attended, full_out)
    normed_mlp = norm_rows(middle, full_gain_mlp).astype(BF16)

    sent = dot(routes, normed_mlp).astype(BF16)
    arrived = exchange(sent.reshape(experts, capacity, width)).reshape(-1, width)
    router_turned = jnp.pad(full_router.T, ((0, LANES - experts), (0, 0)))
    extras = (early, router_turned)
    units0, units1 = (size * ctx_count for size in sizes)
    arrived, packed[1], chunk0 = together(arrived, packed[1], chunk0)
    up, down = gather_hop(packed[1], packed[1], 1)
    hidden, dboth, carried, _ = run_expert(True, False, units0, ctx_count, arrived, [chunk0], extras, None)
    grad0 = expert_weights(units0, ctx_count, arrived, carried[0], dboth, hidden)
    pieces, sent = [packed[1]], (None, None)
    probs = make_probs(queries, keys, query_doc, key_doc, band, lse)
    own0 = lax.dynamic_index_in_dim(grad0.reshape(ctx_count, held, -1), ctx_index, 0, keepdims=False)
    for hop in range(1, ctx_count):
        if hop == 1:
            up, down, grad0 = together(up, down, grad0)
            parts0 = grad0.reshape(ctx_count, held, -1)
        else:
            up, down = gather_hop(up, down, hop)
            sent = scatter_hop(*scatter_add(parts0, hop - 1, *sent), hop - 1)
            up, down, probs, own0, *sent = together(up, down, probs, own0, *sent)
        pieces += [up, down]
    arrived, *sent = together(arrived, *scatter_add(parts0, ctx_count - 1, *sent))
    sent = scatter_hop(*sent, ctx_count - 1)
    hidden, dboth, carried, router_grad = run_expert(
        False, True, units1, ctx_count, arrived, pieces, extras, carried
    )
    low, made, back, _ = carried
    hidden, dboth, low, made, back, *sent = together(hidden, dboth, low, made, back, *sent)
    grad1 = expert_weights(units1, ctx_count, arrived, low, dboth, hidden, True)
    total1 = lax.psum_scatter(grad1, "ctx", scatter_dimension=0, tiled=True)
    back = exchange(back.reshape(experts, capacity, width)).reshape(-1, width)

    upstream = cotangent[0].astype(F32)
    normed_mlp_grad = dot_rows(routes, back)
    _, second_pull = jax.vjp(norm_rows, middle, full_gain_mlp)
    middle_norm_grad, gain_mlp_grad = second_pull(normed_mlp_grad)
    middle_grad = upstream + middle_norm_grad
    branch_grad = middle_grad.astype(BF16)
    attended_grad = dot_last(branch_grad, full_out).astype(BF16)
    query_grad, key_grad, value_grad, dist_grad = attend_back(
        queries, keys, values, attended_grad, attended, probs
    )
    made, query_grad = together(made, query_grad)
    made = exchange(made.reshape(experts, capacity, width)).reshape(-1, width)
    bias_grad = jnp.dot(
        dist_grad.reshape(HEADS, WINDOW), onehot_bucket.T.astype(F32), precision=lax.Precision.HIGHEST
    )

    halo_grad, own_grad, gain_attn_grad = normed_grad_of(
        tokens_all, query_grad, key_grad, value_grad, full_query, full_key, full_value
    )
    gain_attn_grad = jnp.sum(gain_attn_grad, axis=0)

    tail = jnp.concatenate(
        [
            router_grad[:, :experts].reshape(devices, -1),
            gain_attn_grad.reshape(devices, part),
            gain_mlp_grad.reshape(devices, part),
            bias_grad.reshape(devices, bias_part),
        ],
        axis=1,
    ).astype(BF16)
    tail = jnp.pad(tail[:, None, :], ((0, 0), (0, 15), (0, width - tail.shape[1])))
    output = (middle + dot_rows(routes, made)).astype(BF16)
    keep, send = make_slabs(normed_all, query_grad, key_grad, value_grad, attended, branch_grad, tail)
    other = swap_exp(send, 1)
    parts = scatter_exp(keep, other)
    pieces = [halo_grad[place * rows : (place + 1) * rows] for place in range(reach)]
    returning = shift_ctx(pieces[0], -1)
    for piece in pieces[1:]:
        parts, returning, output = together(parts, returning, output)
        returning = shift_ctx((piece.astype(F32) + returning.astype(F32)).astype(BF16), -1)
    expert_grads = expert_sums(sizes, ctx_count, own0, *sent, total1)
    sent = (None, None)
    for hop in range(1, ctx_count):
        sent = scatter_add(parts, hop, *sent)
        sent = scatter_hop(*sent, hop)
        if hop == 1:
            *sent, grad_gate, grad_up, grad_down = together(*sent, *expert_grads)
    sums = scatter_end(parts, *sent)
    _, own_pull = jax.vjp(norm_rows, inputs, full_gain_attn)
    input_grad = middle_grad + own_pull(own_grad + returning.astype(F32))[0]
    tail = sums[4 * part]
    at = part * experts
    return (
        output[None],
        input_grad[None],
        sums[:part],
        sums[part : 2 * part],
        sums[2 * part : 3 * part],
        sums[3 * part : 4 * part],
        tail[:at].reshape(part, experts),
        tail[at : at + part],
        tail[at + part : at + 2 * part],
        tail[at + 2 * part : at + 2 * part + bias_part],
        grad_gate[None],
        grad_up[None],
        grad_down[None],
    )


def solution(mesh):
    rows3 = P("exp", "ctx", None)
    dense2 = P(("ctx", "exp"), None)
    dense1 = P(("ctx", "exp"))
    return jax.shard_map(
        body,
        mesh=mesh,
        in_specs=(
            rows3,
            dense2,
            dense2,
            dense2,
            dense2,
            dense2,
            dense1,
            dense1,
            dense1,
            rows3,
            rows3,
            rows3,
            P("exp", None),
            P(),
            rows3,
            rows3,
        ),
        out_specs=(
            rows3,
            rows3,
            dense2,
            dense2,
            dense2,
            dense2,
            dense2,
            dense1,
            dense1,
            dense1,
            rows3,
            rows3,
            rows3,
        ),
        check_vma=False,
    )
```
